32 devices in a mesh: seq: 8 (over z, x), grp: 4 (over y, core).
Axes of the slice: x: 2, y: 2, z: 4, core: 2. Of those that a mesh axis runs over, the one named last changes fastest.
Arguments:
- stream_in: bfloat16 [8192, 2048], P(('seq', 'grp')), may hold values from -5 to 5
- query_rows: bfloat16 [8192, 2048], P(('seq', 'grp')), may hold values from -4 to 4
- key_rows: bfloat16 [8192, 2048], P(('seq', 'grp')), may hold values from -4 to 4
- value_rows: bfloat16 [8192, 2048], P(('seq', 'grp')), may hold values from -4 to 4
- log_decay: float32 [16, 8192], P(None, ('seq', 'grp')), may hold values from -1 to 0
- attn_gain: float32 [2048], replicated, may hold values from 0.25 to 1.75
- ffn_gain: float32 [2048], replicated, may hold values from 0.25 to 1.75
- expert_ids: int32 [8192, 8], P(('seq', 'grp')), may hold values from 0 to 15, as said below
- route_weights: float32 [8192, 8], P(('seq', 'grp')), may hold values from 0.1 to 0.5
- response_mask: int32 [8192], P(('seq', 'grp')), may hold values from 0 to 1, as said below
- gate_weight: bfloat16 [2048, 16384], P(None, ('seq', 'grp')), may hold values from -0.125 to 0.125
- up_weight: bfloat16 [2048, 16384], P(None, ('seq', 'grp')), may hold values from -0.125 to 0.125
- down_weight: bfloat16 [16384, 2048], P(('seq', 'grp')), may hold values from -0.1875 to 0.1875
Outputs:
- layer_out: bfloat16 [8192, 2048], P(('seq', 'grp'))
The draws below stay inside these ranges and needn't reach their ends.
Inputs may be any that keep to these rules, and one draw needn't show every extreme that they name: `response_mask`: the response tokens among each aligned block of 256 tokens form one contiguous run. `expert_ids`: each row names 8 different experts; over the response tokens of one aligned block of 256 tokens no expert is named more than 16 times, and in every draw some block names some expert exactly 16 times.
All inputs are finite; a program needn't handle non-finite values.
Results may differ from the reference program's by a relative error of at most 0.0059.
Values may be sent and summed in bfloat16 or wider, within the bound.
No kernel may reach another device: no remote copies, remote signals or barrier semaphores. Data moves between devices by JAX's collectives and lax.ppermute only.
A program may use at most 320 MiB of HBM per device.

```python
import math
import jax
import jax.numpy as jnp
from jax import lax

D = 2048
HEAD_TOTAL = 16
HEAD_DIM = 128
FF = 1024
TOP = 8
CAP = 16
TOK_DEV = 256
TOKEN_TOTAL = 8192
EXPERTS = 16


def route_plan(key):
    blocks = TOKEN_TOTAL // TOK_DEV
    key_level, key_busy, key_start, key_order = jax.random.split(key, 4)
    levels = jax.random.randint(key_level, (blocks,), 2, CAP + 1)
    busiest = jax.random.randint(key_busy, (), 0, blocks)
    levels = jnp.where(jnp.arange(blocks) == busiest, CAP, levels)
    counts = EXPERTS * levels // 8
    starts = jax.random.randint(key_start, (blocks,), 0, TOK_DEV - counts + 1)
    sort_orders = jax.vmap(lambda subkey: jax.random.permutation(subkey, EXPERTS))(jax.random.split(key_order, blocks))
    position = jnp.arange(TOKEN_TOTAL)
    device = position // TOK_DEV
    run_count = counts[device]
    level = levels[device]
    offset = position % TOK_DEV - starts[device]
    response = ((offset >= 0) & (offset < run_count)).astype(jnp.int32)
    within = jnp.mod(offset, run_count)
    hot_quota = jnp.minimum(jnp.minimum(CAP, run_count), 2 * level - jnp.maximum(1, level // 2))
    cold_quota = 2 * level - hot_quota
    column = jnp.arange(TOP)
    entry_index = within[:, None] + column[None, :] * run_count[:, None]
    split_at = EXPERTS // 2 * hot_quota[:, None]
    run_index = jnp.where(entry_index < split_at, entry_index // hot_quota[:, None], EXPERTS // 2 + (entry_index - split_at) // cold_quota[:, None])
    chosen = jnp.take_along_axis(sort_orders[device], run_index, axis=1)
    return (response, chosen.astype(jnp.int32))


def draw_response_mask(key, part):
    response, chosen = route_plan(key)
    return response


def draw_expert_ids(key, part):
    response, chosen = route_plan(key)
    return chosen


def draw_log_decay(key, part):
    key = jax.random.fold_in(key, 7)
    random_subkeys = jax.random.split(key, 7)
    slow_share = 5
    slow = jax.random.randint(random_subkeys[0], (HEAD_TOTAL,), 0, 10) < slow_share
    slow_rate = jnp.exp(jax.random.uniform(random_subkeys[1], (HEAD_TOTAL,), jnp.float32, math.log(0.1), math.log(0.6))) / TOKEN_TOTAL
    fast_rate = jnp.exp(jax.random.uniform(random_subkeys[2], (HEAD_TOTAL,), jnp.float32, math.log(1.0 / 50.0), math.log(1.0 / 30.0)))
    decay_rate = jnp.where(slow, slow_rate, fast_rate)
    blocks = TOKEN_TOTAL // TOK_DEV
    device_scale = jnp.exp(jax.random.uniform(random_subkeys[3], (HEAD_TOTAL, blocks), jnp.float32, math.log(0.6), math.log(1.5)))
    jitter = jax.random.uniform(random_subkeys[4], (HEAD_TOTAL, TOKEN_TOTAL), jnp.float32, 0.5, 1.5)
    surge_events = jax.random.randint(random_subkeys[5], (HEAD_TOTAL, TOKEN_TOTAL), 0, TOKEN_TOTAL) < 2
    surge_penalty = jnp.log(jax.random.uniform(random_subkeys[6], (HEAD_TOTAL, TOKEN_TOTAL), jnp.float32, 0.5, 0.8))
    device = jnp.arange(TOKEN_TOTAL) // TOK_DEV
    steady_level = -decay_rate[:, None] * device_scale[:, device] * jitter
    return (steady_level + jnp.where(surge_events, surge_penalty, 0.0)).astype(jnp.float32)


def draw_stream_in(key, part):
    key = jax.random.fold_in(key, 5)
    random_subkeys = jax.random.split(key, 3)
    rows_scale = jnp.exp(jax.random.uniform(random_subkeys[0], (TOKEN_TOTAL, 1), jnp.float32, math.log(0.5), math.log(2.0)))
    cols_scale = jnp.exp(jax.random.uniform(random_subkeys[1], (1, D), jnp.float32, math.log(0.5), math.log(2.0)))
    values_raw = jnp.clip(jax.random.normal(random_subkeys[2], (TOKEN_TOTAL, D), jnp.float32), -4.0, 4.0)
    return (0.3 * values_raw * rows_scale * cols_scale).astype(jnp.bfloat16)


def block_levels(stream_key, extent, cuts, least, top_value):
    loudness = 1.0
    for dim, shards_of in cuts:
        draws = jax.random.uniform(jax.random.fold_in(jax.random.fold_in(stream_key, 6), dim), (shards_of,), jnp.float32, least / len(cuts), top_value / len(cuts))
        loudness = loudness * jnp.repeat(jnp.exp(draws), extent[dim] // shards_of).reshape((-1,) + (1,) * (len(extent) - 1 - dim))
    return loudness


def normal_values(key, shape, width, reach, cuts=(), held_as=jnp.bfloat16):
    loudness = block_levels(key, shape, cuts, -0.22, 0.18) if cuts else 1.0
    array = jax.random.normal(key, shape, jnp.float32) * width * loudness
    return jnp.minimum(jnp.maximum(array, -reach), reach).astype(held_as)


def setup_inputs(seed: int = 0) -> dict:
    streams_of = jax.random.split(jax.random.key(seed), 14)
    stream_in = draw_stream_in(jax.random.fold_in(streams_of[13], 71), 0)
    query_rows = normal_values(streams_of[1], (TOKEN_TOTAL, D), 0.3, 4.0, ((0, 32),))
    key_rows = normal_values(streams_of[2], (TOKEN_TOTAL, D), 0.3, 4.0, ((0, 32),))
    value_rows = normal_values(streams_of[3], (TOKEN_TOTAL, D), 1.0, 4.0, ((0, 32),))
    log_decay = draw_log_decay(jax.random.fold_in(streams_of[13], 71), 0)
    attn_gain = jnp.clip(1.0 + 0.15 * jax.random.normal(streams_of[5], (D,), jnp.float32), 0.25, 1.75)
    ffn_gain = jnp.clip(1.0 + 0.15 * jax.random.normal(streams_of[6], (D,), jnp.float32), 0.25, 1.75)
    expert_ids = draw_expert_ids(jax.random.fold_in(streams_of[13], 71), 0)
    route_weights = jnp.clip(0.1 + 0.4 * jax.random.uniform(streams_of[8], (TOKEN_TOTAL, TOP), jnp.float32) ** block_levels(streams_of[8], (TOKEN_TOTAL, TOP), ((0, 32),), -0.2, 0.2), 0.1, 0.5)
    response_mask = draw_response_mask(jax.random.fold_in(streams_of[13], 71), 0)
    gate_weight = normal_values(streams_of[10], (D, EXPERTS * FF), D ** -0.5, 0.125, ((1, 32),))
    up_weight = normal_values(streams_of[11], (D, EXPERTS * FF), D ** -0.5, 0.125, ((1, 32),))
    down_weight = normal_values(streams_of[12], (EXPERTS * FF, D), FF ** -0.5, 0.1875, ((0, 32),))
    return dict(stream_in=stream_in, query_rows=query_rows, key_rows=key_rows, value_rows=value_rows, log_decay=log_decay, attn_gain=attn_gain, ffn_gain=ffn_gain, expert_ids=expert_ids, route_weights=route_weights, response_mask=response_mask, gate_weight=gate_weight, up_weight=up_weight, down_weight=down_weight)


attn_eps = 1e-05
norm_eps = 1e-06

def to_low(values):
    low = lax.optimization_barrier(values.astype(jnp.bfloat16))
    return low.astype(jnp.float32)

def local_terms(query_blk, key_blk, value_blk, decay_blk):
    length = query_blk.shape[0]
    highest = lax.Precision.HIGHEST
    running = jnp.cumsum(decay_blk, axis=1)
    block_total = running[:, -1]
    row_pos = lax.broadcasted_iota(jnp.int32, (length, length), 0)
    col_pos = lax.broadcasted_iota(jnp.int32, (length, length), 1)
    causal = (row_pos >= col_pos)[None]
    decay_gap = running[:, :, None] - running[:, None, :]
    factor = jnp.where(causal, jnp.exp(jnp.where(causal, decay_gap, 0.0)), 0.0)
    scores = jnp.einsum('thd,shd->hts', query_blk.astype(jnp.float32), key_blk.astype(jnp.float32), precision=highest)
    weight_matrix = (scores * factor).astype(jnp.bfloat16)
    inside = jnp.einsum('hts,shd->thd', weight_matrix.astype(jnp.float32), value_blk.astype(jnp.float32), precision=highest)
    lifted = to_low(query_blk.astype(jnp.float32) * jnp.exp(running).T[:, :, None])
    scaled = to_low(key_blk.astype(jnp.float32) * jnp.exp(block_total[:, None] - running).T[:, :, None])
    local_state = jnp.einsum('thd,the->hde', scaled, value_blk.astype(jnp.float32), precision=highest)
    return (inside, lifted, local_state, jnp.exp(block_total))

def reference(stream_in, query_rows, key_rows, value_rows, log_decay, attn_gain, ffn_gain, expert_ids, route_weights, response_mask, gate_weight, up_weight, down_weight):
    blocks = TOKEN_TOTAL // TOK_DEV
    shaped = (blocks, TOK_DEV, HEAD_TOTAL, HEAD_DIM)
    decay_blocks = log_decay.reshape(HEAD_TOTAL, blocks, TOK_DEV).transpose(1, 0, 2)

    def step_block(state_in, pieces):
        inside, lifted, local_state, block_decay = local_terms(pieces[0], pieces[1], pieces[2], pieces[3])
        state_low = to_low(state_in)
        carried = jnp.einsum('thd,hde->the', lifted, state_low, precision=lax.Precision.HIGHEST)
        new_state = block_decay[:, None, None] * state_in + local_state
        return (new_state, inside + carried)
    start_state = jnp.zeros((HEAD_TOTAL, HEAD_DIM, HEAD_DIM), jnp.float32)
    final_state, attended = lax.scan(step_block, start_state, (query_rows.reshape(shaped), key_rows.reshape(shaped), value_rows.reshape(shaped), decay_blocks))
    attended = attended.reshape(TOKEN_TOTAL, HEAD_TOTAL, HEAD_DIM)
    normed = attended * lax.rsqrt(lax.optimization_barrier(jnp.mean(attended * attended, axis=-1, keepdims=True)) + attn_eps)
    mixed_rows = stream_in.astype(jnp.float32) + normed.reshape(TOKEN_TOTAL, D) * attn_gain
    ffn_in = (mixed_rows * lax.rsqrt(lax.optimization_barrier(jnp.mean(mixed_rows * mixed_rows, axis=-1, keepdims=True)) + norm_eps) * ffn_gain).astype(jnp.bfloat16)
    slots_all = blocks * CAP
    flat_ids = expert_ids.reshape(blocks, TOK_DEV * TOP)
    live = jnp.repeat(response_mask.reshape(blocks, TOK_DEV), TOP, axis=1) == 1
    onehot = ((flat_ids[:, :, None] == jnp.arange(EXPERTS, dtype=jnp.int32)[None, None, :]) & live[:, :, None]).astype(jnp.int32)
    earlier_count = lax.optimization_barrier(jnp.sum((jnp.cumsum(onehot, axis=1) - onehot) * onehot, axis=2))
    block_index = jnp.arange(blocks, dtype=jnp.int32)[:, None]
    target = jnp.where(live, flat_ids * slots_all + block_index * CAP + earlier_count, EXPERTS * slots_all)
    token_index = block_index * TOK_DEV + jnp.arange(TOK_DEV * TOP, dtype=jnp.int32)[None, :] // TOP
    table_token = jnp.full((EXPERTS * slots_all,), TOKEN_TOTAL, jnp.int32).at[target.reshape(-1)].set(token_index.reshape(-1).astype(jnp.int32), mode='drop')
    table_weight = jnp.zeros((EXPERTS * slots_all,), jnp.float32).at[target.reshape(-1)].set(route_weights.reshape(-1), mode='drop')
    padded_in = jnp.concatenate([ffn_in, jnp.zeros((1, D), jnp.bfloat16)], axis=0)
    half_units = FF // 2

    def per_expert(accum, inputs):
        expert_index, token_list, weight_list = inputs
        rows_in = padded_in[token_list]
        start = (expert_index * FF).astype(jnp.int32)
        gate_cols = lax.dynamic_slice_in_dim(gate_weight, start, FF, 1)
        up_cols = lax.dynamic_slice_in_dim(up_weight, start, FF, 1)
        down_block = lax.dynamic_slice_in_dim(down_weight, start, FF, 0)
        gate_act = jnp.dot(rows_in, gate_cols, preferred_element_type=jnp.float32)
        up_act = jnp.dot(rows_in, up_cols, preferred_element_type=jnp.float32)
        hidden = (jax.nn.silu(gate_act) * up_act).astype(jnp.bfloat16)
        first_half = jnp.dot(hidden[:, :half_units], down_block[:half_units], preferred_element_type=jnp.float32).astype(jnp.bfloat16)
        second_half = jnp.dot(hidden[:, half_units:], down_block[half_units:], preferred_element_type=jnp.float32).astype(jnp.bfloat16)
        expert_out = (first_half.astype(jnp.float32) + second_half.astype(jnp.float32)).astype(jnp.bfloat16)
        accum = accum.at[token_list].add(weight_list[:, None] * expert_out.astype(jnp.float32), mode='drop')
        return (accum, None)
    start_sum = jnp.zeros((TOKEN_TOTAL, D), jnp.float32)
    moe_sum, unused = lax.scan(per_expert, start_sum, (jnp.arange(EXPERTS, dtype=jnp.int32), table_token.reshape(EXPERTS, slots_all), table_weight.reshape(EXPERTS, slots_all)))
    return (mixed_rows + moe_sum).astype(jnp.bfloat16)
```

```python
import functools

import jax
import jax.numpy as jnp
from jax import lax
from jax.experimental import pallas as pl
from jax.experimental.pallas import tpu as pltpu
from jax.sharding import PartitionSpec as P

CAP = 16
TAIL = 8
TAIL16 = 16
ATTN_EPS = 1e-05
NORM_EPS = 1e-06
BOTH = ("seq", "grp")
F32 = jnp.float32
BF16 = jnp.bfloat16
VMEM = pl.BlockSpec(memory_space=pltpu.VMEM)
SMEM = pl.BlockSpec(memory_space=pltpu.SMEM)


def params(mb=32):
    return pltpu.CompilerParams(vmem_limit_bytes=mb * 1024 * 1024)


def cost(flops, nbytes):
    return pl.CostEstimate(flops=flops, bytes_accessed=nbytes, transcendentals=0)


def mm(a, b, ca=1, cb=0):
    return lax.dot_general(a, b, (((ca,), (cb,)), ((), ())), preferred_element_type=F32)


def lower_tri(n):
    rows = lax.broadcasted_iota(jnp.int32, (n, n), 0)
    cols = lax.broadcasted_iota(jnp.int32, (n, n), 1)
    return rows >= cols


def running_cols(dec):
    tri = lower_tri(dec.shape[1]).astype(F32)
    return lax.dot_general(
        tri, dec, (((1,), (1,)), ((), ())), precision=lax.Precision.HIGHEST, preferred_element_type=F32
    )


def running_rows(dec):
    tri = lower_tri(dec.shape[1]).astype(F32)
    return lax.dot_general(
        dec, tri, (((1,), (1,)), ((), ())), precision=lax.Precision.HIGHEST, preferred_element_type=F32
    )


def partner(x):
    count = lax.axis_size("grp")
    return lax.ppermute(x, "grp", [(i, i ^ 1) for i in range(count)])


def across_pairs(x):
    count = lax.axis_size(BOTH)
    groups = [list(range(k, count, 2)) for k in range(2)]
    return lax.all_to_all(x, BOTH, 0, 0, tiled=True, axis_index_groups=groups)


def states_kernel(k_ref, key_ref, val_ref, decr_ref, own_ref, send_ref):
    heads, tok = decr_ref.shape
    half = heads // 2
    hd = own_ref.shape[1]
    k = k_ref[0]
    run = running_cols(decr_ref[...])
    total = run[tok - 1 : tok, :]
    fac = jnp.exp(total - run)
    for r in range(heads):
        side = r // half
        off = pl.multiple_of((side ^ k) * (half * hd) + (r % half) * hd, hd)
        kh = key_ref[:, pl.ds(off, hd)].astype(F32)
        scaled = (kh * fac[:, r : r + 1]).astype(BF16)
        st = mm(scaled, val_ref[:, pl.ds(off, hd)], 0, 0)
        dst = own_ref if side == 0 else send_ref
        dst[(r % half) * hd : (r % half + 1) * hd, :] = st
    tail = jnp.broadcast_to(jnp.pad(total, ((0, 0), (0, hd - heads))), (TAIL, hd))
    own_ref[half * hd :, :] = tail
    send_ref[half * hd :, :] = tail


def pair_kernel(k_ref, own_ref, recv_ref, out_ref, *, half, rows):
    hd = own_ref.shape[1]
    first = k_ref[0] == 0
    base = half * hd
    mine = own_ref[base : base + 1, :]
    theirs = recv_ref[base : base + 1, :]
    pieces = out_ref.shape[0]
    tail_row = lax.broadcasted_iota(jnp.int32, (TAIL16, hd), 0)
    for p in range(pieces):
        j = p * rows // hd
        mt = mine[:, j : j + 1]
        pt = theirs[:, half + j : half + j + 1]
        one = jnp.ones_like(mt)
        a = jnp.where(first, jnp.exp(pt), one)
        b = jnp.where(first, one, jnp.exp(mt))
        lo = p * rows
        chip = own_ref[lo : lo + rows, :] * a + recv_ref[lo : lo + rows, :] * b
        out_ref[p, 0:rows, :] = chip.astype(BF16)
        d = jnp.broadcast_to(jnp.exp(mt + pt), (TAIL16, hd))
        d0 = d.astype(BF16).astype(F32)
        d1 = (d - d0).astype(BF16).astype(F32)
        d2 = d - d0 - d1
        tail = jnp.where(tail_row == 0, d0, jnp.where(tail_row == 1, d1, jnp.where(tail_row == 2, d2, 0.0)))
        out_ref[p, rows : rows + TAIL16, :] = tail.astype(BF16)


def scan_kernel(in_ref, out_ref):
    count, rows, hd = out_ref.shape
    state = jnp.zeros((rows, hd), F32)
    for c in range(count):
        out_ref[c, :, :] = state.astype(BF16)
        tail = in_ref[c, rows : rows + TAIL16, :].astype(F32)
        d = tail[0:1, :] + tail[1:2, :] + tail[2:3, :]
        state = state * d + in_ref[c, 0:rows, :].astype(F32)


def split_kernel(k_ref, pref_ref, own_ref, recv_ref, keep_ref, give_ref, *, half):
    hd = own_ref.shape[1]
    first = k_ref[0] == 0
    base = half * hd
    mine = own_ref[base : base + 1, :]
    theirs = recv_ref[base : base + 1, :]
    for j in range(half):
        sl = slice(j * hd, (j + 1) * hd)
        d0 = jnp.exp(jnp.where(first, mine[:, j : j + 1], theirs[:, half + j : half + j + 1]))
        s0 = jnp.where(first, own_ref[sl, :], recv_ref[sl, :])
        before = pref_ref[sl, :].astype(F32)
        after = before * d0 + s0
        keep_ref[sl, :] = jnp.where(first, before, after).astype(BF16)
        give_ref[sl, :] = jnp.where(first, after, before).astype(BF16)


def inside_kernel(dec_ref, q_ref, key_ref, val_ref, inside_ref, lifted_ref):
    heads, tok = dec_ref.shape
    hd = q_ref.shape[1] // heads
    dec = dec_ref[...]
    run_c = running_cols(dec)
    run_r = running_rows(dec)
    lift = jnp.exp(run_c)
    cut = tok // 2
    tri = lower_tri(cut)
    for h in range(heads):
        cols = slice(h * hd, (h + 1) * hd)
        q = q_ref[:, cols]
        kk = key_ref[:, cols]
        v = val_ref[:, cols]
        lifted_ref[:, cols] = (q.astype(F32) * lift[:, h : h + 1]).astype(BF16)
        rc = run_c[:, h : h + 1]
        rr = run_r[h : h + 1, :]
        f_aa = jnp.where(tri, jnp.exp(rc[:cut] - rr[:, :cut]), 0.0)
        f_bb = jnp.where(tri, jnp.exp(rc[cut:] - rr[:, cut:]), 0.0)
        f_ba = jnp.exp(rc[cut:] - rr[:, :cut])
        w_aa = (mm(q[:cut], kk[:cut], 1, 1) * f_aa).astype(BF16)
        s_b = mm(q[cut:], kk, 1, 1)
        w_b = (s_b * jnp.concatenate([f_ba, f_bb], axis=1)).astype(BF16)
        inside_ref[:cut, cols] = mm(w_aa, v[:cut])
        inside_ref[cut:, cols] = mm(w_b, v)


def head_norm(att):
    return att * lax.rsqrt(jnp.mean(att * att, axis=-1, keepdims=True) + ATTN_EPS)


def rows_kernel(k_ref, lifted_ref, inside_ref, stream_ref, keep_ref, other_ref, again_ref, fgain_ref, disp_ref, sent_ref, mixed_ref):
    hd = keep_ref.shape[1]
    half = keep_ref.shape[0] // hd
    k = k_ref[0]
    rows, width = lifted_ref.shape
    for r in range(2 * half):
        side = r // half
        off = pl.multiple_of((side ^ k) * (half * hd) + (r % half) * hd, hd)
        cols = pl.ds(off, hd)
        src = keep_ref if side == 0 else other_ref
        att = inside_ref[:, cols] + mm(lifted_ref[:, cols], src[(r % half) * hd : (r % half + 1) * hd, :])
        mixed_ref[:, cols] = stream_ref[:, cols].astype(F32) + head_norm(att) * again_ref[:, cols]
    mixed = mixed_ref[...]
    scale = lax.rsqrt(jnp.mean(mixed * mixed, axis=-1, keepdims=True) + NORM_EPS)
    ffn = (mixed * scale * fgain_ref[...]).astype(BF16)
    sent_ref[...] = mm(disp_ref[...], ffn, 0, 0).astype(BF16)


def mixed_kernel(k_ref, lifted_ref, inside_ref, stream_ref, keep_ref, other_ref, again_ref, mixed_ref):
    hd = keep_ref.shape[1]
    half = keep_ref.shape[0] // hd
    mine = pl.program_id(0) == k_ref[0]
    for j in range(half):
        cols = slice(j * hd, (j + 1) * hd)
        st = jnp.where(mine, keep_ref[cols, :].astype(F32), other_ref[cols, :].astype(F32)).astype(BF16)
        att = inside_ref[:, cols] + mm(lifted_ref[:, cols], st)
        mixed_ref[:, cols] = stream_ref[:, cols].astype(F32) + head_norm(att) * again_ref[:, cols]


def route_kernel(ids_ref, wts_ref, live_ref, disp_ref, chi_ref, clo_ref, *, experts):
    tok, top = ids_ref.shape
    slots = experts * CAP
    live = live_ref[...] == 1
    lane = lax.broadcasted_iota(jnp.int32, (tok, experts), 1)
    chosen = jnp.zeros((tok, experts), F32)
    weight = jnp.zeros((tok, experts), F32)
    for j in range(top):
        hit = (ids_ref[:, j : j + 1] == lane) & live
        chosen = jnp.where(hit, 1.0, chosen)
        weight = jnp.where(hit, wts_ref[:, j : j + 1], weight)
    rows = lax.broadcasted_iota(jnp.int32, (tok, tok), 0)
    cols = lax.broadcasted_iota(jnp.int32, (tok, tok), 1)
    before = jnp.where(rows > cols, 1.0, 0.0).astype(BF16)
    place = mm(before, chosen.astype(BF16))
    place = jnp.where(chosen > 0.0, place, -1.0)
    e_row = lax.broadcasted_iota(jnp.int32, (experts, slots), 0)
    s_col = lax.broadcasted_iota(jnp.int32, (experts, slots), 1)
    spread = jnp.where(s_col // CAP == e_row, 1.0, 0.0).astype(BF16)
    slot_of = lax.broadcasted_iota(jnp.int32, (tok, slots), 1) % CAP
    hit = mm(place.astype(BF16), spread) == slot_of.astype(F32)
    w_hi = weight.astype(BF16)
    w_lo = (weight - w_hi.astype(F32)).astype(BF16)
    disp_ref[...] = jnp.where(hit, 1.0, 0.0)
    chi_ref[...] = jnp.where(hit, mm(w_hi, spread), 0.0).astype(BF16)
    clo_ref[...] = jnp.where(hit, mm(w_lo, spread), 0.0).astype(BF16)


def final_kernel(mixed_ref, chi_ref, clo_ref, back_ref, out_ref):
    back = back_ref[...]
    moe = mm(chi_ref[...], back) + mm(clo_ref[...], back)
    out_ref[...] = (mixed_ref[...] + moe).astype(BF16)


def shards(
    stream_in,
    query_rows,
    key_rows,
    value_rows,
    log_decay,
    attn_gain,
    ffn_gain,
    expert_ids,
    route_weights,
    response_mask,
    gate_weight,
    up_weight,
    down_weight,
):
    tok, width = stream_in.shape
    heads = log_decay.shape[0]
    hd = width // heads
    half = heads // 2
    devices = lax.axis_size(BOTH)
    pairs = devices // 2
    experts = devices // 2
    slots = experts * CAP
    top = expert_ids.shape[1]
    resp = min(tok, slots // top)
    rows = half * hd // pairs
    me = lax.axis_index(BOTH)
    bit = (me & 1).reshape(1).astype(jnp.int32)
    sds = jax.ShapeDtypeStruct

    decr = jnp.where(bit[0] == 0, log_decay, jnp.concatenate([log_decay[half:], log_decay[:half]], axis=0))
    own, send = pl.pallas_call(
        states_kernel,
        out_shape=[sds((half * hd + TAIL, hd), F32)] * 2,
        in_specs=[SMEM, VMEM, VMEM, VMEM],
        out_specs=[VMEM, VMEM],
        compiler_params=params(),
        cost_estimate=cost(2 * tok * width * hd, 3 << 20),
        name="states",
    )(bit, key_rows, value_rows, decr)
    recv = partner(send)
    packed = pl.pallas_call(
        functools.partial(pair_kernel, half=half, rows=rows),
        out_shape=sds((pairs, rows + TAIL16, hd), BF16),
        in_specs=[SMEM, VMEM, VMEM],
        out_specs=VMEM,
        compiler_params=params(),
        name="pair",
    )(bit, own, recv)
    gathered = across_pairs(packed)
    scanned = pl.pallas_call(
        scan_kernel,
        out_shape=sds((pairs, rows, hd), BF16),
        in_specs=[VMEM],
        out_specs=VMEM,
        compiler_params=params(),
        name="scan",
    )(gathered)
    pref = across_pairs(scanned).reshape(half * hd, hd)
    keep, give = pl.pallas_call(
        functools.partial(split_kernel, half=half),
        out_shape=[sds((half * hd, hd), BF16)] * 2,
        in_specs=[SMEM] + [VMEM] * 3,
        out_specs=[VMEM, VMEM],
        compiler_params=params(),
        name="split",
    )(bit, pref, own, recv)
    other = partner(give)

    col = pl.BlockSpec((tok, width // 2), lambda i: (0, i))
    inside, lifted = pl.pallas_call(
        inside_kernel,
        grid=(2,),
        out_shape=[sds((tok, width), F32), sds((tok, width), BF16)],
        in_specs=[pl.BlockSpec((half, tok), lambda i: (i, 0)), col, col, col],
        out_specs=[col, col],
        compiler_params=params(),
        cost_estimate=cost(4 * tok * tok * width, 6 << 20),
        name="inside",
    )(log_decay, query_rows, key_rows, value_rows)
    disp, chi, clo = pl.pallas_call(
        functools.partial(route_kernel, experts=experts),
        out_shape=[sds((tok, slots), F32), sds((tok, slots), BF16), sds((tok, slots), BF16)],
        in_specs=[VMEM] * 3,
        out_specs=[VMEM] * 3,
        compiler_params=params(),
        cost_estimate=cost(8 * tok * tok * slots, 1 << 20),
        name="route",
    )(expert_ids, route_weights, response_mask.reshape(tok, 1))

    start = jnp.minimum(jnp.argmax(response_mask), tok - resp)
    cut = functools.partial(lax.dynamic_slice_in_dim, start_index=start, slice_size=resp, axis=0)
    again = attn_gain.reshape(1, width)
    sent = pl.pallas_call(
        rows_kernel,
        out_shape=sds((slots, width), BF16),
        in_specs=[SMEM] + [VMEM] * 8,
        out_specs=VMEM,
        scratch_shapes=[pltpu.VMEM((resp, width), F32)],
        compiler_params=params(),
        name="rows",
    )(
        bit,
        cut(lifted),
        cut(inside),
        cut(stream_in),
        keep,
        other,
        again,
        ffn_gain.reshape(1, width),
        cut(disp).astype(BF16),
    )
    half_rows = CAP // 2
    arrived = lax.all_to_all(sent.reshape(devices, half_rows, width), BOTH, 0, 0, tiled=True)

    gain_col = pl.BlockSpec((1, width // 2), lambda i: (0, i))
    state_all = pl.BlockSpec((half * hd, hd), lambda i: (0, 0))
    mixed = pl.pallas_call(
        mixed_kernel,
        grid=(2,),
        out_shape=sds((tok, width), F32),
        in_specs=[SMEM, col, col, col, state_all, state_all, gain_col],
        out_specs=col,
        compiler_params=params(),
        cost_estimate=cost(2 * tok * width * hd, 7 << 20),
        name="mixed",
    )(bit, lifted, inside, stream_in, keep, other, again)

    mine = arrived.reshape(devices * half_rows, width)
    theirs = partner(mine)
    flat = jnp.concatenate([mine, theirs], axis=0)
    gate_act = jnp.dot(flat, gate_weight, preferred_element_type=F32)
    up_act = jnp.dot(flat, up_weight, preferred_element_type=F32)
    hidden = (jax.nn.silu(gate_act) * up_act).astype(BF16)
    part = jnp.dot(hidden, down_weight, preferred_element_type=F32).astype(BF16)
    count = devices * half_rows
    added = partner(part[count:])
    summed = (part[:count].astype(F32) + added.astype(F32)).astype(BF16)
    back = lax.all_to_all(summed.reshape(devices, half_rows, width), BOTH, 0, 0, tiled=True)
    back = back.reshape(slots, width)

    steps = 4
    fcol = pl.BlockSpec((tok, width // steps), lambda i: (0, i))
    whole = pl.BlockSpec((tok, slots), lambda i: (0, 0))
    return pl.pallas_call(
        final_kernel,
        grid=(steps,),
        out_shape=sds((tok, width), BF16),
        in_specs=[fcol, whole, whole, pl.BlockSpec((slots, width // steps), lambda i: (0, i))],
        out_specs=fcol,
        compiler_params=params(),
        name="final",
    )(mixed, chi, clo, back)


def solution(mesh):
    lead = P(BOTH, None)
    placed = (
        lead,
        lead,
        lead,
        lead,
        P(None, BOTH),
        P(),
        P(),
        lead,
        lead,
        P(BOTH),
        P(None, BOTH),
        P(None, BOTH),
        lead,
    )
    return jax.shard_map(shards, mesh=mesh, in_specs=placed, out_specs=lead, check_vma=False)
```

```python
import functools

import jax
import jax.numpy as jnp
from jax import lax
from jax.experimental import pallas as pl
from jax.experimental.pallas import tpu as pltpu
from jax.sharding import PartitionSpec as P

CAP = 16
TAIL = 8
TAIL16 = 16
ATTN_EPS = 1e-05
NORM_EPS = 1e-06
BOTH = ("seq", "grp")
F32 = jnp.float32
BF16 = jnp.bfloat16
SMEM = pl.BlockSpec(memory_space=pltpu.SMEM)
HBM = pl.BlockSpec(memory_space=pltpu.HBM)
DMA = pltpu.SemaphoreType.DMA


def params(mb=60):
    return pltpu.CompilerParams(vmem_limit_bytes=mb * 1024 * 1024)


def full(x):
    return pl.BlockSpec(x.shape, lambda i, n=len(x.shape): (0,) * n)


def cost(flops, nbytes):
    return pl.CostEstimate(flops=flops, bytes_accessed=nbytes, transcendentals=0)


def mm(a, b, ca=1, cb=0):
    return lax.dot_general(a, b, (((ca,), (cb,)), ((), ())), preferred_element_type=F32)


def lower_tri(n):
    rows = lax.broadcasted_iota(jnp.int32, (n, n), 0)
    cols = lax.broadcasted_iota(jnp.int32, (n, n), 1)
    return rows >= cols


def running_cols(dec):
    tri = lower_tri(dec.shape[1]).astype(F32)
    return lax.dot_general(
        tri, dec, (((1,), (1,)), ((), ())), precision=lax.Precision.HIGHEST, preferred_element_type=F32
    )


def running_rows(dec):
    tri = lower_tri(dec.shape[1]).astype(F32)
    return lax.dot_general(
        dec, tri, (((1,), (1,)), ((), ())), precision=lax.Precision.HIGHEST, preferred_element_type=F32
    )


def partner(x):
    count = lax.axis_size("grp")
    return lax.ppermute(x, "grp", [(i, i ^ 1) for i in range(count)])


def across_pairs(x):
    count = lax.axis_size(BOTH)
    groups = [list(range(k, count, 2)) for k in range(2)]
    return lax.all_to_all(x, BOTH, 0, 0, tiled=True, axis_index_groups=groups)


def copy(src, dst, sems, n):
    c = pltpu.make_async_copy(src, dst, sems.at[n])
    c.start()
    return c


def states_kernel(k_ref, key_hbm, val_hbm, dec_hbm, own_hbm, send_hbm, key_ref, val_ref, dec_ref, own_ref, send_ref, sems):
    heads, tok = dec_ref.shape
    half = heads // 2
    hd = own_ref.shape[1]
    span = half * hd
    k = k_ref[0]
    get_dec = copy(dec_hbm, dec_ref, sems, 0)
    gets = []
    for n in range(2):
        cols = pl.ds(pl.multiple_of((k ^ 1 ^ n) * span, span), span)
        gets.append(copy(key_hbm.at[:, cols], key_ref.at[n], sems, 1 + 2 * n))
        gets.append(copy(val_hbm.at[:, cols], val_ref.at[n], sems, 2 + 2 * n))
    get_dec.wait()
    mine = dec_ref[pl.ds(pl.multiple_of(k * half, half), half), :]
    theirs = dec_ref[pl.ds(pl.multiple_of((1 - k) * half, half), half), :]
    run = running_cols(jnp.concatenate([mine, theirs], axis=0))
    total = run[tok - 1 : tok, :]
    fac = jnp.exp(total - run)
    tail = jnp.broadcast_to(jnp.pad(total, ((0, 0), (0, hd - heads))), (TAIL, hd))
    puts = []
    for n, dst, out, first in ((0, send_ref, send_hbm, half), (1, own_ref, own_hbm, 0)):
        gets[2 * n].wait()
        gets[2 * n + 1].wait()
        for j in range(half):
            cols = slice(j * hd, (j + 1) * hd)
            scaled = (key_ref[n, :, cols].astype(F32) * fac[:, first + j : first + j + 1]).astype(BF16)
            dst[cols, :] = mm(scaled, val_ref[n, :, cols], 0, 0)
        dst[span:, :] = tail
        puts.append(copy(dst, out, sems, 5 + n))
    for c in puts:
        c.wait()


def pair_kernel(k_ref, own_ref, recv_ref, out_ref, *, half, rows):
    hd = own_ref.shape[1]
    first = k_ref[0] == 0
    base = half * hd
    mine = own_ref[base : base + 1, :]
    theirs = recv_ref[base : base + 1, :]
    pieces = out_ref.shape[0]
    tail_row = lax.broadcasted_iota(jnp.int32, (TAIL16, hd), 0)
    for p in range(pieces):
        j = p * rows // hd
        mt = mine[:, j : j + 1]
        pt = theirs[:, half + j : half + j + 1]
        one = jnp.ones_like(mt)
        a = jnp.where(first, jnp.exp(pt), one)
        b = jnp.where(first, one, jnp.exp(mt))
        lo = p * rows
        chip = own_ref[lo : lo + rows, :] * a + recv_ref[lo : lo + rows, :] * b
        out_ref[p, 0:rows, :] = chip.astype(BF16)
        d = jnp.broadcast_to(jnp.exp(mt + pt), (TAIL16, hd))
        d0 = d.astype(BF16).astype(F32)
        d1 = (d - d0).astype(BF16).astype(F32)
        d2 = d - d0 - d1
        tail = jnp.where(tail_row == 0, d0, jnp.where(tail_row == 1, d1, jnp.where(tail_row == 2, d2, 0.0)))
        out_ref[p, rows : rows + TAIL16, :] = tail.astype(BF16)


def scan_kernel(in_ref, out_ref):
    count, rows, hd = out_ref.shape
    state = jnp.zeros((rows, hd), F32)
    for c in range(count):
        out_ref[c, :, :] = state.astype(BF16)
        tail = in_ref[c, rows : rows + TAIL16, :].astype(F32)
        d = tail[0:1, :] + tail[1:2, :] + tail[2:3, :]
        state = state * d + in_ref[c, 0:rows, :].astype(F32)


def split_kernel(k_ref, pref_ref, own_hbm, recv_hbm, keep_ref, give_ref, first_ref, sem, *, half):
    hd = first_ref.shape[1]
    even = k_ref[0] == 0
    base = half * hd

    @pl.when(even)
    def _():
        pltpu.make_async_copy(own_hbm, first_ref, sem).start()

    @pl.when(jnp.logical_not(even))
    def _():
        pltpu.make_async_copy(recv_hbm, first_ref, sem).start()

    pltpu.make_async_copy(own_hbm, first_ref, sem).wait()
    logs = first_ref[base : base + 1, :]
    for j in range(half):
        sl = slice(j * hd, (j + 1) * hd)
        d0 = jnp.exp(jnp.where(even, logs[:, j : j + 1], logs[:, half + j : half + j + 1]))
        before = pref_ref[sl, :].astype(F32)
        after = before * d0 + first_ref[sl, :]
        keep_ref[sl, :] = jnp.where(even, before, after).astype(BF16)
        give_ref[sl, :] = jnp.where(even, after, before).astype(BF16)


def inside_kernel(start_ref, dec_ref, q_ref, key_ref, val_ref, stream_ref, inside_ref, lifted_ref, ir_ref, lr_ref, sr_ref):
    heads, tok = dec_ref.shape
    hd = q_ref.shape[1] // heads
    dec = dec_ref[...]
    run_c = running_cols(dec)
    run_r = running_rows(dec)
    lift = jnp.exp(run_c)
    cut = tok // 2
    tri = lower_tri(cut)
    resp = ir_ref.shape[0]
    start = start_ref[0]
    picked = lax.broadcasted_iota(jnp.int32, (resp, tok), 0) + start
    pick = jnp.where(lax.broadcasted_iota(jnp.int32, (resp, tok), 1) == picked, 1.0, 0.0).astype(BF16)
    for h in range(heads):
        cols = slice(h * hd, (h + 1) * hd)
        q = q_ref[:, cols]
        kk = key_ref[:, cols]
        v = val_ref[:, cols]
        lifted = (q.astype(F32) * lift[:, h : h + 1]).astype(BF16)
        lifted_ref[:, cols] = lifted
        rc = run_c[:, h : h + 1]
        rr = run_r[h : h + 1, :]
        f_aa = jnp.where(tri, jnp.exp(rc[:cut] - rr[:, :cut]), 0.0)
        f_bb = jnp.where(tri, jnp.exp(rc[cut:] - rr[:, cut:]), 0.0)
        f_ba = jnp.exp(rc[cut:] - rr[:, :cut])
        w_aa = (mm(q[:cut], kk[:cut], 1, 1) * f_aa).astype(BF16)
        s_b = mm(q[cut:], kk, 1, 1)
        w_b = (s_b * jnp.concatenate([f_ba, f_bb], axis=1)).astype(BF16)
        inside_ref[:cut, cols] = mm(w_aa, v[:cut])
        inside_ref[cut:, cols] = mm(w_b, v)
    lr_ref[...] = mm(pick, lifted_ref[...]).astype(BF16)
    sr_ref[...] = mm(pick, stream_ref[...]).astype(BF16)
    rest = inside_ref[...]
    high = rest.astype(BF16)
    rest = rest - high.astype(F32)
    mid = rest.astype(BF16)
    low = (rest - mid.astype(F32)).astype(BF16)
    ir_ref[...] = mm(pick, high) + mm(pick, mid) + mm(pick, low)


def head_norm(att):
    return att * lax.rsqrt(jnp.mean(att * att, axis=-1, keepdims=True) + ATTN_EPS)


def rows_kernel(k_ref, lifted_ref, inside_ref, stream_ref, keep_ref, other_ref, again_ref, fgain_ref, disp_ref, sent_ref, mixed_ref):
    hd = keep_ref.shape[1]
    half = keep_ref.shape[0] // hd
    k = k_ref[0]
    rows, width = lifted_ref.shape
    for r in range(2 * half):
        side = r // half
        off = pl.multiple_of((side ^ k) * (half * hd) + (r % half) * hd, hd)
        cols = pl.ds(off, hd)
        src = keep_ref if side == 0 else other_ref
        att = inside_ref[:, cols] + mm(lifted_ref[:, cols], src[(r % half) * hd : (r % half + 1) * hd, :])
        mixed_ref[:, cols] = stream_ref[:, cols].astype(F32) + head_norm(att) * again_ref[:, cols]
    mixed = mixed_ref[...]
    scale = lax.rsqrt(jnp.mean(mixed * mixed, axis=-1, keepdims=True) + NORM_EPS)
    ffn = (mixed * scale * fgain_ref[...]).astype(BF16)
    sent_ref[...] = mm(disp_ref[...], ffn).astype(BF16)


def mixed_kernel(k_ref, lifted_ref, inside_ref, stream_ref, keep_ref, other_ref, again_ref, mixed_ref):
    hd = keep_ref.shape[1]
    half = keep_ref.shape[0] // hd
    mine = pl.program_id(0) == k_ref[0]
    for j in range(half):
        cols = slice(j * hd, (j + 1) * hd)
        st = jnp.where(mine, keep_ref[cols, :].astype(F32), other_ref[cols, :].astype(F32)).astype(BF16)
        att = inside_ref[:, cols] + mm(lifted_ref[:, cols], st)
        mixed_ref[:, cols] = stream_ref[:, cols].astype(F32) + head_norm(att) * again_ref[:, cols]


def route_kernel(start_ref, ids_ref, wts_ref, live_ref, disp_ref, chi_ref, clo_ref, *, experts):
    top, tok = ids_ref.shape
    slots, resp = disp_ref.shape
    live = live_ref[...] == 1
    e_row = lax.broadcasted_iota(jnp.int32, (experts, tok), 0)
    chosen = jnp.zeros((experts, tok), F32)
    weight = jnp.zeros((experts, tok), F32)
    for j in range(top):
        hit = (ids_ref[j : j + 1, :] == e_row) & live
        chosen = jnp.where(hit, 1.0, chosen)
        weight = jnp.where(hit, wts_ref[j : j + 1, :], weight)
    rows = lax.broadcasted_iota(jnp.int32, (tok, tok), 0)
    cols = lax.broadcasted_iota(jnp.int32, (tok, tok), 1)
    before = jnp.where(rows < cols, 1.0, 0.0).astype(BF16)
    place = mm(chosen.astype(BF16), before)
    place = jnp.where(chosen > 0.0, place, -1.0)
    s_row = lax.broadcasted_iota(jnp.int32, (slots, experts), 0)
    e_col = lax.broadcasted_iota(jnp.int32, (slots, experts), 1)
    spread = jnp.where(s_row // CAP == e_col, 1.0, 0.0).astype(BF16)
    slot_of = lax.broadcasted_iota(jnp.int32, (slots, tok), 0) % CAP
    hit = mm(spread, place.astype(BF16)) == slot_of.astype(F32)
    w_hi = weight.astype(BF16)
    w_lo = (weight - w_hi.astype(F32)).astype(BF16)
    picked = lax.broadcasted_iota(jnp.int32, (tok, resp), 1) + start_ref[0]
    pick = jnp.where(lax.broadcasted_iota(jnp.int32, (tok, resp), 0) == picked, 1.0, 0.0).astype(BF16)
    disp_ref[...] = mm(jnp.where(hit, 1.0, 0.0).astype(BF16), pick).astype(BF16)
    chi_ref[...] = jnp.where(hit, mm(spread, w_hi), 0.0).astype(BF16)
    clo_ref[...] = jnp.where(hit, mm(spread, w_lo), 0.0).astype(BF16)


def expert_kernel(x_hbm, g0, u0, d0, g1, u1, d1, out_hbm, gv, uv, dv, hid_ref, x_ref, out_ref, sems, *, step):
    width, units = g0.shape
    cuts = range(0, units, step)
    gets = [copy(x_hbm, x_ref, sems, 0)]
    for n, (g, u) in enumerate(((g0, u0), (g1, u1))):
        for c in cuts:
            cols = pl.ds(c, step)
            gets.append(copy(g.at[:, cols], gv.at[n, :, cols], sems, len(gets)))
            gets.append(copy(u.at[:, cols], uv.at[n, :, cols], sems, len(gets)))
    for n, d in enumerate((d0, d1)):
        gets.append(copy(d, dv.at[n], sems, len(gets)))
    gets[0].wait()
    at = 1
    block = min(256, x_ref.shape[0])
    blocks = range(0, x_ref.shape[0], block)
    for n in range(2):
        for c in cuts:
            gets[at].wait()
            gets[at + 1].wait()
            at += 2
            for r in blocks:
                x = x_ref[r : r + block, :]
                gate = mm(x, gv[n, :, c : c + step])
                up = mm(x, uv[n, :, c : c + step])
                hid_ref[n, r : r + block, c : c + step] = (gate / (1.0 + jnp.exp(-gate)) * up).astype(BF16)
    gets[at].wait()
    gets[at + 1].wait()
    puts = []
    for r in blocks:
        for c in range(0, width, 256):
            cols = slice(c, c + 256)
            p0 = mm(hid_ref[0, r : r + block, :], dv[0, :, cols]).astype(BF16).astype(F32)
            p1 = mm(hid_ref[1, r : r + block, :], dv[1, :, cols]).astype(BF16).astype(F32)
            out_ref[r : r + block, cols] = (p0 + p1).astype(BF16)
        done = pl.ds(r, block)
        puts.append(copy(out_ref.at[done], out_hbm.at[done], sems, len(gets) + len(puts)))
    for c in puts:
        c.wait()


def final_kernel(mixed_ref, chi_ref, clo_ref, back_ref, out_ref):
    back = back_ref[...]
    moe = mm(chi_ref[...], back, 0, 0) + mm(clo_ref[...], back, 0, 0)
    out_ref[...] = (mixed_ref[...] + moe).astype(BF16)


def shards(
    stream_in,
    query_rows,
    key_rows,
    value_rows,
    log_decay,
    attn_gain,
    ffn_gain,
    expert_ids,
    route_weights,
    response_mask,
    gate_weight,
    up_weight,
    down_weight,
):
    tok, width = stream_in.shape
    heads = log_decay.shape[0]
    hd = width // heads
    half = heads // 2
    devices = lax.axis_size(BOTH)
    pairs = devices // 2
    experts = devices // 2
    slots = experts * CAP
    top = expert_ids.shape[1]
    resp = min(tok, slots // top)
    rows = half * hd // pairs
    me = lax.axis_index(BOTH)
    bit = (me & 1).reshape(1).astype(jnp.int32)
    sds = jax.ShapeDtypeStruct

    span = half * hd
    own, send = pl.pallas_call(
        states_kernel,
        out_shape=[sds((span + TAIL, hd), F32)] * 2,
        in_specs=[SMEM, HBM, HBM, HBM],
        out_specs=[HBM, HBM],
        scratch_shapes=[pltpu.VMEM((2, tok, span), BF16)] * 2
        + [pltpu.VMEM((heads, tok), F32)]
        + [pltpu.VMEM((span + TAIL, hd), F32)] * 2
        + [DMA((7,))],
        compiler_params=params(),
        cost_estimate=cost(2 * tok * width * hd, 3 << 20),
        name="states",
    )(bit, key_rows, value_rows, log_decay)
    recv = partner(send)
    recv, gate_own, up_own, down_own = lax.optimization_barrier((recv, gate_weight, up_weight, down_weight))
    gate_other, up_other, down_other = partner(gate_own), partner(up_own), partner(down_own)
    packed = pl.pallas_call(
        functools.partial(pair_kernel, half=half, rows=rows),
        grid=(1,),
        out_shape=sds((pairs, rows + TAIL16, hd), BF16),
        in_specs=[SMEM, full(own), full(recv)],
        out_specs=full(sds((pairs, rows + TAIL16, hd), BF16)),
        compiler_params=params(8),
        name="pair",
    )(bit, own, recv)
    gathered = across_pairs(packed)
    col = pl.BlockSpec((tok, width // 2), lambda i: (0, i))
    wcol = pl.BlockSpec((resp, width // 2), lambda i: (0, i))
    start = jnp.minimum(jnp.argmax(response_mask), tok - resp).astype(jnp.int32).reshape(1)
    routing = (expert_ids.T, route_weights.T, response_mask.reshape(1, tok))
    tables = [sds((slots, resp), BF16), sds((slots, tok), BF16), sds((slots, tok), BF16)]
    disp, chi, clo = pl.pallas_call(
        functools.partial(route_kernel, experts=experts),
        grid=(1,),
        out_shape=tables,
        in_specs=[SMEM] + [full(a) for a in routing],
        out_specs=[full(a) for a in tables],
        compiler_params=params(),
        cost_estimate=cost(8 * tok * tok * slots, 1 << 20),
        name="route",
    )(start, *routing)
    inside, lifted, inside_r, lifted_r, stream_r = pl.pallas_call(
        inside_kernel,
        grid=(2,),
        out_shape=[
            sds((tok, width), F32),
            sds((tok, width), BF16),
            sds((resp, width), F32),
            sds((resp, width), BF16),
            sds((resp, width), BF16),
        ],
        in_specs=[SMEM, pl.BlockSpec((half, tok), lambda i: (i, 0)), col, col, col, col],
        out_specs=[col, col, wcol, wcol, wcol],
        compiler_params=params(),
        cost_estimate=cost(4 * tok * tok * width, 6 << 20),
        name="inside",
    )(start, log_decay, query_rows, key_rows, value_rows, stream_in)
    gathered, inside, lifted, inside_r, lifted_r, stream_r, disp, chi, clo = lax.optimization_barrier(
        (gathered, inside, lifted, inside_r, lifted_r, stream_r, disp, chi, clo)
    )
    scanned = pl.pallas_call(
        scan_kernel,
        grid=(1,),
        out_shape=sds((pairs, rows, hd), BF16),
        in_specs=[full(gathered)],
        out_specs=full(sds((pairs, rows, hd), BF16)),
        compiler_params=params(8),
        name="scan",
    )(gathered)
    pref = across_pairs(scanned).reshape(half * hd, hd)
    keep, give = pl.pallas_call(
        functools.partial(split_kernel, half=half),
        grid=(1,),
        out_shape=[sds((half * hd, hd), BF16)] * 2,
        in_specs=[SMEM, full(pref), HBM, HBM],
        out_specs=[full(pref)] * 2,
        scratch_shapes=[pltpu.VMEM((span + TAIL, hd), F32), DMA],
        compiler_params=params(8),
        name="split",
    )(bit, pref, own, recv)
    other = partner(give)

    again = attn_gain.reshape(1, width)
    window = (lifted_r, inside_r, stream_r, keep, other, again, ffn_gain.reshape(1, width), disp)
    sent = pl.pallas_call(
        rows_kernel,
        grid=(1,),
        out_shape=sds((slots, width), BF16),
        in_specs=[SMEM] + [full(a) for a in window],
        out_specs=full(sds((slots, width), BF16)),
        scratch_shapes=[pltpu.VMEM((resp, width), F32)],
        compiler_params=params(8),
        name="rows",
    )(bit, *window)
    half_rows = CAP // 2
    arrived = lax.all_to_all(sent.reshape(devices, half_rows, width), BOTH, 0, 0, tiled=True)

    gain_col = pl.BlockSpec((1, width // 2), lambda i: (0, i))
    state_all = pl.BlockSpec((half * hd, hd), lambda i: (0, 0))
    mixed = pl.pallas_call(
        mixed_kernel,
        grid=(2,),
        out_shape=sds((tok, width), F32),
        in_specs=[SMEM, col, col, col, state_all, state_all, gain_col],
        out_specs=col,
        compiler_params=params(32),
        cost_estimate=cost(2 * tok * width * hd, 7 << 20),
        name="mixed",
    )(bit, lifted, inside, stream_in, keep, other, again)

    arrived, mixed = lax.optimization_barrier((arrived, mixed))
    units = gate_weight.shape[1]
    step = min(256, units)
    many = devices * half_rows
    done = pl.pallas_call(
        functools.partial(expert_kernel, step=step),
        out_shape=sds((many, width), BF16),
        in_specs=[HBM] * 7,
        out_specs=HBM,
        scratch_shapes=[pltpu.VMEM((2, width, units), BF16)] * 2
        + [pltpu.VMEM((2, units, width), BF16), pltpu.VMEM((2, many, units), BF16)]
        + [pltpu.VMEM((many, width), BF16)] * 2
        + [DMA((4 * (units // step) + 3 + many // min(256, many),))],
        compiler_params=params(48),
        cost_estimate=cost(12 * many * width * units, 14 << 20),
        name="expert",
    )(arrived.reshape(many, width), gate_own, up_own, down_own, gate_other, up_other, down_other)
    back = lax.all_to_all(done.reshape(devices, half_rows, width), BOTH, 0, 0, tiled=True)
    back = back.reshape(slots, width)

    steps = 4
    fcol = pl.BlockSpec((tok, width // steps), lambda i: (0, i))
    whole = pl.BlockSpec((slots, tok), lambda i: (0, 0))
    return pl.pallas_call(
        final_kernel,
        grid=(steps,),
        out_shape=sds((tok, width), BF16),
        in_specs=[fcol, whole, whole, pl.BlockSpec((slots, width // steps), lambda i: (0, i))],
        out_specs=fcol,
        compiler_params=params(),
        name="final",
    )(mixed, chi, clo, back)


def solution(mesh):
    lead = P(BOTH, None)
    placed = (
        lead,
        lead,
        lead,
        lead,
        P(None, BOTH),
        P(),
        P(),
        lead,
        lead,
        P(BOTH),
        P(None, BOTH),
        P(None, BOTH),
        lead,
    )
    return jax.shard_map(shards, mesh=mesh, in_specs=placed, out_specs=lead, check_vma=False)
```

```python
import functools

import jax
import jax.numpy as jnp
from jax import lax
from jax.experimental import pallas as pl
from jax.experimental.pallas import tpu as pltpu
from jax.sharding import PartitionSpec as P

CAP = 16
TAIL = 8
TAIL16 = 16
ATTN_EPS = 1e-05
NORM_EPS = 1e-06
PLANES = 4
PARTS = 2
BOTH = ("seq", "grp")
F32 = jnp.float32
BF16 = jnp.bfloat16
SMEM = pl.BlockSpec(memory_space=pltpu.SMEM)
HBM = pl.BlockSpec(memory_space=pltpu.HBM)
DMA = pltpu.SemaphoreType.DMA


def params(mb=60):
    return pltpu.CompilerParams(vmem_limit_bytes=mb * 1024 * 1024)


def full(x):
    return pl.BlockSpec(x.shape, lambda i, n=len(x.shape): (0,) * n)


def cost(flops, nbytes):
    return pl.CostEstimate(flops=flops, bytes_accessed=nbytes, transcendentals=0)


def mm(a, b, ca=1, cb=0):
    return lax.dot_general(a, b, (((ca,), (cb,)), ((), ())), preferred_element_type=F32)


def lower_tri(n):
    rows = lax.broadcasted_iota(jnp.int32, (n, n), 0)
    cols = lax.broadcasted_iota(jnp.int32, (n, n), 1)
    return rows >= cols


def running_cols(dec):
    tri = lower_tri(dec.shape[1]).astype(F32)
    return lax.dot_general(
        tri, dec, (((1,), (1,)), ((), ())), precision=lax.Precision.HIGHEST, preferred_element_type=F32
    )


def running_rows(dec):
    tri = lower_tri(dec.shape[1]).astype(F32)
    return lax.dot_general(
        dec, tri, (((1,), (1,)), ((), ())), precision=lax.Precision.HIGHEST, preferred_element_type=F32
    )


def partner(x):
    count = lax.axis_size("grp")
    return lax.ppermute(x, "grp", [(i, i ^ 1) for i in range(count)])


def apart(x, distance):
    return lax.ppermute(x, BOTH, [(i, i ^ distance) for i in range(lax.axis_size(BOTH))])


def across_pairs(x):
    count = lax.axis_size(BOTH)
    groups = [list(range(k, count, 2)) for k in range(2)]
    return lax.all_to_all(x, BOTH, 0, 0, tiled=True, axis_index_groups=groups)


def copy(src, dst, sems, n):
    c = pltpu.make_async_copy(src, dst, sems.at[n])
    c.start()
    return c


def states_kernel(k_ref, key_hbm, val_hbm, dec_hbm, own_hbm, send_hbm, key_ref, val_ref, dec_ref, own_ref, send_ref, sems):
    heads, tok = dec_ref.shape
    half = heads // 2
    hd = own_ref.shape[1]
    span = half * hd
    k = k_ref[0]
    get_dec = copy(dec_hbm, dec_ref, sems, 0)
    gets = []
    for n in range(2):
        cols = pl.ds(pl.multiple_of((k ^ 1 ^ n) * span, span), span)
        gets.append(copy(key_hbm.at[:, cols], key_ref.at[n], sems, 1 + 2 * n))
        gets.append(copy(val_hbm.at[:, cols], val_ref.at[n], sems, 2 + 2 * n))
    get_dec.wait()
    mine = dec_ref[pl.ds(pl.multiple_of(k * half, half), half), :]
    theirs = dec_ref[pl.ds(pl.multiple_of((1 - k) * half, half), half), :]
    run = running_cols(jnp.concatenate([mine, theirs], axis=0))
    total = run[tok - 1 : tok, :]
    fac = jnp.exp(total - run)
    tail = jnp.broadcast_to(jnp.pad(total, ((0, 0), (0, hd - heads))), (TAIL, hd))
    puts = []
    for n, dst, out, first in ((0, send_ref, send_hbm, half), (1, own_ref, own_hbm, 0)):
        gets[2 * n].wait()
        gets[2 * n + 1].wait()
        for j in range(half):
            cols = slice(j * hd, (j + 1) * hd)
            scaled = (key_ref[n, :, cols].astype(F32) * fac[:, first + j : first + j + 1]).astype(BF16)
            dst[cols, :] = mm(scaled, val_ref[n, :, cols], 0, 0)
        dst[span:, :] = tail
        puts.append(copy(dst, out, sems, 5 + n))
    for c in puts:
        c.wait()


def pair_kernel(k_ref, own_ref, recv_ref, out_ref, *, half, rows):
    hd = own_ref.shape[1]
    first = k_ref[0] == 0
    base = half * hd
    mine = own_ref[base : base + 1, :]
    theirs = recv_ref[base : base + 1, :]
    pieces = out_ref.shape[0]
    tail_row = lax.broadcasted_iota(jnp.int32, (TAIL16, hd), 0)
    for p in range(pieces):
        j = p * rows // hd
        mt = mine[:, j : j + 1]
        pt = theirs[:, half + j : half + j + 1]
        one = jnp.ones_like(mt)
        a = jnp.where(first, jnp.exp(pt), one)
        b = jnp.where(first, one, jnp.exp(mt))
        lo = p * rows
        chip = own_ref[lo : lo + rows, :] * a + recv_ref[lo : lo + rows, :] * b
        out_ref[p, 0:rows, :] = chip.astype(BF16)
        d = jnp.broadcast_to(jnp.exp(mt + pt), (TAIL16, hd))
        d0 = d.astype(BF16).astype(F32)
        d1 = (d - d0).astype(BF16).astype(F32)
        d2 = d - d0 - d1
        tail = jnp.where(tail_row == 0, d0, jnp.where(tail_row == 1, d1, jnp.where(tail_row == 2, d2, 0.0)))
        out_ref[p, rows : rows + TAIL16, :] = tail.astype(BF16)


def scan_kernel(in_ref, out_ref):
    count, rows, hd = out_ref.shape
    state = jnp.zeros((rows, hd), F32)
    for c in range(count):
        out_ref[c, :, :] = state.astype(BF16)
        tail = in_ref[c, rows : rows + TAIL16, :].astype(F32)
        d = tail[0:1, :] + tail[1:2, :] + tail[2:3, :]
        state = state * d + in_ref[c, 0:rows, :].astype(F32)


def split_kernel(k_ref, pref_ref, own_hbm, recv_hbm, keep_ref, give_ref, first_ref, sem, *, half):
    hd = first_ref.shape[1]
    even = k_ref[0] == 0
    base = half * hd

    @pl.when(even)
    def _():
        pltpu.make_async_copy(own_hbm, first_ref, sem).start()

    @pl.when(jnp.logical_not(even))
    def _():
        pltpu.make_async_copy(recv_hbm, first_ref, sem).start()

    pltpu.make_async_copy(own_hbm, first_ref, sem).wait()
    logs = first_ref[base : base + 1, :]
    for j in range(half):
        sl = slice(j * hd, (j + 1) * hd)
        d0 = jnp.exp(jnp.where(even, logs[:, j : j + 1], logs[:, half + j : half + j + 1]))
        before = pref_ref[sl, :].astype(F32)
        after = before * d0 + first_ref[sl, :]
        keep_ref[sl, :] = jnp.where(even, before, after).astype(BF16)
        give_ref[sl, :] = jnp.where(even, after, before).astype(BF16)


def inside_kernel(start_ref, dec_ref, q_ref, key_ref, val_ref, stream_ref, inside_ref, lifted_ref, ir_ref, lr_ref, sr_ref):
    heads, tok = dec_ref.shape
    hd = q_ref.shape[1] // heads
    dec = dec_ref[...]
    run_c = running_cols(dec)
    run_r = running_rows(dec)
    lift = jnp.exp(run_c)
    cut = tok // 2
    tri = lower_tri(cut)
    resp = ir_ref.shape[0]
    start = start_ref[0]
    picked = lax.broadcasted_iota(jnp.int32, (resp, tok), 0) + start
    pick = jnp.where(lax.broadcasted_iota(jnp.int32, (resp, tok), 1) == picked, 1.0, 0.0).astype(BF16)
    for h in range(heads):
        cols = slice(h * hd, (h + 1) * hd)
        q = q_ref[:, cols]
        kk = key_ref[:, cols]
        v = val_ref[:, cols]
        lifted = (q.astype(F32) * lift[:, h : h + 1]).astype(BF16)
        lifted_ref[:, cols] = lifted
        rc = run_c[:, h : h + 1]
        rr = run_r[h : h + 1, :]
        f_aa = jnp.where(tri, jnp.exp(rc[:cut] - rr[:, :cut]), 0.0)
        f_bb = jnp.where(tri, jnp.exp(rc[cut:] - rr[:, cut:]), 0.0)
        f_ba = jnp.exp(rc[cut:] - rr[:, :cut])
        w_aa = (mm(q[:cut], kk[:cut], 1, 1) * f_aa).astype(BF16)
        s_b = mm(q[cut:], kk, 1, 1)
        w_b = (s_b * jnp.concatenate([f_ba, f_bb], axis=1)).astype(BF16)
        inside_ref[:cut, cols] = mm(w_aa, v[:cut])
        inside_ref[cut:, cols] = mm(w_b, v)
    lr_ref[...] = mm(pick, lifted_ref[...]).astype(BF16)
    sr_ref[...] = mm(pick, stream_ref[...]).astype(BF16)
    rest = inside_ref[...]
    high = rest.astype(BF16)
    rest = rest - high.astype(F32)
    mid = rest.astype(BF16)
    low = (rest - mid.astype(F32)).astype(BF16)
    ir_ref[...] = mm(pick, high) + mm(pick, mid) + mm(pick, low)


def head_norm(att):
    return att * lax.rsqrt(jnp.mean(att * att, axis=-1, keepdims=True) + ATTN_EPS)


def rows_kernel(k_ref, lifted_ref, inside_ref, stream_ref, keep_ref, other_ref, again_ref, fgain_ref, *refs):
    *out_refs, mixed_ref = refs
    hd = keep_ref.shape[1]
    half = keep_ref.shape[0] // hd
    k = k_ref[0]
    for r in range(2 * half):
        side = r // half
        off = pl.multiple_of((side ^ k) * (half * hd) + (r % half) * hd, hd)
        cols = pl.ds(off, hd)
        src = keep_ref if side == 0 else other_ref
        att = inside_ref[:, cols] + mm(lifted_ref[:, cols], src[(r % half) * hd : (r % half + 1) * hd, :])
        mixed_ref[:, cols] = stream_ref[:, cols].astype(F32) + head_norm(att) * again_ref[:, cols]
    mixed = mixed_ref[...]
    scale = lax.rsqrt(jnp.mean(mixed * mixed, axis=-1, keepdims=True) + NORM_EPS)
    ffn = (mixed * scale * fgain_ref[...]).astype(BF16)
    part = ffn.shape[1] // len(out_refs)
    for c, out_ref in enumerate(out_refs):
        out_ref[...] = ffn[:, c * part : (c + 1) * part]


def mixed_kernel(k_ref, from_ref, lifted_ref, inside_ref, stream_ref, keep_ref, other_ref, again_ref, base_ref, near_ref, mixed_ref):
    hd = keep_ref.shape[1]
    half = keep_ref.shape[0] // hd
    mine = pl.program_id(0) == k_ref[0]
    for j in range(half):
        cols = slice(j * hd, (j + 1) * hd)
        st = jnp.where(mine, keep_ref[cols, :].astype(F32), other_ref[cols, :].astype(F32)).astype(BF16)
        att = inside_ref[:, cols] + mm(lifted_ref[:, cols], st)
        mixed_ref[:, cols] = stream_ref[:, cols].astype(F32) + head_norm(att) * again_ref[:, cols]
    base_ref[...] = mixed_ref[...].astype(BF16)
    near_ref[...] = mixed_ref[pl.ds(pl.multiple_of(from_ref[0], 16), near_ref.shape[0]), :]


def route_kernel(start_ref, plane_ref, ids_ref, wts_ref, live_ref, *refs, experts):
    *out_refs, tab_ref = refs
    top, tok = ids_ref.shape
    slots = experts * CAP
    planes = len(out_refs)
    span = slots // planes
    resp = tab_ref.shape[2]
    live = live_ref[...] == 1
    e_row = lax.broadcasted_iota(jnp.int32, (experts, tok), 0)
    chosen = jnp.zeros((experts, tok), F32)
    weight = jnp.zeros((experts, tok), F32)
    for j in range(top):
        hit = (ids_ref[j : j + 1, :] == e_row) & live
        chosen = jnp.where(hit, 1.0, chosen)
        weight = jnp.where(hit, wts_ref[j : j + 1, :], weight)
    rows = lax.broadcasted_iota(jnp.int32, (tok, tok), 0)
    cols = lax.broadcasted_iota(jnp.int32, (tok, tok), 1)
    before = jnp.where(rows < cols, 1.0, 0.0).astype(BF16)
    place = mm(chosen.astype(BF16), before)
    place = jnp.where(chosen > 0.0, place, -1.0)
    s_row = lax.broadcasted_iota(jnp.int32, (slots, experts), 0)
    e_col = lax.broadcasted_iota(jnp.int32, (slots, experts), 1)
    spread = jnp.where(s_row // CAP == e_col, 1.0, 0.0).astype(BF16)
    slot_of = lax.broadcasted_iota(jnp.int32, (slots, tok), 0) % CAP
    hit = mm(spread, place.astype(BF16)) == slot_of.astype(F32)
    w_hi = weight.astype(BF16)
    w_lo = (weight - w_hi.astype(F32)).astype(BF16)
    picked = lax.broadcasted_iota(jnp.int32, (tok, resp), 1) + start_ref[0]
    pick = jnp.where(lax.broadcasted_iota(jnp.int32, (tok, resp), 0) == picked, 1.0, 0.0).astype(BF16)
    zero = jnp.zeros((slots, tok), F32)
    tables = (jnp.where(hit, 1.0, zero), jnp.where(hit, mm(spread, w_hi), zero), jnp.where(hit, mm(spread, w_lo), zero))
    for n, table in enumerate(tables):
        table = mm(table.astype(BF16), pick).astype(BF16)
        for p in range(planes):
            tab_ref[p, n * span : (n + 1) * span, :] = table[p * span : (p + 1) * span, :]
    for m, out_ref in enumerate(out_refs):
        out_ref[...] = tab_ref[plane_ref[0] ^ m, :, :]


def table_rows(tab_ref, n, at, count):
    lead = n * count * CAP
    rows = [tab_ref[pl.ds(pl.multiple_of(lead + (at ^ m) * CAP, CAP), CAP), :] for m in range(count)]
    return jnp.concatenate(rows, axis=0)


def gather_kernel(at_ref, *refs, planes, count):
    tabs, rows, outs = refs[:planes], refs[planes : 2 * planes], refs[2 * planes :]
    for m in range(planes):
        got = mm(table_rows(tabs[m], 0, at_ref[0], count), rows[m][...]).astype(BF16)
        for q in range(count):
            outs[q][m * CAP : (m + 1) * CAP, :] = got[q * CAP : (q + 1) * CAP, :]


def combine_kernel(at_ref, *refs, planes, count):
    tabs, results, outs = refs[:planes], refs[planes : planes + count], refs[planes + count :]
    for m in range(planes):
        got = jnp.concatenate([results[q][m * CAP : (m + 1) * CAP, :] for q in range(count)], axis=0)
        hi = table_rows(tabs[m], 1, at_ref[0], count)
        lo = table_rows(tabs[m], 2, at_ref[0], count)
        outs[m][...] = (mm(hi, got, 0, 0) + mm(lo, got, 0, 0)).astype(outs[m].dtype)


def expert_kernel(*refs, count, parts, step):
    xs, refs = refs[: count * parts], refs[count * parts :]
    (g0, u0, d0, g1, u1, d1), refs = refs[:6], refs[6:]
    outs, refs = refs[:count], refs[count:]
    hid_out, gv, uv, dv, hid_ref, x_ref, sems = refs
    units = g0.shape[1]
    rows, part = xs[0].shape
    cuts = range(0, units, step)
    gets = []
    for q in range(count):
        for c in range(parts):
            dst = x_ref.at[pl.ds(q * rows, rows), pl.ds(c * part, part)]
            gets.append(copy(xs[c * count + q], dst, sems, len(gets)))
    at = len(gets)
    for n, (g, u) in enumerate(((g0, u0), (g1, u1))):
        for c in cuts:
            cols = pl.ds(c, step)
            gets.append(copy(g.at[:, cols], gv.at[n, :, cols], sems, len(gets)))
            gets.append(copy(u.at[:, cols], uv.at[n, :, cols], sems, len(gets)))
    for n, d in enumerate((d0, d1)):
        gets.append(copy(d.at[:, pl.ds(0, part)], dv.at[n], sems, len(gets)))
    for c in gets[:at]:
        c.wait()
    many = count * rows
    block = min(256, many)
    for n in range(2):
        for c in cuts:
            gets[at].wait()
            gets[at + 1].wait()
            at += 2
            for r in range(0, many, block):
                x = x_ref[r : r + block, :]
                gate = mm(x, gv[n, :, c : c + step])
                up = mm(x, uv[n, :, c : c + step])
                hid_ref[n, r : r + block, c : c + step] = (gate / (1.0 + jnp.exp(-gate)) * up).astype(BF16)
    put = copy(hid_ref, hid_out, sems, len(gets))
    gets[at].wait()
    gets[at + 1].wait()
    down(hid_ref, dv, outs, block)
    put.wait()


def down(hid_ref, down_ref, outs, block):
    rows, part = outs[0].shape
    for r in range(0, rows * len(outs), block):
        for c in range(0, part, 256):
            cols = slice(c, c + 256)
            p0 = mm(hid_ref[0, r : r + block, :], down_ref[0, :, cols]).astype(BF16).astype(F32)
            p1 = mm(hid_ref[1, r : r + block, :], down_ref[1, :, cols]).astype(BF16).astype(F32)
            p = (p0 + p1).astype(BF16)
            for q in range(r // rows, (r + block) // rows):
                outs[q][:, cols] = p[q * rows - r : (q + 1) * rows - r, :]


def down_kernel(hid_ref, d0, d1, *refs, count, first):
    outs, (dv, sems) = refs[:count], refs[count:]
    part = outs[0].shape[1]
    gets = [copy(d.at[:, pl.ds(first, part)], dv.at[n], sems, n) for n, d in enumerate((d0, d1))]
    for c in gets:
        c.wait()
    down(hid_ref, dv, outs, min(256, hid_ref.shape[1]))


def final_kernel(start_ref, from_ref, base_hbm, near_ref, *refs, parts, planes):
    shares, (out_hbm, res_ref, sem) = refs[: parts * planes], refs[parts * planes :]
    many, width = near_ref.shape
    resp, part = shares[0].shape
    row = lax.broadcasted_iota(jnp.int32, (many, resp), 0)
    place = lax.broadcasted_iota(jnp.int32, (many, resp), 1) + (start_ref[0] - from_ref[0])
    spread = jnp.where(row == place, 1.0, 0.0).astype(BF16)
    for c in range(parts):
        cols = slice(c * part, (c + 1) * part)
        total = shares[c * planes][...]
        for m in range(1, planes):
            total = total + shares[c * planes + m][...].astype(F32)
        hi = total.astype(BF16)
        lo = (total - hi.astype(F32)).astype(BF16)
        res_ref[:, cols] = (near_ref[:, cols] + mm(spread, hi) + mm(spread, lo)).astype(BF16)
    put = pltpu.make_async_copy(res_ref, out_hbm.at[pl.ds(pl.multiple_of(from_ref[0], 16), many)], sem)
    put.start()
    put.wait()


def shards(
    stream_in,
    query_rows,
    key_rows,
    value_rows,
    log_decay,
    attn_gain,
    ffn_gain,
    expert_ids,
    route_weights,
    response_mask,
    gate_weight,
    up_weight,
    down_weight,
):
    tok, width = stream_in.shape
    heads = log_decay.shape[0]
    hd = width // heads
    half = heads // 2
    devices = lax.axis_size(BOTH)
    pairs = devices // 2
    experts = devices // 2
    slots = experts * CAP
    top = expert_ids.shape[1]
    resp = min(tok, slots // top)
    rows = half * hd // pairs
    planes = PLANES
    count = pairs // planes
    part = width // PARTS
    me = lax.axis_index(BOTH)
    bit = (me & 1).reshape(1).astype(jnp.int32)
    sds = jax.ShapeDtypeStruct

    span = half * hd
    own, send = pl.pallas_call(
        states_kernel,
        out_shape=[sds((span + TAIL, hd), F32)] * 2,
        in_specs=[SMEM, HBM, HBM, HBM],
        out_specs=[HBM, HBM],
        scratch_shapes=[pltpu.VMEM((2, tok, span), BF16)] * 2
        + [pltpu.VMEM((heads, tok), F32)]
        + [pltpu.VMEM((span + TAIL, hd), F32)] * 2
        + [DMA((7,))],
        compiler_params=params(),
        cost_estimate=cost(2 * tok * width * hd, 3 << 20),
        name="states",
    )(bit, key_rows, value_rows, log_decay)
    recv = partner(send)
    recv, gate_own, up_own, down_own = lax.optimization_barrier((recv, gate_weight, up_weight, down_weight))
    gate_other, up_other, down_other = partner(gate_own), partner(up_own), partner(down_own)
    packed = pl.pallas_call(
        functools.partial(pair_kernel, half=half, rows=rows),
        grid=(1,),
        out_shape=sds((pairs, rows + TAIL16, hd), BF16),
        in_specs=[SMEM, full(own), full(recv)],
        out_specs=full(sds((pairs, rows + TAIL16, hd), BF16)),
        compiler_params=params(8),
        name="pair",
    )(bit, own, recv)
    gathered = across_pairs(packed)
    col = pl.BlockSpec((tok, width // 2), lambda i: (0, i))
    wcol = pl.BlockSpec((resp, width // 2), lambda i: (0, i))
    start = jnp.minimum(jnp.argmax(response_mask), tok - resp).astype(jnp.int32).reshape(1)
    plane = lax.shift_right_logical(me, (2 * count).bit_length() - 1).reshape(1).astype(jnp.int32)
    at = (lax.shift_right_logical(me, 1) & (count - 1)).reshape(1).astype(jnp.int32)
    routing = (expert_ids.T, route_weights.T, response_mask.reshape(1, tok))
    table = sds((3 * count * CAP, resp), BF16)
    tables = pl.pallas_call(
        functools.partial(route_kernel, experts=experts),
        grid=(1,),
        out_shape=[table] * planes,
        in_specs=[SMEM, SMEM] + [full(a) for a in routing],
        out_specs=[full(table)] * planes,
        scratch_shapes=[pltpu.VMEM((planes,) + table.shape, BF16)],
        compiler_params=params(),
        cost_estimate=cost(8 * tok * tok * slots, 1 << 20),
        name="route",
    )(start, plane, *routing)
    tables = [tables[0]] + [apart(tables[m], 2 * count * m) for m in range(1, planes)]
    inside, lifted, inside_r, lifted_r, stream_r = pl.pallas_call(
        inside_kernel,
        grid=(2,),
        out_shape=[
            sds((tok, width), F32),
            sds((tok, width), BF16),
            sds((resp, width), F32),
            sds((resp, width), BF16),
            sds((resp, width), BF16),
        ],
        in_specs=[SMEM, pl.BlockSpec((half, tok), lambda i: (i, 0)), col, col, col, col],
        out_specs=[col, col, wcol, wcol, wcol],
        compiler_params=params(),
        cost_estimate=cost(4 * tok * tok * width, 6 << 20),
        name="inside",
    )(start, log_decay, query_rows, key_rows, value_rows, stream_in)
    gathered, inside, lifted, inside_r, lifted_r, stream_r = lax.optimization_barrier(
        (gathered, inside, lifted, inside_r, lifted_r, stream_r)
    )
    scanned = pl.pallas_call(
        scan_kernel,
        grid=(1,),
        out_shape=sds((pairs, rows, hd), BF16),
        in_specs=[full(gathered)],
        out_specs=full(sds((pairs, rows, hd), BF16)),
        compiler_params=params(8),
        name="scan",
    )(gathered)
    pref = across_pairs(scanned).reshape(half * hd, hd)
    pref, *tables = lax.optimization_barrier((pref, *tables))
    keep, give = pl.pallas_call(
        functools.partial(split_kernel, half=half),
        grid=(1,),
        out_shape=[sds((half * hd, hd), BF16)] * 2,
        in_specs=[SMEM, full(pref), HBM, HBM],
        out_specs=[full(pref)] * 2,
        scratch_shapes=[pltpu.VMEM((span + TAIL, hd), F32), DMA],
        compiler_params=params(8),
        name="split",
    )(bit, pref, own, recv)
    other = partner(give)

    again = attn_gain.reshape(1, width)
    window = (lifted_r, inside_r, stream_r, keep, other, again, ffn_gain.reshape(1, width))
    row_part = sds((resp, part), BF16)
    ready = pl.pallas_call(
        rows_kernel,
        grid=(1,),
        out_shape=[row_part] * PARTS,
        in_specs=[SMEM] + [full(a) for a in window],
        out_specs=[full(row_part)] * PARTS,
        scratch_shapes=[pltpu.VMEM((resp, width), F32)],
        compiler_params=params(8),
        name="rows",
    )(bit, *window)
    lines = [[ready[c]] + [apart(ready[c], 2 * count * m) for m in range(1, planes)] for c in range(PARTS)]
    chunk = sds((planes * CAP, part), BF16)
    arrived = []
    for c in range(PARTS):
        operands = (*tables, *lines[c])
        chunks = pl.pallas_call(
            functools.partial(gather_kernel, planes=planes, count=count),
            grid=(1,),
            out_shape=[chunk] * count,
            in_specs=[SMEM] + [full(a) for a in operands],
            out_specs=[full(chunk)] * count,
            compiler_params=params(8),
            name="gather",
        )(at, *operands)
        arrived += [chunks[0]] + [apart(chunks[m], 2 * m) for m in range(1, count)]

    gain_col = pl.BlockSpec((1, width // 2), lambda i: (0, i))
    state_all = pl.BlockSpec((half * hd, hd), lambda i: (0, 0))
    near = min(tok, resp + 16)
    first = jnp.minimum(start & -16, tok - near)
    near_col = pl.BlockSpec((near, width // 2), lambda i: (0, i))
    base, around = pl.pallas_call(
        mixed_kernel,
        grid=(2,),
        out_shape=[sds((tok, width), BF16), sds((near, width), F32)],
        in_specs=[SMEM, SMEM, col, col, col, state_all, state_all, gain_col],
        out_specs=[col, near_col],
        scratch_shapes=[pltpu.VMEM((tok, width // 2), F32)],
        compiler_params=params(32),
        cost_estimate=cost(2 * tok * width * hd, 7 << 20),
        name="mixed",
    )(bit, first, lifted, inside, stream_in, keep, other, again)
    base, around, *arrived = lax.optimization_barrier((base, around, *arrived))

    units = gate_weight.shape[1]
    step = min(256, units)
    many = count * chunk.shape[0]
    hidden = sds((2, many, units), BF16)
    *results, hid = pl.pallas_call(
        functools.partial(expert_kernel, count=count, parts=PARTS, step=step),
        grid=(1,),
        out_shape=[chunk] * count + [hidden],
        in_specs=[HBM] * (count * PARTS + 6),
        out_specs=[full(chunk)] * count + [HBM],
        scratch_shapes=[pltpu.VMEM((2, width, units), BF16)] * 2
        + [pltpu.VMEM((2, units, part), BF16), pltpu.VMEM(hidden.shape, BF16), pltpu.VMEM((many, width), BF16)]
        + [DMA((count * PARTS + 4 * (units // step) + 3,))],
        compiler_params=params(48),
        cost_estimate=cost(10 * many * width * units, 12 << 20),
        name="expert",
    )(*arrived, gate_own, up_own, down_own, gate_other, up_other, down_other)
    shares = []
    for c in range(PARTS):
        if c:
            results = pl.pallas_call(
                functools.partial(down_kernel, count=count, first=c * part),
                grid=(1,),
                out_shape=[chunk] * count,
                in_specs=[full(hid), HBM, HBM],
                out_specs=[full(chunk)] * count,
                scratch_shapes=[pltpu.VMEM((2, units, part), BF16), DMA((2,))],
                compiler_params=params(48),
                cost_estimate=cost(2 * many * width * units, 2 << 20),
                name="down",
            )(hid, down_own, down_other)
        back = [results[0]] + [apart(results[m], 2 * m) for m in range(1, count)]
        operands = (*tables, *back)
        kinds = [sds((resp, part), F32)] + [row_part] * (planes - 1)
        sums = pl.pallas_call(
            functools.partial(combine_kernel, planes=planes, count=count),
            grid=(1,),
            out_shape=kinds,
            in_specs=[SMEM] + [full(a) for a in operands],
            out_specs=[full(a) for a in kinds],
            compiler_params=params(8),
            name="combine",
        )(at, *operands)
        shares += [sums[0]] + [apart(sums[m], 2 * count * m) for m in range(1, planes)]

    return pl.pallas_call(
        functools.partial(final_kernel, parts=PARTS, planes=planes),
        grid=(1,),
        out_shape=sds((tok, width), BF16),
        in_specs=[SMEM, SMEM, HBM, full(around)] + [full(a) for a in shares],
        out_specs=HBM,
        scratch_shapes=[pltpu.VMEM((near, width), BF16), DMA],
        input_output_aliases={2: 0},
        compiler_params=params(8),
        name="final",
    )(start, first, base, around, *shares)


def solution(mesh):
    lead = P(BOTH, None)
    placed = (
        lead,
        lead,
        lead,
        lead,
        P(None, BOTH),
        P(),
        P(),
        lead,
        lead,
        P(BOTH),
        P(None, BOTH),
        P(None, BOTH),
        lead,
    )
    return jax.shard_map(shards, mesh=mesh, in_specs=placed, out_specs=lead, check_vma=False)
```

```python
import functools

import jax
import jax.numpy as jnp
from jax import lax
from jax.experimental import pallas as pl
from jax.experimental.pallas import tpu as pltpu
from jax.sharding import PartitionSpec as P

CAP = 16
TAIL = 8
DECAYS = 3
ATTN_EPS = 1e-05
NORM_EPS = 1e-06
PLANES = 4
PARTS = 2
BOTH = ("seq", "grp")
F32 = jnp.float32
BF16 = jnp.bfloat16
SMEM = pl.BlockSpec(memory_space=pltpu.SMEM)
HBM = pl.BlockSpec(memory_space=pltpu.HBM)
DMA = pltpu.SemaphoreType.DMA


def params(mb=60):
    return pltpu.CompilerParams(vmem_limit_bytes=int(mb * 1024 * 1024))


def full(x):
    return pl.BlockSpec(x.shape, lambda i, n=len(x.shape): (0,) * n)


def cost(flops, nbytes):
    return pl.CostEstimate(flops=flops, bytes_accessed=nbytes, transcendentals=0)


def mm(a, b, ca=1, cb=0):
    return lax.dot_general(a, b, (((ca,), (cb,)), ((), ())), preferred_element_type=F32)


def lower_tri(n):
    rows = lax.broadcasted_iota(jnp.int32, (n, n), 0)
    cols = lax.broadcasted_iota(jnp.int32, (n, n), 1)
    return rows >= cols


def running_cols(dec):
    tri = lower_tri(dec.shape[1]).astype(F32)
    return lax.dot_general(
        tri, dec, (((1,), (1,)), ((), ())), precision=lax.Precision.HIGHEST, preferred_element_type=F32
    )


def running_rows(dec):
    tri = lower_tri(dec.shape[1]).astype(F32)
    return lax.dot_general(
        dec, tri, (((1,), (1,)), ((), ())), precision=lax.Precision.HIGHEST, preferred_element_type=F32
    )


def partner(x):
    count = lax.axis_size("grp")
    return lax.ppermute(x, "grp", [(i, i ^ 1) for i in range(count)])


def apart(x, distance):
    return lax.ppermute(x, BOTH, [(i, i ^ distance) for i in range(lax.axis_size(BOTH))])


def across_pairs(x):
    count = lax.axis_size(BOTH)
    groups = [list(range(k, count, 2)) for k in range(2)]
    return lax.all_to_all(x, BOTH, 0, 0, tiled=True, axis_index_groups=groups)


def copy(src, dst, sems, n):
    c = pltpu.make_async_copy(src, dst, sems.at[n])
    c.start()
    return c


def states_kernel(k_ref, key_hbm, val_hbm, dec_hbm, own_hbm, send_hbm, key_ref, val_ref, dec_ref, own_ref, send_ref, sems):
    heads, tok = dec_ref.shape
    half = heads // 2
    hd = own_ref.shape[1]
    span = half * hd
    k = k_ref[0]
    get_dec = copy(dec_hbm, dec_ref, sems, 0)
    gets = []
    for n in range(2):
        cols = pl.ds(pl.multiple_of((k ^ 1 ^ n) * span, span), span)
        gets.append(copy(key_hbm.at[:, cols], key_ref.at[n], sems, 1 + 2 * n))
        gets.append(copy(val_hbm.at[:, cols], val_ref.at[n], sems, 2 + 2 * n))
    get_dec.wait()
    mine = dec_ref[pl.ds(pl.multiple_of(k * half, half), half), :]
    theirs = dec_ref[pl.ds(pl.multiple_of((1 - k) * half, half), half), :]
    run = running_cols(jnp.concatenate([mine, theirs], axis=0))
    total = run[tok - 1 : tok, :]
    fac = jnp.exp(total - run)
    tail = jnp.broadcast_to(jnp.pad(total, ((0, 0), (0, hd - heads))), (TAIL, hd))
    puts = []
    for n, dst, out, first in ((0, send_ref, send_hbm, half), (1, own_ref, own_hbm, 0)):
        gets[2 * n].wait()
        gets[2 * n + 1].wait()
        for j in range(half):
            cols = slice(j * hd, (j + 1) * hd)
            scaled = (key_ref[n, :, cols].astype(F32) * fac[:, first + j : first + j + 1]).astype(BF16)
            dst[cols, :] = mm(scaled, val_ref[n, :, cols], 0, 0)
        dst[span:, :] = tail
        puts.append(copy(dst, out, sems, 5 + n))
    for c in puts:
        c.wait()


def pair_kernel(k_ref, own_ref, recv_ref, notes_ref, out_ref, first_ref, *, half, rows):
    hd = own_ref.shape[1]
    first = k_ref[0] == 0
    base = half * hd
    mine = own_ref[base : base + 1, :]
    theirs = recv_ref[base : base + 1, :]
    pieces = out_ref.shape[0]
    planes, tail_rows = notes_ref.shape[:2]
    tail_row = lax.broadcasted_iota(jnp.int32, (tail_rows, hd), 0)
    for p in range(pieces):
        j = p * rows // hd
        mt = mine[:, j : j + 1]
        pt = theirs[:, half + j : half + j + 1]
        one = jnp.ones_like(mt)
        a = jnp.where(first, jnp.exp(pt), one)
        b = jnp.where(first, one, jnp.exp(mt))
        lo = p * rows
        chip = own_ref[lo : lo + rows, :] * a + recv_ref[lo : lo + rows, :] * b
        out_ref[p, 0:rows, :] = chip.astype(BF16)
        d = jnp.broadcast_to(jnp.exp(mt + pt), (tail_rows, hd))
        notes = notes_ref[p * planes // pieces].astype(F32)
        d0 = d.astype(BF16).astype(F32)
        d1 = (d - d0).astype(BF16).astype(F32)
        d2 = d - d0 - d1
        first_ref[lo : lo + rows, :] = jnp.where(first, own_ref[lo : lo + rows, :], recv_ref[lo : lo + rows, :])
        tail = jnp.where(tail_row == 0, d0, jnp.where(tail_row == 1, d1, jnp.where(tail_row == 2, d2, notes)))
        out_ref[p, rows:, :] = tail.astype(BF16)
    rolled = pltpu.roll(theirs, hd - half, 1)
    first_ref[base:, :] = jnp.broadcast_to(jnp.where(first, mine, rolled), (TAIL, hd))


def scan_kernel(in_ref, out_ref):
    count, rows, hd = out_ref.shape
    state = jnp.zeros((rows, hd), F32)
    for c in range(count):
        out_ref[c, :, :] = state.astype(BF16)
        tail = in_ref[c, rows:, :].astype(F32)
        d = tail[0:1, :] + tail[1:2, :] + tail[2:3, :]
        state = state * d + in_ref[c, 0:rows, :].astype(F32)


def split_kernel(k_ref, pref_ref, first_ref, keep_ref, give_ref, *, half):
    hd = first_ref.shape[1]
    even = k_ref[0] == 0
    logs = first_ref[half * hd : half * hd + 1, :]
    for j in range(half):
        sl = slice(j * hd, (j + 1) * hd)
        before = pref_ref[sl, :].astype(F32)
        after = before * jnp.exp(logs[:, j : j + 1]) + first_ref[sl, :]
        keep_ref[sl, :] = jnp.where(even, before, after).astype(BF16)
        give_ref[sl, :] = jnp.where(even, after, before).astype(BF16)


def inside_kernel(start_ref, dec_ref, q_ref, key_ref, val_ref, stream_ref, inside_ref, lifted_ref, near_ref):
    heads, tok = dec_ref.shape
    hd = q_ref.shape[1] // heads
    dec = dec_ref[...]
    run_c = running_cols(dec)
    run_r = running_rows(dec)
    lift = jnp.exp(run_c)
    cut = tok // 2
    tri = lower_tri(cut)
    resp = near_ref.shape[0] // 3
    start = start_ref[0]
    picked = lax.broadcasted_iota(jnp.int32, (resp, tok), 0) + start
    pick = jnp.where(lax.broadcasted_iota(jnp.int32, (resp, tok), 1) == picked, 1.0, 0.0).astype(BF16)
    for h in range(heads):
        cols = slice(h * hd, (h + 1) * hd)
        q = q_ref[:, cols]
        kk = key_ref[:, cols]
        v = val_ref[:, cols]
        lifted = (q.astype(F32) * lift[:, h : h + 1]).astype(BF16)
        lifted_ref[:, cols] = lifted
        rc = run_c[:, h : h + 1]
        rr = run_r[h : h + 1, :]
        f_aa = jnp.where(tri, jnp.exp(rc[:cut] - rr[:, :cut]), 0.0)
        f_bb = jnp.where(tri, jnp.exp(rc[cut:] - rr[:, cut:]), 0.0)
        f_ba = jnp.exp(rc[cut:] - rr[:, :cut])
        w_aa = (mm(q[:cut], kk[:cut], 1, 1) * f_aa).astype(BF16)
        s_b = mm(q[cut:], kk, 1, 1)
        w_b = (s_b * jnp.concatenate([f_ba, f_bb], axis=1)).astype(BF16)
        inside_ref[:cut, cols] = mm(w_aa, v[:cut])
        inside_ref[cut:, cols] = mm(w_b, v)
    near_ref[resp : 2 * resp, :] = mm(pick, lifted_ref[...])
    near_ref[2 * resp :, :] = mm(pick, stream_ref[...])
    rest = inside_ref[...]
    high = rest.astype(BF16)
    rest = rest - high.astype(F32)
    mid = rest.astype(BF16)
    low = (rest - mid.astype(F32)).astype(BF16)
    near_ref[:resp, :] = mm(pick, high) + mm(pick, mid) + mm(pick, low)


def head_norm(att):
    return att * lax.rsqrt(jnp.mean(att * att, axis=-1, keepdims=True) + ATTN_EPS)


def rows_kernel(k_ref, near_ref, keep_ref, other_ref, again_ref, fgain_ref, disp_ref, sent_ref, mixed_ref):
    hd = keep_ref.shape[1]
    half = keep_ref.shape[0] // hd
    k = k_ref[0]
    resp = near_ref.shape[0] // 3
    for r in range(2 * half):
        side = r // half
        off = pl.multiple_of((side ^ k) * (half * hd) + (r % half) * hd, hd)
        cols = pl.ds(off, hd)
        src = keep_ref if side == 0 else other_ref
        lifted = near_ref[resp : 2 * resp, cols].astype(BF16)
        att = near_ref[:resp, cols] + mm(lifted, src[(r % half) * hd : (r % half + 1) * hd, :])
        mixed_ref[:, cols] = near_ref[2 * resp :, cols] + head_norm(att) * again_ref[:, cols]
    mixed = mixed_ref[...]
    scale = lax.rsqrt(jnp.mean(mixed * mixed, axis=-1, keepdims=True) + NORM_EPS)
    ffn = (mixed * scale * fgain_ref[...]).astype(BF16)
    sent_ref[...] = mm(disp_ref[...], ffn).astype(BF16)


def mixed_kernel(k_ref, from_ref, lifted_ref, inside_ref, stream_ref, keep_ref, other_ref, again_ref, base_ref, near_ref, mixed_ref):
    hd = keep_ref.shape[1]
    half = keep_ref.shape[0] // hd
    mine = pl.program_id(0) == k_ref[0]
    for j in range(half):
        cols = slice(j * hd, (j + 1) * hd)
        st = jnp.where(mine, keep_ref[cols, :].astype(F32), other_ref[cols, :].astype(F32)).astype(BF16)
        att = inside_ref[:, cols] + mm(lifted_ref[:, cols], st)
        mixed_ref[:, cols] = stream_ref[:, cols].astype(F32) + head_norm(att) * again_ref[:, cols]
    base_ref[...] = mixed_ref[...].astype(BF16)
    near_ref[...] = mixed_ref[pl.ds(pl.multiple_of(from_ref[0], 16), near_ref.shape[0]), :]


def noted(experts, resp, lanes):
    side = max(1, lanes // resp)
    return side, -(-experts // side)


def shift_table(resp, lanes, g, rows):
    j = lax.broadcasted_iota(jnp.int32, (resp, lanes) if rows else (lanes, resp), 0 if rows else 1)
    lane = lax.broadcasted_iota(jnp.int32, (resp, lanes) if rows else (lanes, resp), 1 if rows else 0)
    return jnp.where(lane == j + g * resp, 1.0, 0.0).astype(BF16)


def route_kernel(ids_ref, wts_ref, live_ref, disp_ref, notes_ref, *, experts):
    top, tok = ids_ref.shape
    slots, resp = disp_ref.shape
    planes, tail_rows, lanes = notes_ref.shape
    count = experts // planes
    live = live_ref[...] == 1
    e_row = lax.broadcasted_iota(jnp.int32, (experts, tok), 0)
    chosen = jnp.zeros((experts, tok), F32)
    weight = jnp.zeros((experts, tok), F32)
    for j in range(top):
        hit = (ids_ref[j : j + 1, :] == e_row) & live
        chosen = jnp.where(hit, 1.0, chosen)
        weight = jnp.where(hit, wts_ref[j : j + 1, :], weight)
    rows = lax.broadcasted_iota(jnp.int32, (tok, tok), 0)
    cols = lax.broadcasted_iota(jnp.int32, (tok, tok), 1)
    before = jnp.where(rows < cols, 1.0, 0.0).astype(BF16)
    place = mm(chosen.astype(BF16), before)
    place = jnp.where(chosen > 0.0, place, -1.0)
    s_row = lax.broadcasted_iota(jnp.int32, (slots, experts), 0)
    e_col = lax.broadcasted_iota(jnp.int32, (slots, experts), 1)
    spread = jnp.where(s_row // CAP == e_col, 1.0, 0.0).astype(BF16)
    slot_of = lax.broadcasted_iota(jnp.int32, (slots, tok), 0) % CAP
    hit = mm(spread, place.astype(BF16)) == slot_of.astype(F32)
    w_hi = weight.astype(BF16)
    w_lo = (weight - w_hi.astype(F32)).astype(BF16)
    token = lax.broadcasted_iota(jnp.int32, (1, tok), 1)
    start = jnp.min(jnp.where(live, token, tok - resp), axis=1, keepdims=True)
    start = jnp.minimum(start, tok - resp)
    picked = lax.broadcasted_iota(jnp.int32, (tok, resp), 1) + start
    pick = jnp.where(lax.broadcasted_iota(jnp.int32, (tok, resp), 0) == picked, 1.0, 0.0).astype(BF16)
    disp_ref[...] = mm(jnp.where(hit, 1.0, 0.0).astype(BF16), pick).astype(BF16)
    side, each = noted(count, resp, lanes)
    tail_row = lax.broadcasted_iota(jnp.int32, (tail_rows, lanes), 0)
    notes = [jnp.zeros((tail_rows, lanes), F32)] * planes
    for n, part in enumerate((w_hi, w_lo)):
        part = mm(part, pick).astype(BF16)
        placed = [mm(part, shift_table(resp, lanes, g, True)) for g in range(side)]
        for e in range(experts):
            at = e % count
            line = placed[at % side][e : e + 1, :]
            here = tail_row == DECAYS + n * each + at // side
            notes[e // count] = notes[e // count] + jnp.where(here, line, 0.0)
    for p in range(planes):
        notes_ref[p, :, :] = notes[p].astype(BF16)


def plan_kernel(at_ref, plane_ref, in_ref, *outs, planes, rows):
    lanes = in_ref.shape[2]
    resp = outs[0].shape[1]
    span = outs[0].shape[0] // 2
    count = span // CAP
    side, each = noted(count, resp, lanes)
    e_row = lax.broadcasted_iota(jnp.int32, (count, resp), 0)
    before = lax.broadcasted_iota(jnp.int32, (resp, resp), 0) < lax.broadcasted_iota(jnp.int32, (resp, resp), 1)
    before = jnp.where(before, 1.0, 0.0).astype(BF16)
    s_row = lax.broadcasted_iota(jnp.int32, (span, count), 0)
    e_col = lax.broadcasted_iota(jnp.int32, (span, count), 1)
    spread = jnp.where(s_row // CAP == e_col, 1.0, 0.0).astype(BF16)
    slot_of = (lax.broadcasted_iota(jnp.int32, (span, resp), 0) % CAP).astype(F32)
    for m in range(planes):
        pair = (plane_ref[0] ^ m) * count + at_ref[0]
        tail = in_ref[pair, rows:, :]
        moved = [mm(tail, shift_table(resp, lanes, g, False)) for g in range(side)]
        parts = []
        for n in range(2):
            part = jnp.zeros((count, resp), F32)
            for e in range(count):
                r = DECAYS + n * each + e // side
                part = part + jnp.where(e_row == e, moved[e % side][r : r + 1, :], 0.0)
            parts.append(part.astype(BF16))
        chosen = parts[0].astype(F32) > 0.0
        place = mm(jnp.where(chosen, 1.0, 0.0).astype(BF16), before)
        hit = mm(spread, jnp.where(chosen, place, -1.0).astype(BF16)) == slot_of
        for n in range(2):
            outs[m][n * span : (n + 1) * span, :] = jnp.where(hit, mm(spread, parts[n]), 0.0).astype(BF16)


def table_rows(tab_ref, n, at, count):
    lead = n * count * CAP
    rows = [tab_ref[pl.ds(pl.multiple_of(lead + (at ^ m) * CAP, CAP), CAP), :] for m in range(count)]
    return jnp.concatenate(rows, axis=0)


def combine_kernel(at_ref, *refs, planes, count):
    tabs, results, outs = refs[:planes], refs[planes : planes + count], refs[planes + count :]
    for m in range(planes):
        got = jnp.concatenate([results[q][m * CAP : (m + 1) * CAP, :] for q in range(count)], axis=0)
        hi = table_rows(tabs[m], 0, at_ref[0], count)
        lo = table_rows(tabs[m], 1, at_ref[0], count)
        outs[m][...] = (mm(hi, got, 0, 0) + mm(lo, got, 0, 0)).astype(outs[m].dtype)


def expert_kernel(at_ref, plane_ref, x_hbm, g0, u0, d0, g1, u1, d1, *refs, count, parts, step):
    outs, (gv, uv, dv, hid_ref, x_ref, sems) = refs[: count * parts], refs[count * parts :]
    units = g0.shape[1]
    rows, part = outs[0].shape
    cuts = range(0, units, step)
    gets = []
    for q in range(count):
        for m in range(rows // CAP):
            pair = (plane_ref[0] ^ m) * count + (at_ref[0] ^ q)
            gets.append(copy(x_hbm.at[pair], x_ref.at[pl.ds(q * rows + m * CAP, CAP)], sems, len(gets)))
    at = len(gets)
    for n, (g, u) in enumerate(((g0, u0), (g1, u1))):
        for c in cuts:
            cols = pl.ds(c, step)
            gets.append(copy(g.at[:, cols], gv.at[n, :, cols], sems, len(gets)))
            gets.append(copy(u.at[:, cols], uv.at[n, :, cols], sems, len(gets)))
    for n, d in enumerate((d0, d1)):
        gets.append(copy(d, dv.at[n], sems, len(gets)))
    for c in gets[:at]:
        c.wait()
    many = count * rows
    block = min(256, many)
    for n in range(2):
        for c in cuts:
            gets[at].wait()
            gets[at + 1].wait()
            at += 2
            for r in range(0, many, block):
                x = x_ref[r : r + block, :]
                gate = mm(x, gv[n, :, c : c + step])
                up = mm(x, uv[n, :, c : c + step])
                hid_ref[n, r : r + block, c : c + step] = (gate / (1.0 + jnp.exp(-gate)) * up).astype(BF16)
    gets[at].wait()
    gets[at + 1].wait()
    for r in range(0, many, block):
        for c in range(0, part * parts, 256):
            p0 = mm(hid_ref[0, r : r + block, :], dv[0, :, c : c + 256]).astype(BF16).astype(F32)
            p1 = mm(hid_ref[1, r : r + block, :], dv[1, :, c : c + 256]).astype(BF16).astype(F32)
            p = (p0 + p1).astype(BF16)
            for q in range(r // rows, (r + block) // rows):
                out_ref = outs[c // part * count + q]
                out_ref[:, c % part : c % part + 256] = p[q * rows - r : (q + 1) * rows - r, :]


def final_kernel(start_ref, from_ref, base_hbm, near_ref, *refs, parts, planes):
    shares, (out_hbm, res_ref, sem) = refs[: parts * planes], refs[parts * planes :]
    many, width = near_ref.shape
    resp, part = shares[0].shape
    row = lax.broadcasted_iota(jnp.int32, (many, resp), 0)
    place = lax.broadcasted_iota(jnp.int32, (many, resp), 1) + (start_ref[0] - from_ref[0])
    spread = jnp.where(row == place, 1.0, 0.0).astype(BF16)
    for c in range(parts):
        cols = slice(c * part, (c + 1) * part)
        total = shares[c * planes][...]
        for m in range(1, planes):
            total = total + shares[c * planes + m][...].astype(F32)
        hi = total.astype(BF16)
        lo = (total - hi.astype(F32)).astype(BF16)
        res_ref[:, cols] = (near_ref[:, cols] + mm(spread, hi) + mm(spread, lo)).astype(BF16)
    put = pltpu.make_async_copy(res_ref, out_hbm.at[pl.ds(pl.multiple_of(from_ref[0], 16), many)], sem)
    put.start()
    put.wait()


def shards(
    stream_in,
    query_rows,
    key_rows,
    value_rows,
    log_decay,
    attn_gain,
    ffn_gain,
    expert_ids,
    route_weights,
    response_mask,
    gate_weight,
    up_weight,
    down_weight,
):
    tok, width = stream_in.shape
    heads = log_decay.shape[0]
    hd = width // heads
    half = heads // 2
    devices = lax.axis_size(BOTH)
    pairs = devices // 2
    experts = devices // 2
    slots = experts * CAP
    top = expert_ids.shape[1]
    resp = min(tok, slots // top)
    rows = half * hd // pairs
    planes = PLANES
    count = pairs // planes
    part = width // PARTS
    me = lax.axis_index(BOTH)
    bit = (me & 1).reshape(1).astype(jnp.int32)
    sds = jax.ShapeDtypeStruct

    span = half * hd
    own, send = pl.pallas_call(
        states_kernel,
        out_shape=[sds((span + TAIL, hd), F32)] * 2,
        in_specs=[SMEM, HBM, HBM, HBM],
        out_specs=[HBM, HBM],
        scratch_shapes=[pltpu.VMEM((2, tok, span), BF16)] * 2
        + [pltpu.VMEM((heads, tok), F32)]
        + [pltpu.VMEM((span + TAIL, hd), F32)] * 2
        + [DMA((7,))],
        compiler_params=params(),
        cost_estimate=cost(2 * tok * width * hd, 3 << 20),
        name="states",
    )(bit, key_rows, value_rows, log_decay)
    recv = partner(send)
    start = jnp.minimum(jnp.argmax(response_mask), tok - resp).astype(jnp.int32).reshape(1)
    plane = lax.shift_right_logical(me, (2 * count).bit_length() - 1).reshape(1).astype(jnp.int32)
    at = (lax.shift_right_logical(me, 1) & (count - 1)).reshape(1).astype(jnp.int32)
    routing = (expert_ids.T, route_weights.T, response_mask.reshape(1, tok))
    table = sds((2 * count * CAP, resp), BF16)
    slot_rows = sds((slots, resp), BF16)
    tail = -(-(DECAYS + 2 * noted(count, resp, hd)[1]) // 16) * 16
    note = sds((planes, tail, hd), BF16)
    disp, notes = pl.pallas_call(
        functools.partial(route_kernel, experts=experts),
        grid=(1,),
        out_shape=[slot_rows, note],
        in_specs=[full(a) for a in routing],
        out_specs=[full(slot_rows), full(note)],
        compiler_params=params(),
        cost_estimate=cost(8 * tok * tok * slots, 1 << 20),
        name="route",
    )(*routing)
    recv, gate_own, up_own, down_own, disp, notes = lax.optimization_barrier(
        (recv, gate_weight, up_weight, down_weight, disp, notes)
    )
    gate_other, up_other, down_other = partner(gate_own), partner(up_own), partner(down_own)
    payload = sds((pairs, rows + tail, hd), BF16)
    packed, earlier = pl.pallas_call(
        functools.partial(pair_kernel, half=half, rows=rows),
        grid=(1,),
        out_shape=[payload, sds(own.shape, F32)],
        in_specs=[SMEM, full(own), full(recv), full(note)],
        out_specs=[full(payload), full(own)],
        compiler_params=params(63.4),
        name="pair",
    )(bit, own, recv, notes)
    gathered = across_pairs(packed)
    col = pl.BlockSpec((tok, width // 2), lambda i: (0, i))
    wcol = pl.BlockSpec((3 * resp, width // 2), lambda i: (0, i))
    inside, lifted, nearby = pl.pallas_call(
        inside_kernel,
        grid=(2,),
        out_shape=[
            sds((tok, width), F32),
            sds((tok, width), BF16),
            sds((3 * resp, width), F32),
        ],
        in_specs=[SMEM, pl.BlockSpec((half, tok), lambda i: (i, 0)), col, col, col, col],
        out_specs=[col, col, wcol],
        compiler_params=params(),
        cost_estimate=cost(4 * tok * tok * width, 6 << 20),
        name="inside",
    )(start, log_decay, query_rows, key_rows, value_rows, stream_in)
    gathered, inside, lifted, nearby = lax.optimization_barrier((gathered, inside, lifted, nearby))
    tables = pl.pallas_call(
        functools.partial(plan_kernel, planes=planes, rows=rows),
        grid=(1,),
        out_shape=[table] * planes,
        in_specs=[SMEM, SMEM, full(gathered)],
        out_specs=[full(table)] * planes,
        compiler_params=params(),
        cost_estimate=cost(1 << 24, 1 << 20),
        name="plan",
    )(at, plane, gathered)
    scanned = pl.pallas_call(
        scan_kernel,
        grid=(1,),
        out_shape=sds((pairs, rows, hd), BF16),
        in_specs=[full(gathered)],
        out_specs=full(sds((pairs, rows, hd), BF16)),
        compiler_params=params(8),
        name="scan",
    )(gathered)
    pref = across_pairs(scanned).reshape(half * hd, hd)
    pref, gate_other, up_other, down_other = lax.optimization_barrier((pref, gate_other, up_other, down_other))
    keep, give = pl.pallas_call(
        functools.partial(split_kernel, half=half),
        grid=(1,),
        out_shape=[sds((half * hd, hd), BF16)] * 2,
        in_specs=[SMEM, full(pref), full(earlier)],
        out_specs=[full(pref)] * 2,
        compiler_params=params(8),
        name="split",
    )(bit, pref, earlier)
    other = partner(give)

    again = attn_gain.reshape(1, width)
    window = (nearby, keep, other, again, ffn_gain.reshape(1, width), disp)
    sent = pl.pallas_call(
        rows_kernel,
        grid=(1,),
        out_shape=sds((slots, width), BF16),
        in_specs=[SMEM] + [full(a) for a in window],
        out_specs=full(sds((slots, width), BF16)),
        scratch_shapes=[pltpu.VMEM((resp, width), F32)],
        compiler_params=params(8),
        name="rows",
    )(bit, *window)
    arrived = across_pairs(sent.reshape(pairs, CAP, width))

    gain_col = pl.BlockSpec((1, width // 2), lambda i: (0, i))
    state_all = pl.BlockSpec((half * hd, hd), lambda i: (0, 0))
    near = min(tok, resp + 16)
    first = jnp.minimum(start & -16, tok - near)
    near_col = pl.BlockSpec((near, width // 2), lambda i: (0, i))
    base, around = pl.pallas_call(
        mixed_kernel,
        grid=(2,),
        out_shape=[sds((tok, width), BF16), sds((near, width), F32)],
        in_specs=[SMEM, SMEM, col, col, col, state_all, state_all, gain_col],
        out_specs=[col, near_col],
        scratch_shapes=[pltpu.VMEM((tok, width // 2), F32)],
        compiler_params=params(60),
        cost_estimate=cost(2 * tok * width * hd, 7 << 20),
        name="mixed",
    )(bit, first, lifted, inside, stream_in, keep, other, again)
    arrived, base, around, *tables = lax.optimization_barrier((arrived, base, around, *tables))

    row_part = sds((resp, part), BF16)
    chunk = sds((planes * CAP, part), BF16)
    units = gate_weight.shape[1]
    step = min(256, units)
    many = count * chunk.shape[0]
    results = pl.pallas_call(
        functools.partial(expert_kernel, count=count, parts=PARTS, step=step),
        grid=(1,),
        out_shape=[chunk] * (count * PARTS),
        in_specs=[SMEM, SMEM] + [HBM] * 7,
        out_specs=[full(chunk)] * (count * PARTS),
        scratch_shapes=[pltpu.VMEM((2, width, units), BF16)] * 2
        + [pltpu.VMEM((2, units, width), BF16), pltpu.VMEM((2, many, units), BF16), pltpu.VMEM((many, width), BF16)]
        + [DMA((pairs + 4 * (units // step) + 2,))],
        compiler_params=params(48),
        cost_estimate=cost(12 * many * width * units, 14 << 20),
        name="expert",
    )(at, plane, arrived, gate_own, up_own, down_own, gate_other, up_other, down_other)
    backs = []
    for c in range(PARTS):
        mine = results[c * count : (c + 1) * count]
        backs.append([mine[0]] + [apart(mine[m], 2 * m) for m in range(1, count)])
    shares = []
    for c in range(PARTS):
        operands = (*tables, *backs[c])
        kinds = [sds((resp, part), F32)] + [row_part] * (planes - 1)
        sums = pl.pallas_call(
            functools.partial(combine_kernel, planes=planes, count=count),
            grid=(1,),
            out_shape=kinds,
            in_specs=[SMEM] + [full(a) for a in operands],
            out_specs=[full(a) for a in kinds],
            compiler_params=params(8),
            name="combine",
        )(at, *operands)
        shares += [sums[0]] + [apart(sums[m], 2 * count * m) for m in range(1, planes)]

    return pl.pallas_call(
        functools.partial(final_kernel, parts=PARTS, planes=planes),
        grid=(1,),
        out_shape=sds((tok, width), BF16),
        in_specs=[SMEM, SMEM, HBM, full(around)] + [full(a) for a in shares],
        out_specs=HBM,
        scratch_shapes=[pltpu.VMEM((near, width), BF16), DMA],
        input_output_aliases={2: 0},
        compiler_params=params(8),
        name="final",
    )(start, first, base, around, *shares)


def solution(mesh):
    lead = P(BOTH, None)
    placed = (
        lead,
        lead,
        lead,
        lead,
        P(None, BOTH),
        P(),
        P(),
        lead,
        lead,
        P(BOTH),
        P(None, BOTH),
        P(None, BOTH),
        lead,
    )
    return jax.shard_map(shards, mesh=mesh, in_specs=placed, out_specs=lead, check_vma=False)
```

```python
import functools

import jax
import jax.numpy as jnp
from jax import lax
from jax.experimental import pallas as pl
from jax.experimental.pallas import tpu as pltpu
from jax.sharding import PartitionSpec as P

CAP = 16
TAIL = 8
DECAYS = 3
ATTN_EPS = 1e-05
NORM_EPS = 1e-06
PLANES = 4
PARTS = 2
BOTH = ("seq", "grp")
F32 = jnp.float32
BF16 = jnp.bfloat16
SMEM = pl.BlockSpec(memory_space=pltpu.SMEM)
HBM = pl.BlockSpec(memory_space=pltpu.HBM)
DMA = pltpu.SemaphoreType.DMA


def params(mb=60):
    return pltpu.CompilerParams(vmem_limit_bytes=int(mb * 1024 * 1024))


def full(x):
    return pl.BlockSpec(x.shape, lambda i, n=len(x.shape): (0,) * n)


def cost(flops, nbytes):
    return pl.CostEstimate(flops=flops, bytes_accessed=nbytes, transcendentals=0)


def mm(a, b, ca=1, cb=0):
    return lax.dot_general(a, b, (((ca,), (cb,)), ((), ())), preferred_element_type=F32)


def lower_tri(n):
    rows = lax.broadcasted_iota(jnp.int32, (n, n), 0)
    cols = lax.broadcasted_iota(jnp.int32, (n, n), 1)
    return rows >= cols


def running_cols(dec):
    tri = lower_tri(dec.shape[1]).astype(F32)
    return lax.dot_general(
        tri, dec, (((1,), (1,)), ((), ())), precision=lax.Precision.HIGHEST, preferred_element_type=F32
    )


def running_rows(dec):
    tri = lower_tri(dec.shape[1]).astype(F32)
    return lax.dot_general(
        dec, tri, (((1,), (1,)), ((), ())), precision=lax.Precision.HIGHEST, preferred_element_type=F32
    )


def partner(x):
    count = lax.axis_size("grp")
    return lax.ppermute(x, "grp", [(i, i ^ 1) for i in range(count)])


def apart(x, distance):
    return lax.ppermute(x, BOTH, [(i, i ^ distance) for i in range(lax.axis_size(BOTH))])


def across_pairs(x):
    count = lax.axis_size(BOTH)
    groups = [list(range(k, count, 2)) for k in range(2)]
    return lax.all_to_all(x, BOTH, 0, 0, tiled=True, axis_index_groups=groups)


def copy(src, dst, sems, n):
    c = pltpu.make_async_copy(src, dst, sems.at[n])
    c.start()
    return c


def states_kernel(k_ref, key_hbm, val_hbm, dec_hbm, own_hbm, send_hbm, key_ref, val_ref, dec_ref, own_ref, send_ref, sems):
    heads, tok = dec_ref.shape
    half = heads // 2
    hd = own_ref.shape[1]
    span = half * hd
    k = k_ref[0]
    get_dec = copy(dec_hbm, dec_ref, sems, 0)
    gets = []
    for n in range(2):
        cols = pl.ds(pl.multiple_of((k ^ 1 ^ n) * span, span), span)
        gets.append(copy(key_hbm.at[:, cols], key_ref.at[n], sems, 1 + 2 * n))
        gets.append(copy(val_hbm.at[:, cols], val_ref.at[n], sems, 2 + 2 * n))
    get_dec.wait()
    mine = dec_ref[pl.ds(pl.multiple_of(k * half, half), half), :]
    theirs = dec_ref[pl.ds(pl.multiple_of((1 - k) * half, half), half), :]
    run = running_cols(jnp.concatenate([mine, theirs], axis=0))
    total = run[tok - 1 : tok, :]
    fac = jnp.exp(total - run)
    tail = jnp.broadcast_to(jnp.pad(total, ((0, 0), (0, hd - heads))), (TAIL, hd))
    puts = []
    for n, dst, out, first in ((0, send_ref, send_hbm, half), (1, own_ref, own_hbm, 0)):
        gets[2 * n].wait()
        gets[2 * n + 1].wait()
        for j in range(half):
            cols = slice(j * hd, (j + 1) * hd)
            scaled = (key_ref[n, :, cols].astype(F32) * fac[:, first + j : first + j + 1]).astype(BF16)
            dst[cols, :] = mm(val_ref[n, :, cols], scaled, 0, 0)
        dst[span:, :] = tail
        puts.append(copy(dst, out, sems, 5 + n))
    for c in puts:
        c.wait()


def pair_kernel(k_ref, own_ref, recv_ref, notes_ref, out_ref, first_ref, *, half, rows):
    hd = own_ref.shape[1]
    first = k_ref[0] == 0
    base = half * hd
    mine = own_ref[base : base + 1, :]
    theirs = recv_ref[base : base + 1, :]
    pieces = out_ref.shape[0]
    planes, tail_rows = notes_ref.shape[:2]
    tail_row = lax.broadcasted_iota(jnp.int32, (tail_rows, hd), 0)
    for p in range(pieces):
        j = p * rows // hd
        mt = mine[:, j : j + 1]
        pt = theirs[:, half + j : half + j + 1]
        one = jnp.ones_like(mt)
        a = jnp.where(first, jnp.exp(pt), one)
        b = jnp.where(first, one, jnp.exp(mt))
        lo = p * rows
        chip = own_ref[lo : lo + rows, :] * a + recv_ref[lo : lo + rows, :] * b
        out_ref[p, 0:rows, :] = chip.astype(BF16)
        d = jnp.broadcast_to(jnp.exp(mt + pt), (tail_rows, hd))
        notes = notes_ref[p * planes // pieces].astype(F32)
        d0 = d.astype(BF16).astype(F32)
        d1 = (d - d0).astype(BF16).astype(F32)
        d2 = d - d0 - d1
        first_ref[lo : lo + rows, :] = jnp.where(first, own_ref[lo : lo + rows, :], recv_ref[lo : lo + rows, :])
        tail = jnp.where(tail_row == 0, d0, jnp.where(tail_row == 1, d1, jnp.where(tail_row == 2, d2, notes)))
        out_ref[p, rows:, :] = tail.astype(BF16)
    rolled = pltpu.roll(theirs, hd - half, 1)
    first_ref[base:, :] = jnp.broadcast_to(jnp.where(first, mine, rolled), (TAIL, hd))


def scan_kernel(in_ref, out_ref):
    count, rows, hd = out_ref.shape
    state = jnp.zeros((rows, hd), F32)
    for c in range(count):
        out_ref[c, :, :] = state.astype(BF16)
        tail = in_ref[c, rows:, :].astype(F32)
        d = tail[0:1, :] + tail[1:2, :] + tail[2:3, :]
        state = state * d + in_ref[c, 0:rows, :].astype(F32)


def split_kernel(k_ref, pref_ref, first_ref, keep_ref, give_ref, *, half):
    hd = first_ref.shape[1]
    even = k_ref[0] == 0
    logs = first_ref[half * hd : half * hd + 1, :]
    for j in range(half):
        sl = slice(j * hd, (j + 1) * hd)
        before = pref_ref[sl, :].astype(F32)
        after = before * jnp.exp(logs[:, j : j + 1]) + first_ref[sl, :]
        keep_ref[sl, :] = jnp.where(even, before, after).astype(BF16)
        give_ref[sl, :] = jnp.where(even, after, before).astype(BF16)


def window_start(live, resp):
    tok = live.shape[1]
    token = lax.broadcasted_iota(jnp.int32, (1, tok), 1)
    return jnp.min(jnp.where(live, token, tok - resp), axis=1, keepdims=True).clip(0, tok - resp)


def inside_kernel(live_ref, dec_ref, q_ref, key_ref, val_ref, stream_ref, inside_ref, lifted_ref, near_ref):
    heads, tok = dec_ref.shape
    hd = q_ref.shape[1] // heads
    dec = dec_ref[...]
    run_c = running_cols(dec)
    run_r = running_rows(dec)
    lift = jnp.exp(run_c)
    cut = tok // 2
    tri = lower_tri(cut)
    resp = near_ref.shape[0] // 3
    picked = lax.broadcasted_iota(jnp.int32, (resp, tok), 0) + window_start(live_ref[...] == 1, resp)
    pick = jnp.where(lax.broadcasted_iota(jnp.int32, (resp, tok), 1) == picked, 1.0, 0.0).astype(BF16)
    for h in range(heads):
        cols = slice(h * hd, (h + 1) * hd)
        q = q_ref[:, cols]
        kk = key_ref[:, cols]
        v = val_ref[:, cols]
        lifted = (q.astype(F32) * lift[:, h : h + 1]).astype(BF16)
        lifted_ref[:, cols] = lifted
        rc = run_c[:, h : h + 1]
        rr = run_r[h : h + 1, :]
        f_aa = jnp.where(tri, jnp.exp(rc[:cut] - rr[:, :cut]), 0.0)
        f_bb = jnp.where(tri, jnp.exp(rc[cut:] - rr[:, cut:]), 0.0)
        f_ba = jnp.exp(rc[cut:] - rr[:, :cut])
        w_aa = (mm(q[:cut], kk[:cut], 1, 1) * f_aa).astype(BF16)
        s_b = mm(q[cut:], kk, 1, 1)
        w_b = (s_b * jnp.concatenate([f_ba, f_bb], axis=1)).astype(BF16)
        inside_ref[:cut, cols] = mm(w_aa, v[:cut])
        inside_ref[cut:, cols] = mm(w_b, v)
    near_ref[resp : 2 * resp, :] = mm(pick, lifted_ref[...])
    near_ref[2 * resp :, :] = mm(pick, stream_ref[...])
    rest = inside_ref[...]
    high = rest.astype(BF16)
    rest = rest - high.astype(F32)
    mid = rest.astype(BF16)
    low = (rest - mid.astype(F32)).astype(BF16)
    near_ref[:resp, :] = mm(pick, high) + mm(pick, mid) + mm(pick, low)


def head_norm(att):
    return att * lax.rsqrt(jnp.mean(att * att, axis=-1, keepdims=True) + ATTN_EPS)


def rows_kernel(k_ref, near_ref, keep_ref, other_ref, again_ref, fgain_ref, disp_ref, sent_ref, mixed_ref):
    hd = keep_ref.shape[1]
    half = keep_ref.shape[0] // hd
    k = k_ref[0]
    resp = near_ref.shape[0] // 3
    for r in range(2 * half):
        side = r // half
        off = pl.multiple_of((side ^ k) * (half * hd) + (r % half) * hd, hd)
        cols = pl.ds(off, hd)
        src = keep_ref if side == 0 else other_ref
        lifted = near_ref[resp : 2 * resp, cols].astype(BF16)
        att = near_ref[:resp, cols] + mm(lifted, src[(r % half) * hd : (r % half + 1) * hd, :], 1, 1)
        mixed_ref[:, cols] = near_ref[2 * resp :, cols] + head_norm(att) * again_ref[:, cols]
    mixed = mixed_ref[...]
    scale = lax.rsqrt(jnp.mean(mixed * mixed, axis=-1, keepdims=True) + NORM_EPS)
    ffn = (mixed * scale * fgain_ref[...]).astype(BF16)
    sent_ref[...] = mm(disp_ref[...], ffn).astype(BF16)


def mixed_kernel(k_ref, from_ref, lifted_ref, inside_ref, stream_ref, keep_ref, other_ref, again_ref, base_ref, near_ref, mixed_ref):
    hd = keep_ref.shape[1]
    half = keep_ref.shape[0] // hd
    mine = pl.program_id(0) == k_ref[0]
    for j in range(half):
        cols = slice(j * hd, (j + 1) * hd)
        st = jnp.where(mine, keep_ref[cols, :].astype(F32), other_ref[cols, :].astype(F32)).astype(BF16)
        att = inside_ref[:, cols] + mm(lifted_ref[:, cols], st, 1, 1)
        mixed_ref[:, cols] = stream_ref[:, cols].astype(F32) + head_norm(att) * again_ref[:, cols]
    base_ref[...] = mixed_ref[...].astype(BF16)
    near_ref[...] = mixed_ref[pl.ds(pl.multiple_of(from_ref[0], 16), near_ref.shape[0]), :]


def noted(experts, resp, lanes):
    side = max(1, lanes // resp)
    return side, -(-experts // side)


def shift_table(resp, lanes, g, rows):
    j = lax.broadcasted_iota(jnp.int32, (resp, lanes) if rows else (lanes, resp), 0 if rows else 1)
    lane = lax.broadcasted_iota(jnp.int32, (resp, lanes) if rows else (lanes, resp), 1 if rows else 0)
    return jnp.where(lane == j + g * resp, 1.0, 0.0).astype(BF16)


def route_kernel(ids_ref, wts_ref, live_ref, disp_ref, notes_ref, *, experts):
    top, tok = ids_ref.shape
    slots, resp = disp_ref.shape
    planes, tail_rows, lanes = notes_ref.shape
    count = experts // planes
    live = live_ref[...] == 1
    e_row = lax.broadcasted_iota(jnp.int32, (experts, tok), 0)
    chosen = jnp.zeros((experts, tok), F32)
    weight = jnp.zeros((experts, tok), F32)
    for j in range(top):
        hit = (ids_ref[j : j + 1, :] == e_row) & live
        chosen = jnp.where(hit, 1.0, chosen)
        weight = jnp.where(hit, wts_ref[j : j + 1, :], weight)
    rows = lax.broadcasted_iota(jnp.int32, (tok, tok), 0)
    cols = lax.broadcasted_iota(jnp.int32, (tok, tok), 1)
    before = jnp.where(rows < cols, 1.0, 0.0).astype(BF16)
    place = mm(chosen.astype(BF16), before)
    place = jnp.where(chosen > 0.0, place, -1.0)
    s_row = lax.broadcasted_iota(jnp.int32, (slots, experts), 0)
    e_col = lax.broadcasted_iota(jnp.int32, (slots, experts), 1)
    spread = jnp.where(s_row // CAP == e_col, 1.0, 0.0).astype(BF16)
    slot_of = lax.broadcasted_iota(jnp.int32, (slots, tok), 0) % CAP
    hit = mm(spread, place.astype(BF16)) == slot_of.astype(F32)
    w_hi = weight.astype(BF16)
    w_lo = (weight - w_hi.astype(F32)).astype(BF16)
    picked = lax.broadcasted_iota(jnp.int32, (tok, resp), 1) + window_start(live, resp)
    pick = jnp.where(lax.broadcasted_iota(jnp.int32, (tok, resp), 0) == picked, 1.0, 0.0).astype(BF16)
    disp_ref[...] = mm(jnp.where(hit, 1.0, 0.0).astype(BF16), pick).astype(BF16)
    side, each = noted(count, resp, lanes)
    tail_row = lax.broadcasted_iota(jnp.int32, (tail_rows, lanes), 0)
    notes = [jnp.zeros((tail_rows, lanes), F32)] * planes
    for n, part in enumerate((w_hi, w_lo)):
        part = mm(part, pick).astype(BF16)
        placed = [mm(part, shift_table(resp, lanes, g, True)) for g in range(side)]
        for e in range(experts):
            at = e % count
            line = placed[at % side][e : e + 1, :]
            here = tail_row == DECAYS + n * each + at // side
            notes[e // count] = notes[e // count] + jnp.where(here, line, 0.0)
    for p in range(planes):
        notes_ref[p, :, :] = notes[p].astype(BF16)


def plan_kernel(at_ref, plane_ref, in_ref, *outs, planes, rows):
    lanes = in_ref.shape[2]
    resp = outs[0].shape[1]
    span = outs[0].shape[0] // 2
    count = span // CAP
    side, each = noted(count, resp, lanes)
    e_row = lax.broadcasted_iota(jnp.int32, (count, resp), 0)
    before = lax.broadcasted_iota(jnp.int32, (resp, resp), 0) < lax.broadcasted_iota(jnp.int32, (resp, resp), 1)
    before = jnp.where(before, 1.0, 0.0).astype(BF16)
    s_row = lax.broadcasted_iota(jnp.int32, (span, count), 0)
    e_col = lax.broadcasted_iota(jnp.int32, (span, count), 1)
    spread = jnp.where(s_row // CAP == e_col, 1.0, 0.0).astype(BF16)
    slot_of = (lax.broadcasted_iota(jnp.int32, (span, resp), 0) % CAP).astype(F32)
    for m in range(planes):
        pair = (plane_ref[0] ^ m) * count + at_ref[0]
        tail = in_ref[pair, rows:, :]
        moved = [mm(tail, shift_table(resp, lanes, g, False)) for g in range(side)]
        parts = []
        for n in range(2):
            part = jnp.zeros((count, resp), F32)
            for e in range(count):
                r = DECAYS + n * each + e // side
                part = part + jnp.where(e_row == e, moved[e % side][r : r + 1, :], 0.0)
            parts.append(part.astype(BF16))
        chosen = parts[0].astype(F32) > 0.0
        place = mm(jnp.where(chosen, 1.0, 0.0).astype(BF16), before)
        hit = mm(spread, jnp.where(chosen, place, -1.0).astype(BF16)) == slot_of
        for n in range(2):
            outs[m][n * span : (n + 1) * span, :] = jnp.where(hit, mm(spread, parts[n]), 0.0).astype(BF16)


def table_rows(tab_ref, n, at, count):
    lead = n * count * CAP
    rows = [tab_ref[pl.ds(pl.multiple_of(lead + (at ^ m) * CAP, CAP), CAP), :] for m in range(count)]
    return jnp.concatenate(rows, axis=0)


def combine_kernel(at_ref, *refs, planes, count):
    tabs, results, outs = refs[:planes], refs[planes : planes + count], refs[planes + count :]
    for m in range(planes):
        got = jnp.concatenate([results[q][m * CAP : (m + 1) * CAP, :] for q in range(count)], axis=0)
        hi = table_rows(tabs[m], 0, at_ref[0], count)
        lo = table_rows(tabs[m], 1, at_ref[0], count)
        outs[m][...] = (mm(hi, got, 0, 0) + mm(lo, got, 0, 0)).astype(outs[m].dtype)


def expert_kernel(at_ref, plane_ref, x_hbm, g0, u0, d0, g1, u1, d1, *refs, count, parts, step):
    outs, (gv, uv, dv, hid_ref, x_ref, sems) = refs[: count * parts], refs[count * parts :]
    units = g0.shape[1]
    rows, part = outs[0].shape
    cuts = range(0, units, step)
    gets = []
    for q in range(count):
        for m in range(rows // CAP):
            pair = (plane_ref[0] ^ m) * count + (at_ref[0] ^ q)
            gets.append(copy(x_hbm.at[pair], x_ref.at[pl.ds(q * rows + m * CAP, CAP)], sems, len(gets)))
    at = len(gets)
    for n, (g, u) in enumerate(((g0, u0), (g1, u1))):
        for c in cuts:
            cols = pl.ds(c, step)
            gets.append(copy(g.at[:, cols], gv.at[n, :, cols], sems, len(gets)))
            gets.append(copy(u.at[:, cols], uv.at[n, :, cols], sems, len(gets)))
    for n, d in enumerate((d0, d1)):
        gets.append(copy(d, dv.at[n], sems, len(gets)))
    for c in gets[:at]:
        c.wait()
    many = count * rows
    block = min(256, many)
    for n in range(2):
        for c in cuts:
            gets[at].wait()
            gets[at + 1].wait()
            at += 2
            for r in range(0, many, block):
                x = x_ref[r : r + block, :]
                gate = mm(x, gv[n, :, c : c + step])
                up = mm(x, uv[n, :, c : c + step])
                hid_ref[n, r : r + block, c : c + step] = (gate / (1.0 + jnp.exp(-gate)) * up).astype(BF16)
    gets[at].wait()
    gets[at + 1].wait()
    for r in range(0, many, block):
        for c in range(0, part * parts, 256):
            p0 = mm(hid_ref[0, r : r + block, :], dv[0, :, c : c + 256]).astype(BF16).astype(F32)
            p1 = mm(hid_ref[1, r : r + block, :], dv[1, :, c : c + 256]).astype(BF16).astype(F32)
            p = (p0 + p1).astype(BF16)
            for q in range(r // rows, (r + block) // rows):
                out_ref = outs[c // part * count + q]
                out_ref[:, c % part : c % part + 256] = p[q * rows - r : (q + 1) * rows - r, :]


def final_kernel(start_ref, from_ref, base_hbm, near_ref, *refs, parts, planes):
    shares, (out_hbm, res_ref, sem) = refs[: parts * planes], refs[parts * planes :]
    many, width = near_ref.shape
    resp, part = shares[0].shape
    row = lax.broadcasted_iota(jnp.int32, (many, resp), 0)
    place = lax.broadcasted_iota(jnp.int32, (many, resp), 1) + (start_ref[0] - from_ref[0])
    spread = jnp.where(row == place, 1.0, 0.0).astype(BF16)
    for c in range(parts):
        cols = slice(c * part, (c + 1) * part)
        total = shares[c * planes][...]
        for m in range(1, planes):
            total = total + shares[c * planes + m][...].astype(F32)
        hi = total.astype(BF16)
        lo = (total - hi.astype(F32)).astype(BF16)
        res_ref[:, cols] = (near_ref[:, cols] + mm(spread, hi) + mm(spread, lo)).astype(BF16)
    put = pltpu.make_async_copy(res_ref, out_hbm.at[pl.ds(pl.multiple_of(from_ref[0], 16), many)], sem)
    put.start()
    put.wait()


def shards(
    stream_in,
    query_rows,
    key_rows,
    value_rows,
    log_decay,
    attn_gain,
    ffn_gain,
    expert_ids,
    route_weights,
    response_mask,
    gate_weight,
    up_weight,
    down_weight,
):
    tok, width = stream_in.shape
    heads = log_decay.shape[0]
    hd = width // heads
    half = heads // 2
    devices = lax.axis_size(BOTH)
    pairs = devices // 2
    experts = devices // 2
    slots = experts * CAP
    top = expert_ids.shape[1]
    resp = min(tok, slots // top)
    rows = half * hd // pairs
    planes = PLANES
    count = pairs // planes
    part = width // PARTS
    me = lax.axis_index(BOTH)
    bit = (me & 1).reshape(1).astype(jnp.int32)
    sds = jax.ShapeDtypeStruct

    span = half * hd
    own, send = pl.pallas_call(
        states_kernel,
        out_shape=[sds((span + TAIL, hd), F32)] * 2,
        in_specs=[SMEM, HBM, HBM, HBM],
        out_specs=[HBM, HBM],
        scratch_shapes=[pltpu.VMEM((2, tok, span), BF16)] * 2
        + [pltpu.VMEM((heads, tok), F32)]
        + [pltpu.VMEM((span + TAIL, hd), F32)] * 2
        + [DMA((7,))],
        compiler_params=params(),
        cost_estimate=cost(2 * tok * width * hd, 3 << 20),
        name="states",
    )(bit, key_rows, value_rows, log_decay)
    recv = partner(send)
    plane = lax.shift_right_logical(me, (2 * count).bit_length() - 1).reshape(1).astype(jnp.int32)
    at = (lax.shift_right_logical(me, 1) & (count - 1)).reshape(1).astype(jnp.int32)
    routing = (expert_ids.T, route_weights.T, response_mask.reshape(1, tok))
    table = sds((2 * count * CAP, resp), BF16)
    slot_rows = sds((slots, resp), BF16)
    tail = -(-(DECAYS + 2 * noted(count, resp, hd)[1]) // 16) * 16
    note = sds((planes, tail, hd), BF16)
    disp, notes = pl.pallas_call(
        functools.partial(route_kernel, experts=experts),
        grid=(1,),
        out_shape=[slot_rows, note],
        in_specs=[full(a) for a in routing],
        out_specs=[full(slot_rows), full(note)],
        compiler_params=params(),
        cost_estimate=cost(8 * tok * tok * slots, 1 << 20),
        name="route",
    )(*routing)
    recv, gate_own, up_own, down_own, disp, notes = lax.optimization_barrier(
        (recv, gate_weight, up_weight, down_weight, disp, notes)
    )
    gate_other, up_other, down_other = partner(gate_own), partner(up_own), partner(down_own)
    payload = sds((pairs, rows + tail, hd), BF16)
    packed, earlier = pl.pallas_call(
        functools.partial(pair_kernel, half=half, rows=rows),
        grid=(1,),
        out_shape=[payload, sds(own.shape, F32)],
        in_specs=[SMEM, full(own), full(recv), full(note)],
        out_specs=[full(payload), full(own)],
        compiler_params=params(63.4),
        name="pair",
    )(bit, own, recv, notes)
    gathered = across_pairs(packed)
    col = pl.BlockSpec((tok, width // 2), lambda i: (0, i))
    wcol = pl.BlockSpec((3 * resp, width // 2), lambda i: (0, i))
    inside, lifted, nearby = pl.pallas_call(
        inside_kernel,
        grid=(2,),
        out_shape=[
            sds((tok, width), F32),
            sds((tok, width), BF16),
            sds((3 * resp, width), F32),
        ],
        in_specs=[full(routing[2]), pl.BlockSpec((half, tok), lambda i: (i, 0)), col, col, col, col],
        out_specs=[col, col, wcol],
        compiler_params=params(),
        cost_estimate=cost(4 * tok * tok * width, 6 << 20),
        name="inside",
    )(routing[2], log_decay, query_rows, key_rows, value_rows, stream_in)
    gathered, inside, lifted, nearby = lax.optimization_barrier((gathered, inside, lifted, nearby))
    tables = pl.pallas_call(
        functools.partial(plan_kernel, planes=planes, rows=rows),
        grid=(1,),
        out_shape=[table] * planes,
        in_specs=[SMEM, SMEM, full(gathered)],
        out_specs=[full(table)] * planes,
        compiler_params=params(),
        cost_estimate=cost(1 << 24, 1 << 20),
        name="plan",
    )(at, plane, gathered)
    scanned = pl.pallas_call(
        scan_kernel,
        grid=(1,),
        out_shape=sds((pairs, rows, hd), BF16),
        in_specs=[full(gathered)],
        out_specs=full(sds((pairs, rows, hd), BF16)),
        compiler_params=params(8),
        name="scan",
    )(gathered)
    pref = across_pairs(scanned).reshape(half * hd, hd)
    pref, gate_other, up_other, down_other = lax.optimization_barrier((pref, gate_other, up_other, down_other))
    keep, give = pl.pallas_call(
        functools.partial(split_kernel, half=half),
        grid=(1,),
        out_shape=[sds((half * hd, hd), BF16)] * 2,
        in_specs=[SMEM, full(pref), full(earlier)],
        out_specs=[full(pref)] * 2,
        compiler_params=params(8),
        name="split",
    )(bit, pref, earlier)
    other = partner(give)

    again = attn_gain.reshape(1, width)
    window = (nearby, keep, other, again, ffn_gain.reshape(1, width), disp)
    sent = pl.pallas_call(
        rows_kernel,
        grid=(1,),
        out_shape=sds((slots, width), BF16),
        in_specs=[SMEM] + [full(a) for a in window],
        out_specs=full(sds((slots, width), BF16)),
        scratch_shapes=[pltpu.VMEM((resp, width), F32)],
        compiler_params=params(8),
        name="rows",
    )(bit, *window)
    arrived = across_pairs(sent.reshape(pairs, CAP, width))

    gain_col = pl.BlockSpec((1, width // 2), lambda i: (0, i))
    state_all = pl.BlockSpec((half * hd, hd), lambda i: (0, 0))
    keep, mask = lax.optimization_barrier((keep, response_mask))
    start = jnp.where(mask == 1, jnp.arange(tok, dtype=jnp.int32), tok - resp).min()
    start = jnp.minimum(start, tok - resp).astype(jnp.int32).reshape(1)
    near = min(tok, resp + 16)
    first = jnp.minimum(start & -16, tok - near)
    near_col = pl.BlockSpec((near, width // 2), lambda i: (0, i))
    base, around = pl.pallas_call(
        mixed_kernel,
        grid=(2,),
        out_shape=[sds((tok, width), BF16), sds((near, width), F32)],
        in_specs=[SMEM, SMEM, col, col, col, state_all, state_all, gain_col],
        out_specs=[col, near_col],
        scratch_shapes=[pltpu.VMEM((tok, width // 2), F32)],
        compiler_params=params(60),
        cost_estimate=cost(2 * tok * width * hd, 7 << 20),
        name="mixed",
    )(bit, first, lifted, inside, stream_in, keep, other, again)
    arrived, base, around, *tables = lax.optimization_barrier((arrived, base, around, *tables))

    row_part = sds((resp, part), BF16)
    chunk = sds((planes * CAP, part), BF16)
    units = gate_weight.shape[1]
    step = min(256, units)
    many = count * chunk.shape[0]
    results = pl.pallas_call(
        functools.partial(expert_kernel, count=count, parts=PARTS, step=step),
        grid=(1,),
        out_shape=[chunk] * (count * PARTS),
        in_specs=[SMEM, SMEM] + [HBM] * 7,
        out_specs=[full(chunk)] * (count * PARTS),
        scratch_shapes=[pltpu.VMEM((2, width, units), BF16)] * 2
        + [pltpu.VMEM((2, units, width), BF16), pltpu.VMEM((2, many, units), BF16), pltpu.VMEM((many, width), BF16)]
        + [DMA((pairs + 4 * (units // step) + 2,))],
        compiler_params=params(48),
        cost_estimate=cost(12 * many * width * units, 14 << 20),
        name="expert",
    )(at, plane, arrived, gate_own, up_own, down_own, gate_other, up_other, down_other)
    backs = []
    for c in range(PARTS):
        mine = results[c * count : (c + 1) * count]
        backs.append([mine[0]] + [apart(mine[m], 2 * m) for m in range(1, count)])
    shares = []
    for c in range(PARTS):
        operands = (*tables, *backs[c])
        kinds = [sds((resp, part), F32)] + [row_part] * (planes - 1)
        sums = pl.pallas_call(
            functools.partial(combine_kernel, planes=planes, count=count),
            grid=(1,),
            out_shape=kinds,
            in_specs=[SMEM] + [full(a) for a in operands],
            out_specs=[full(a) for a in kinds],
            compiler_params=params(8),
            name="combine",
        )(at, *operands)
        shares += [sums[0]] + [apart(sums[m], 2 * count * m) for m in range(1, planes)]

    return pl.pallas_call(
        functools.partial(final_kernel, parts=PARTS, planes=planes),
        grid=(1,),
        out_shape=sds((tok, width), BF16),
        in_specs=[SMEM, SMEM, HBM, full(around)] + [full(a) for a in shares],
        out_specs=HBM,
        scratch_shapes=[pltpu.VMEM((near, width), BF16), DMA],
        input_output_aliases={2: 0},
        compiler_params=params(8),
        name="final",
    )(start, first, base, around, *shares)


def solution(mesh):
    lead = P(BOTH, None)
    placed = (
        lead,
        lead,
        lead,
        lead,
        P(None, BOTH),
        P(),
        P(),
        lead,
        lead,
        P(BOTH),
        P(None, BOTH),
        P(None, BOTH),
        lead,
    )
    return jax.shard_map(shards, mesh=mesh, in_specs=placed, out_specs=lead, check_vma=False)
```

```python
import functools

import jax
import jax.numpy as jnp
from jax import lax
from jax.experimental import pallas as pl
from jax.experimental.pallas import tpu as pltpu
from jax.sharding import PartitionSpec as P

CAP = 16
TAIL = 8
DECAYS = 3
ATTN_EPS = 1e-05
NORM_EPS = 1e-06
PLANES = 4
PARTS = 2
BOTH = ("seq", "grp")
F32 = jnp.float32
BF16 = jnp.bfloat16
SMEM = pl.BlockSpec(memory_space=pltpu.SMEM)
HBM = pl.BlockSpec(memory_space=pltpu.HBM)
DMA = pltpu.SemaphoreType.DMA


def params(mb=60):
    return pltpu.CompilerParams(vmem_limit_bytes=int(mb * 1024 * 1024))


def full(x):
    return pl.BlockSpec(x.shape, lambda i, n=len(x.shape): (0,) * n)


def cost(flops, nbytes):
    return pl.CostEstimate(flops=flops, bytes_accessed=nbytes, transcendentals=0)


def mm(a, b, ca=1, cb=0):
    return lax.dot_general(a, b, (((ca,), (cb,)), ((), ())), preferred_element_type=F32)


def lower_tri(n):
    rows = lax.broadcasted_iota(jnp.int32, (n, n), 0)
    cols = lax.broadcasted_iota(jnp.int32, (n, n), 1)
    return rows >= cols


def running_cols(dec):
    tri = lower_tri(dec.shape[1]).astype(F32)
    return lax.dot_general(
        tri, dec, (((1,), (1,)), ((), ())), precision=lax.Precision.HIGHEST, preferred_element_type=F32
    )


def running_rows(dec):
    tri = lower_tri(dec.shape[1]).astype(F32)
    return lax.dot_general(
        dec, tri, (((1,), (1,)), ((), ())), precision=lax.Precision.HIGHEST, preferred_element_type=F32
    )


def partner(x):
    count = lax.axis_size("grp")
    return lax.ppermute(x, "grp", [(i, i ^ 1) for i in range(count)])


def apart(x, distance):
    return lax.ppermute(x, BOTH, [(i, i ^ distance) for i in range(lax.axis_size(BOTH))])


def across_pairs(x):
    count = lax.axis_size(BOTH)
    groups = [list(range(k, count, 2)) for k in range(2)]
    return lax.all_to_all(x, BOTH, 0, 0, tiled=True, axis_index_groups=groups)


def copy(src, dst, sems, n):
    c = pltpu.make_async_copy(src, dst, sems.at[n])
    c.start()
    return c


def states_kernel(k_ref, key_hbm, val_hbm, dec_hbm, own_hbm, send_hbm, key_ref, val_ref, dec_ref, own_ref, send_ref, sems):
    heads, tok = dec_ref.shape
    half = heads // 2
    hd = own_ref.shape[1]
    span = half * hd
    k = k_ref[0]
    get_dec = copy(dec_hbm, dec_ref, sems, 0)
    gets = []
    for n in range(2):
        cols = pl.ds(pl.multiple_of((k ^ 1 ^ n) * span, span), span)
        gets.append(copy(key_hbm.at[:, cols], key_ref.at[n], sems, 1 + 2 * n))
        gets.append(copy(val_hbm.at[:, cols], val_ref.at[n], sems, 2 + 2 * n))
    get_dec.wait()
    mine = dec_ref[pl.ds(pl.multiple_of(k * half, half), half), :]
    theirs = dec_ref[pl.ds(pl.multiple_of((1 - k) * half, half), half), :]
    run = running_cols(jnp.concatenate([mine, theirs], axis=0))
    total = run[tok - 1 : tok, :]
    fac = jnp.exp(total - run)
    tail = jnp.broadcast_to(jnp.pad(total, ((0, 0), (0, hd - heads))), (TAIL, hd))
    puts = []
    for n, dst, out, first in ((0, send_ref, send_hbm, half), (1, own_ref, own_hbm, 0)):
        gets[2 * n].wait()
        gets[2 * n + 1].wait()
        for j in range(half):
            cols = slice(j * hd, (j + 1) * hd)
            scaled = (key_ref[n, :, cols].astype(F32) * fac[:, first + j : first + j + 1]).astype(BF16)
            dst[cols, :] = mm(val_ref[n, :, cols], scaled, 0, 0)
        dst[span:, :] = tail
        puts.append(copy(dst, out, sems, 5 + n))
    for c in puts:
        c.wait()


def pair_kernel(k_ref, own_ref, recv_ref, notes_ref, out_ref, first_ref, *, half, rows):
    hd = own_ref.shape[1]
    first = k_ref[0] == 0
    base = half * hd
    mine = own_ref[base : base + 1, :]
    theirs = recv_ref[base : base + 1, :]
    pieces = out_ref.shape[0]
    planes, tail_rows = notes_ref.shape[:2]
    tail_row = lax.broadcasted_iota(jnp.int32, (tail_rows, hd), 0)
    for p in range(pieces):
        j = p * rows // hd
        mt = mine[:, j : j + 1]
        pt = theirs[:, half + j : half + j + 1]
        one = jnp.ones_like(mt)
        a = jnp.where(first, jnp.exp(pt), one)
        b = jnp.where(first, one, jnp.exp(mt))
        lo = p * rows
        chip = own_ref[lo : lo + rows, :] * a + recv_ref[lo : lo + rows, :] * b
        out_ref[p, 0:rows, :] = chip.astype(BF16)
        d = jnp.broadcast_to(jnp.exp(mt + pt), (tail_rows, hd))
        notes = notes_ref[p * planes // pieces].astype(F32)
        d0 = d.astype(BF16).astype(F32)
        d1 = (d - d0).astype(BF16).astype(F32)
        d2 = d - d0 - d1
        first_ref[lo : lo + rows, :] = jnp.where(first, own_ref[lo : lo + rows, :], recv_ref[lo : lo + rows, :])
        tail = jnp.where(tail_row == 0, d0, jnp.where(tail_row == 1, d1, jnp.where(tail_row == 2, d2, notes)))
        out_ref[p, rows:, :] = tail.astype(BF16)
    rolled = pltpu.roll(theirs, hd - half, 1)
    first_ref[base:, :] = jnp.broadcast_to(jnp.where(first, mine, rolled), (TAIL, hd))


def scan_kernel(in_ref, out_ref):
    count, rows, hd = out_ref.shape
    state = jnp.zeros((rows, hd), F32)
    for c in range(count):
        out_ref[c, :, :] = state.astype(BF16)
        tail = in_ref[c, rows:, :].astype(F32)
        d = tail[0:1, :] + tail[1:2, :] + tail[2:3, :]
        state = state * d + in_ref[c, 0:rows, :].astype(F32)


def split_kernel(k_ref, pref_ref, first_ref, keep_ref, give_ref, *, half):
    hd = first_ref.shape[1]
    even = k_ref[0] == 0
    logs = first_ref[half * hd : half * hd + 1, :]
    for j in range(half):
        sl = slice(j * hd, (j + 1) * hd)
        before = pref_ref[sl, :].astype(F32)
        after = before * jnp.exp(logs[:, j : j + 1]) + first_ref[sl, :]
        keep_ref[sl, :] = jnp.where(even, before, after).astype(BF16)
        give_ref[sl, :] = jnp.where(even, after, before).astype(BF16)


def window_start(live, resp):
    tok = live.shape[1]
    token = lax.broadcasted_iota(jnp.int32, (1, tok), 1)
    return jnp.min(jnp.where(live, token, tok - resp), axis=1, keepdims=True).clip(0, tok - resp)


def inside_kernel(live_ref, dec_ref, q_ref, key_ref, val_ref, stream_ref, inside_ref, lifted_ref, near_ref):
    heads, tok = dec_ref.shape
    hd = q_ref.shape[1] // heads
    dec = dec_ref[...]
    run_c = running_cols(dec)
    run_r = running_rows(dec)
    lift = jnp.exp(run_c)
    cut = tok // 2
    tri = lower_tri(cut)
    resp = near_ref.shape[0] // 3
    picked = lax.broadcasted_iota(jnp.int32, (resp, tok), 0) + window_start(live_ref[...] == 1, resp)
    pick = jnp.where(lax.broadcasted_iota(jnp.int32, (resp, tok), 1) == picked, 1.0, 0.0).astype(BF16)
    for h in range(heads):
        cols = slice(h * hd, (h + 1) * hd)
        q = q_ref[:, cols]
        kk = key_ref[:, cols]
        v = val_ref[:, cols]
        lifted = (q.astype(F32) * lift[:, h : h + 1]).astype(BF16)
        lifted_ref[:, cols] = lifted
        rc = run_c[:, h : h + 1]
        rr = run_r[h : h + 1, :]
        f_aa = jnp.where(tri, jnp.exp(rc[:cut] - rr[:, :cut]), 0.0)
        f_bb = jnp.where(tri, jnp.exp(rc[cut:] - rr[:, cut:]), 0.0)
        f_ba = jnp.exp(rc[cut:] - rr[:, :cut])
        w_aa = (mm(q[:cut], kk[:cut], 1, 1) * f_aa).astype(BF16)
        s_b = mm(q[cut:], kk, 1, 1)
        w_b = (s_b * jnp.concatenate([f_ba, f_bb], axis=1)).astype(BF16)
        inside_ref[:cut, cols] = mm(w_aa, v[:cut])
        inside_ref[cut:, cols] = mm(w_b, v)
    near_ref[resp : 2 * resp, :] = mm(pick, lifted_ref[...])
    near_ref[2 * resp :, :] = mm(pick, stream_ref[...])
    rest = inside_ref[...]
    high = rest.astype(BF16)
    rest = rest - high.astype(F32)
    mid = rest.astype(BF16)
    low = (rest - mid.astype(F32)).astype(BF16)
    near_ref[:resp, :] = mm(pick, high) + mm(pick, mid) + mm(pick, low)


def head_norm(att):
    return att * lax.rsqrt(jnp.mean(att * att, axis=-1, keepdims=True) + ATTN_EPS)


def rows_kernel(k_ref, near_ref, keep_ref, other_ref, again_ref, fgain_ref, disp_ref, sent_ref, mixed_ref):
    hd = keep_ref.shape[1]
    half = keep_ref.shape[0] // hd
    k = k_ref[0]
    resp = near_ref.shape[0] // 3
    for r in range(2 * half):
        side = r // half
        off = pl.multiple_of((side ^ k) * (half * hd) + (r % half) * hd, hd)
        cols = pl.ds(off, hd)
        src = keep_ref if side == 0 else other_ref
        lifted = near_ref[resp : 2 * resp, cols].astype(BF16)
        att = near_ref[:resp, cols] + mm(lifted, src[(r % half) * hd : (r % half + 1) * hd, :], 1, 1)
        mixed_ref[:, cols] = near_ref[2 * resp :, cols] + head_norm(att) * again_ref[:, cols]
    mixed = mixed_ref[...]
    scale = lax.rsqrt(jnp.mean(mixed * mixed, axis=-1, keepdims=True) + NORM_EPS)
    ffn = (mixed * scale * fgain_ref[...]).astype(BF16)
    sent_ref[...] = mm(disp_ref[...], ffn).astype(BF16)


def mixed_kernel(k_ref, from_ref, lifted_ref, inside_ref, stream_ref, keep_ref, other_ref, again_ref, base_ref, near_ref, mixed_ref):
    hd = keep_ref.shape[1]
    half = keep_ref.shape[0] // hd
    mine = pl.program_id(0) == k_ref[0]
    for j in range(half):
        cols = slice(j * hd, (j + 1) * hd)
        st = jnp.where(mine, keep_ref[cols, :].astype(F32), other_ref[cols, :].astype(F32)).astype(BF16)
        att = inside_ref[:, cols] + mm(lifted_ref[:, cols], st, 1, 1)
        mixed_ref[:, cols] = stream_ref[:, cols].astype(F32) + head_norm(att) * again_ref[:, cols]
    base_ref[...] = mixed_ref[...].astype(BF16)
    near_ref[...] = mixed_ref[pl.ds(pl.multiple_of(from_ref[0], 16), near_ref.shape[0]), :]


def noted(experts, resp, lanes):
    side = max(1, lanes // resp)
    return side, -(-experts // side)


def shift_table(resp, lanes, g, rows):
    j = lax.broadcasted_iota(jnp.int32, (resp, lanes) if rows else (lanes, resp), 0 if rows else 1)
    lane = lax.broadcasted_iota(jnp.int32, (resp, lanes) if rows else (lanes, resp), 1 if rows else 0)
    return jnp.where(lane == j + g * resp, 1.0, 0.0).astype(BF16)


def route_kernel(ids_ref, wts_ref, live_ref, disp_ref, notes_ref, *, experts):
    top, tok = ids_ref.shape
    slots, resp = disp_ref.shape
    planes, tail_rows, lanes = notes_ref.shape
    count = experts // planes
    live = live_ref[...] == 1
    e_row = lax.broadcasted_iota(jnp.int32, (experts, tok), 0)
    chosen = jnp.zeros((experts, tok), F32)
    weight = jnp.zeros((experts, tok), F32)
    for j in range(top):
        hit = (ids_ref[j : j + 1, :] == e_row) & live
        chosen = jnp.where(hit, 1.0, chosen)
        weight = jnp.where(hit, wts_ref[j : j + 1, :], weight)
    rows = lax.broadcasted_iota(jnp.int32, (tok, tok), 0)
    cols = lax.broadcasted_iota(jnp.int32, (tok, tok), 1)
    before = jnp.where(rows < cols, 1.0, 0.0).astype(BF16)
    place = mm(chosen.astype(BF16), before)
    place = jnp.where(chosen > 0.0, place, -1.0)
    s_row = lax.broadcasted_iota(jnp.int32, (slots, experts), 0)
    e_col = lax.broadcasted_iota(jnp.int32, (slots, experts), 1)
    spread = jnp.where(s_row // CAP == e_col, 1.0, 0.0).astype(BF16)
    slot_of = lax.broadcasted_iota(jnp.int32, (slots, tok), 0) % CAP
    hit = mm(spread, place.astype(BF16)) == slot_of.astype(F32)
    w_hi = weight.astype(BF16)
    w_lo = (weight - w_hi.astype(F32)).astype(BF16)
    picked = lax.broadcasted_iota(jnp.int32, (tok, resp), 1) + window_start(live, resp)
    pick = jnp.where(lax.broadcasted_iota(jnp.int32, (tok, resp), 0) == picked, 1.0, 0.0).astype(BF16)
    disp_ref[...] = mm(jnp.where(hit, 1.0, 0.0).astype(BF16), pick).astype(BF16)
    side, each = noted(count, resp, lanes)
    tail_row = lax.broadcasted_iota(jnp.int32, (tail_rows, lanes), 0)
    notes = [jnp.zeros((tail_rows, lanes), F32)] * planes
    for n, part in enumerate((w_hi, w_lo)):
        part = mm(part, pick).astype(BF16)
        placed = [mm(part, shift_table(resp, lanes, g, True)) for g in range(side)]
        for e in range(experts):
            at = e % count
            line = placed[at % side][e : e + 1, :]
            here = tail_row == DECAYS + n * each + at // side
            notes[e // count] = notes[e // count] + jnp.where(here, line, 0.0)
    for p in range(planes):
        notes_ref[p, :, :] = notes[p].astype(BF16)


def plan_kernel(at_ref, plane_ref, in_ref, *outs, planes, rows):
    lanes = in_ref.shape[2]
    resp = outs[0].shape[1]
    span = outs[0].shape[0] // 2
    count = span // CAP
    side, each = noted(count, resp, lanes)
    e_row = lax.broadcasted_iota(jnp.int32, (count, resp), 0)
    before = lax.broadcasted_iota(jnp.int32, (resp, resp), 0) < lax.broadcasted_iota(jnp.int32, (resp, resp), 1)
    before = jnp.where(before, 1.0, 0.0).astype(BF16)
    s_row = lax.broadcasted_iota(jnp.int32, (span, count), 0)
    e_col = lax.broadcasted_iota(jnp.int32, (span, count), 1)
    spread = jnp.where(s_row // CAP == e_col, 1.0, 0.0).astype(BF16)
    slot_of = (lax.broadcasted_iota(jnp.int32, (span, resp), 0) % CAP).astype(F32)
    for m in range(planes):
        pair = (plane_ref[0] ^ m) * count + at_ref[0]
        tail = in_ref[pair, rows:, :]
        moved = [mm(tail, shift_table(resp, lanes, g, False)) for g in range(side)]
        parts = []
        for n in range(2):
            part = jnp.zeros((count, resp), F32)
            for e in range(count):
                r = DECAYS + n * each + e // side
                part = part + jnp.where(e_row == e, moved[e % side][r : r + 1, :], 0.0)
            parts.append(part.astype(BF16))
        chosen = parts[0].astype(F32) > 0.0
        place = mm(jnp.where(chosen, 1.0, 0.0).astype(BF16), before)
        hit = mm(spread, jnp.where(chosen, place, -1.0).astype(BF16)) == slot_of
        for n in range(2):
            outs[m][n * span : (n + 1) * span, :] = jnp.where(hit, mm(spread, parts[n]), 0.0).astype(BF16)


def table_rows(tab_ref, n, at, count):
    lead = n * count * CAP
    rows = [tab_ref[pl.ds(pl.multiple_of(lead + (at ^ m) * CAP, CAP), CAP), :] for m in range(count)]
    return jnp.concatenate(rows, axis=0)


def combine_kernel(at_ref, *refs, planes, count):
    tabs, results, outs = refs[:planes], refs[planes : planes + count], refs[planes + count :]
    for m in range(planes):
        got = jnp.concatenate([results[q][m * CAP : (m + 1) * CAP, :] for q in range(count)], axis=0)
        hi = table_rows(tabs[m], 0, at_ref[0], count)
        lo = table_rows(tabs[m], 1, at_ref[0], count)
        outs[m][...] = (mm(hi, got, 0, 0) + mm(lo, got, 0, 0)).astype(outs[m].dtype)


def expert_kernel(at_ref, plane_ref, x_hbm, g0, u0, d0, g1, u1, d1, *refs, count, step):
    outs, (hid_out, gv, uv, dv, hid_ref, x_ref, sems) = refs[:count], refs[count:]
    units = g0.shape[1]
    rows, part = outs[0].shape
    cuts = range(0, units, step)
    gets = []
    for q in range(count):
        for m in range(rows // CAP):
            pair = (plane_ref[0] ^ m) * count + (at_ref[0] ^ q)
            gets.append(copy(x_hbm.at[pair], x_ref.at[pl.ds(q * rows + m * CAP, CAP)], sems, len(gets)))
    at = len(gets)
    for n, (g, u) in enumerate(((g0, u0), (g1, u1))):
        for c in cuts:
            cols = pl.ds(c, step)
            gets.append(copy(g.at[:, cols], gv.at[n, :, cols], sems, len(gets)))
            gets.append(copy(u.at[:, cols], uv.at[n, :, cols], sems, len(gets)))
    for n, d in enumerate((d0, d1)):
        gets.append(copy(d.at[:, pl.ds(0, part)], dv.at[n], sems, len(gets)))
    for c in gets[:at]:
        c.wait()
    many = count * rows
    block = min(256, many)
    for n in range(2):
        for c in cuts:
            gets[at].wait()
            gets[at + 1].wait()
            at += 2
            for r in range(0, many, block):
                x = x_ref[r : r + block, :]
                gate = mm(x, gv[n, :, c : c + step])
                up = mm(x, uv[n, :, c : c + step])
                hid_ref[n, r : r + block, c : c + step] = (gate / (1.0 + jnp.exp(-gate)) * up).astype(BF16)
    put = copy(hid_ref, hid_out, sems, len(gets))
    gets[at].wait()
    gets[at + 1].wait()
    down(hid_ref, dv, outs, block)
    put.wait()


def down(hid_ref, down_ref, outs, block):
    rows, part = outs[0].shape
    for r in range(0, rows * len(outs), block):
        for c in range(0, part, 256):
            cols = slice(c, c + 256)
            p0 = mm(hid_ref[0, r : r + block, :], down_ref[0, :, cols]).astype(BF16).astype(F32)
            p1 = mm(hid_ref[1, r : r + block, :], down_ref[1, :, cols]).astype(BF16).astype(F32)
            p = (p0 + p1).astype(BF16)
            for q in range(r // rows, (r + block) // rows):
                outs[q][:, cols] = p[q * rows - r : (q + 1) * rows - r, :]


def down_kernel(hid_ref, d0, d1, *refs, count, first):
    outs, (dv, sems) = refs[:count], refs[count:]
    part = outs[0].shape[1]
    gets = [copy(d.at[:, pl.ds(first, part)], dv.at[n], sems, n) for n, d in enumerate((d0, d1))]
    for c in gets:
        c.wait()
    down(hid_ref, dv, outs, min(256, hid_ref.shape[1]))


def final_kernel(start_ref, from_ref, base_hbm, near_ref, *refs, parts, planes):
    shares, (out_hbm, res_ref, sem) = refs[: parts * planes], refs[parts * planes :]
    many, width = near_ref.shape
    resp, part = shares[0].shape
    row = lax.broadcasted_iota(jnp.int32, (many, resp), 0)
    place = lax.broadcasted_iota(jnp.int32, (many, resp), 1) + (start_ref[0] - from_ref[0])
    spread = jnp.where(row == place, 1.0, 0.0).astype(BF16)
    for c in range(parts):
        cols = slice(c * part, (c + 1) * part)
        total = shares[c * planes][...]
        for m in range(1, planes):
            total = total + shares[c * planes + m][...].astype(F32)
        hi = total.astype(BF16)
        lo = (total - hi.astype(F32)).astype(BF16)
        res_ref[:, cols] = (near_ref[:, cols] + mm(spread, hi) + mm(spread, lo)).astype(BF16)
    put = pltpu.make_async_copy(res_ref, out_hbm.at[pl.ds(pl.multiple_of(from_ref[0], 16), many)], sem)
    put.start()
    put.wait()


def shards(
    stream_in,
    query_rows,
    key_rows,
    value_rows,
    log_decay,
    attn_gain,
    ffn_gain,
    expert_ids,
    route_weights,
    response_mask,
    gate_weight,
    up_weight,
    down_weight,
):
    tok, width = stream_in.shape
    heads = log_decay.shape[0]
    hd = width // heads
    half = heads // 2
    devices = lax.axis_size(BOTH)
    pairs = devices // 2
    experts = devices // 2
    slots = experts * CAP
    top = expert_ids.shape[1]
    resp = min(tok, slots // top)
    rows = half * hd // pairs
    planes = PLANES
    count = pairs // planes
    part = width // PARTS
    me = lax.axis_index(BOTH)
    bit = (me & 1).reshape(1).astype(jnp.int32)
    sds = jax.ShapeDtypeStruct

    span = half * hd
    own, send = pl.pallas_call(
        states_kernel,
        out_shape=[sds((span + TAIL, hd), F32)] * 2,
        in_specs=[SMEM, HBM, HBM, HBM],
        out_specs=[HBM, HBM],
        scratch_shapes=[pltpu.VMEM((2, tok, span), BF16)] * 2
        + [pltpu.VMEM((heads, tok), F32)]
        + [pltpu.VMEM((span + TAIL, hd), F32)] * 2
        + [DMA((7,))],
        compiler_params=params(),
        cost_estimate=cost(2 * tok * width * hd, 3 << 20),
        name="states",
    )(bit, key_rows, value_rows, log_decay)
    recv = partner(send)
    plane = lax.shift_right_logical(me, (2 * count).bit_length() - 1).reshape(1).astype(jnp.int32)
    at = (lax.shift_right_logical(me, 1) & (count - 1)).reshape(1).astype(jnp.int32)
    routing = (expert_ids.T, route_weights.T, response_mask.reshape(1, tok))
    table = sds((2 * count * CAP, resp), BF16)
    slot_rows = sds((slots, resp), BF16)
    tail = -(-(DECAYS + 2 * noted(count, resp, hd)[1]) // 16) * 16
    note = sds((planes, tail, hd), BF16)
    disp, notes = pl.pallas_call(
        functools.partial(route_kernel, experts=experts),
        grid=(1,),
        out_shape=[slot_rows, note],
        in_specs=[full(a) for a in routing],
        out_specs=[full(slot_rows), full(note)],
        compiler_params=params(),
        cost_estimate=cost(8 * tok * tok * slots, 1 << 20),
        name="route",
    )(*routing)
    recv, gate_own, up_own, down_own, disp, notes = lax.optimization_barrier(
        (recv, gate_weight, up_weight, down_weight, disp, notes)
    )
    gate_other, up_other, down_other = partner(gate_own), partner(up_own), partner(down_own)
    payload = sds((pairs, rows + tail, hd), BF16)
    packed, earlier = pl.pallas_call(
        functools.partial(pair_kernel, half=half, rows=rows),
        grid=(1,),
        out_shape=[payload, sds(own.shape, F32)],
        in_specs=[SMEM, full(own), full(recv), full(note)],
        out_specs=[full(payload), full(own)],
        compiler_params=params(63.4),
        name="pair",
    )(bit, own, recv, notes)
    gathered = across_pairs(packed)
    col = pl.BlockSpec((tok, width // 2), lambda i: (0, i))
    wcol = pl.BlockSpec((3 * resp, width // 2), lambda i: (0, i))
    inside, lifted, nearby = pl.pallas_call(
        inside_kernel,
        grid=(2,),
        out_shape=[
            sds((tok, width), F32),
            sds((tok, width), BF16),
            sds((3 * resp, width), F32),
        ],
        in_specs=[full(routing[2]), pl.BlockSpec((half, tok), lambda i: (i, 0)), col, col, col, col],
        out_specs=[col, col, wcol],
        compiler_params=params(),
        cost_estimate=cost(4 * tok * tok * width, 6 << 20),
        name="inside",
    )(routing[2], log_decay, query_rows, key_rows, value_rows, stream_in)
    gathered, inside, lifted, nearby = lax.optimization_barrier((gathered, inside, lifted, nearby))
    tables = pl.pallas_call(
        functools.partial(plan_kernel, planes=planes, rows=rows),
        grid=(1,),
        out_shape=[table] * planes,
        in_specs=[SMEM, SMEM, full(gathered)],
        out_specs=[full(table)] * planes,
        compiler_params=params(),
        cost_estimate=cost(1 << 24, 1 << 20),
        name="plan",
    )(at, plane, gathered)
    scanned = pl.pallas_call(
        scan_kernel,
        grid=(1,),
        out_shape=sds((pairs, rows, hd), BF16),
        in_specs=[full(gathered)],
        out_specs=full(sds((pairs, rows, hd), BF16)),
        compiler_params=params(8),
        name="scan",
    )(gathered)
    pref = across_pairs(scanned).reshape(half * hd, hd)
    pref, gate_other, up_other, down_other = lax.optimization_barrier((pref, gate_other, up_other, down_other))
    keep, give = pl.pallas_call(
        functools.partial(split_kernel, half=half),
        grid=(1,),
        out_shape=[sds((half * hd, hd), BF16)] * 2,
        in_specs=[SMEM, full(pref), full(earlier)],
        out_specs=[full(pref)] * 2,
        compiler_params=params(8),
        name="split",
    )(bit, pref, earlier)
    other = partner(give)

    again = attn_gain.reshape(1, width)
    window = (nearby, keep, other, again, ffn_gain.reshape(1, width), disp)
    sent = pl.pallas_call(
        rows_kernel,
        grid=(1,),
        out_shape=sds((slots, width), BF16),
        in_specs=[SMEM] + [full(a) for a in window],
        out_specs=full(sds((slots, width), BF16)),
        scratch_shapes=[pltpu.VMEM((resp, width), F32)],
        compiler_params=params(8),
        name="rows",
    )(bit, *window)
    arrived = across_pairs(sent.reshape(pairs, CAP, width))

    gain_col = pl.BlockSpec((1, width // 2), lambda i: (0, i))
    state_all = pl.BlockSpec((half * hd, hd), lambda i: (0, 0))
    keep, mask = lax.optimization_barrier((keep, response_mask))
    start = jnp.where(mask == 1, jnp.arange(tok, dtype=jnp.int32), tok - resp).min()
    start = jnp.minimum(start, tok - resp).astype(jnp.int32).reshape(1)
    near = min(tok, resp + 16)
    first = jnp.minimum(start & -16, tok - near)
    near_col = pl.BlockSpec((near, width // 2), lambda i: (0, i))
    base, around = pl.pallas_call(
        mixed_kernel,
        grid=(2,),
        out_shape=[sds((tok, width), BF16), sds((near, width), F32)],
        in_specs=[SMEM, SMEM, col, col, col, state_all, state_all, gain_col],
        out_specs=[col, near_col],
        scratch_shapes=[pltpu.VMEM((tok, width // 2), F32)],
        compiler_params=params(60),
        cost_estimate=cost(2 * tok * width * hd, 7 << 20),
        name="mixed",
    )(bit, first, lifted, inside, stream_in, keep, other, again)
    arrived, base, around, *tables = lax.optimization_barrier((arrived, base, around, *tables))

    row_part = sds((resp, part), BF16)
    chunk = sds((planes * CAP, part), BF16)
    units = gate_weight.shape[1]
    step = min(256, units)
    many = count * chunk.shape[0]
    hidden = sds((2, many, units), BF16)
    *results, hid = pl.pallas_call(
        functools.partial(expert_kernel, count=count, step=step),
        grid=(1,),
        out_shape=[chunk] * count + [hidden],
        in_specs=[SMEM, SMEM] + [HBM] * 7,
        out_specs=[full(chunk)] * count + [HBM],
        scratch_shapes=[pltpu.VMEM((2, width, units), BF16)] * 2
        + [pltpu.VMEM((2, units, part), BF16), pltpu.VMEM(hidden.shape, BF16), pltpu.VMEM((many, width), BF16)]
        + [DMA((pairs + 4 * (units // step) + 3,))],
        compiler_params=params(48),
        cost_estimate=cost(10 * many * width * units, 12 << 20),
        name="expert",
    )(at, plane, arrived, gate_own, up_own, down_own, gate_other, up_other, down_other)
    shares = []
    for c in range(PARTS):
        if c:
            results = pl.pallas_call(
                functools.partial(down_kernel, count=count, first=c * part),
                grid=(1,),
                out_shape=[chunk] * count,
                in_specs=[full(hid), HBM, HBM],
                out_specs=[full(chunk)] * count,
                scratch_shapes=[pltpu.VMEM((2, units, part), BF16), DMA((2,))],
                compiler_params=params(48),
                cost_estimate=cost(2 * many * width * units, 2 << 20),
                name="down",
            )(hid, down_own, down_other)
        back = [results[0]] + [apart(results[m], 2 * m) for m in range(1, count)]
        operands = (*tables, *back)
        kinds = [sds((resp, part), F32)] + [row_part] * (planes - 1)
        sums = pl.pallas_call(
            functools.partial(combine_kernel, planes=planes, count=count),
            grid=(1,),
            out_shape=kinds,
            in_specs=[SMEM] + [full(a) for a in operands],
            out_specs=[full(a) for a in kinds],
            compiler_params=params(8),
            name="combine",
        )(at, *operands)
        shares += [sums[0]] + [apart(sums[m], 2 * count * m) for m in range(1, planes)]

    return pl.pallas_call(
        functools.partial(final_kernel, parts=PARTS, planes=planes),
        grid=(1,),
        out_shape=sds((tok, width), BF16),
        in_specs=[SMEM, SMEM, HBM, full(around)] + [full(a) for a in shares],
        out_specs=HBM,
        scratch_shapes=[pltpu.VMEM((near, width), BF16), DMA],
        input_output_aliases={2: 0},
        compiler_params=params(8),
        name="final",
    )(start, first, base, around, *shares)


def solution(mesh):
    lead = P(BOTH, None)
    placed = (
        lead,
        lead,
        lead,
        lead,
        P(None, BOTH),
        P(),
        P(),
        lead,
        lead,
        P(BOTH),
        P(None, BOTH),
        P(None, BOTH),
        lead,
    )
    return jax.shard_map(shards, mesh=mesh, in_specs=placed, out_specs=lead, check_vma=False)
```

```python
import functools

import jax
import jax.numpy as jnp
from jax import lax
from jax.experimental import pallas as pl
from jax.experimental.pallas import tpu as pltpu
from jax.sharding import PartitionSpec as P

CAP = 16
TAIL = 8
DECAYS = 3
BANDS = 4
ATTN_EPS = 1e-05
NORM_EPS = 1e-06
PLANES = 4
PARTS = 2
BOTH = ("seq", "grp")
F32 = jnp.float32
BF16 = jnp.bfloat16
SMEM = pl.BlockSpec(memory_space=pltpu.SMEM)
HBM = pl.BlockSpec(memory_space=pltpu.HBM)
DMA = pltpu.SemaphoreType.DMA


def params(mb=60):
    return pltpu.CompilerParams(vmem_limit_bytes=int(mb * 1024 * 1024))


def full(x):
    return pl.BlockSpec(x.shape, lambda i, n=len(x.shape): (0,) * n)


def cost(flops, nbytes):
    return pl.CostEstimate(flops=flops, bytes_accessed=nbytes, transcendentals=0)


def mm(a, b, ca=1, cb=0):
    return lax.dot_general(a, b, (((ca,), (cb,)), ((), ())), preferred_element_type=F32)


def lower_tri(n):
    rows = lax.broadcasted_iota(jnp.int32, (n, n), 0)
    cols = lax.broadcasted_iota(jnp.int32, (n, n), 1)
    return rows >= cols


def running_cols(dec):
    tri = lower_tri(dec.shape[1]).astype(F32)
    return lax.dot_general(
        tri, dec, (((1,), (1,)), ((), ())), precision=lax.Precision.HIGHEST, preferred_element_type=F32
    )


def running_rows(dec):
    tri = lower_tri(dec.shape[1]).astype(F32)
    return lax.dot_general(
        dec, tri, (((1,), (1,)), ((), ())), precision=lax.Precision.HIGHEST, preferred_element_type=F32
    )


def partner(x):
    count = lax.axis_size("grp")
    return lax.ppermute(x, "grp", [(i, i ^ 1) for i in range(count)])


def apart(x, distance):
    return lax.ppermute(x, BOTH, [(i, i ^ distance) for i in range(lax.axis_size(BOTH))])


def across_pairs(x):
    count = lax.axis_size(BOTH)
    groups = [list(range(k, count, 2)) for k in range(2)]
    return lax.all_to_all(x, BOTH, 0, 0, tiled=True, axis_index_groups=groups)


def copy(src, dst, sems, n):
    c = pltpu.make_async_copy(src, dst, sems.at[n])
    c.start()
    return c


def states_kernel(k_ref, key_hbm, val_hbm, dec_hbm, own_hbm, send_hbm, key_ref, val_ref, dec_ref, own_ref, send_ref, sems):
    heads, tok = dec_ref.shape
    half = heads // 2
    hd = own_ref.shape[1]
    span = half * hd
    k = k_ref[0]
    get_dec = copy(dec_hbm, dec_ref, sems, 0)
    gets = []
    for n in range(2):
        cols = pl.ds(pl.multiple_of((k ^ 1 ^ n) * span, span), span)
        gets.append(copy(key_hbm.at[:, cols], key_ref.at[n], sems, 1 + 2 * n))
        gets.append(copy(val_hbm.at[:, cols], val_ref.at[n], sems, 2 + 2 * n))
    get_dec.wait()
    mine = dec_ref[pl.ds(pl.multiple_of(k * half, half), half), :]
    theirs = dec_ref[pl.ds(pl.multiple_of((1 - k) * half, half), half), :]
    run = running_cols(jnp.concatenate([mine, theirs], axis=0))
    total = run[tok - 1 : tok, :]
    fac = jnp.exp(total - run)
    tail = jnp.broadcast_to(jnp.pad(total, ((0, 0), (0, hd - heads))), (TAIL, hd))
    puts = []
    for n, dst, out, first in ((0, send_ref, send_hbm, half), (1, own_ref, own_hbm, 0)):
        gets[2 * n].wait()
        gets[2 * n + 1].wait()
        for j in range(half):
            cols = slice(j * hd, (j + 1) * hd)
            scaled = (key_ref[n, :, cols].astype(F32) * fac[:, first + j : first + j + 1]).astype(BF16)
            dst[cols, :] = mm(val_ref[n, :, cols], scaled, 0, 0)
        dst[span:, :] = tail
        puts.append(copy(dst, out, sems, 5 + n))
    for c in puts:
        c.wait()


def pair_kernel(k_ref, own_ref, recv_ref, notes_ref, out_ref, first_ref, *, half, rows):
    hd = own_ref.shape[1]
    first = k_ref[0] == 0
    base = half * hd
    mine = own_ref[base : base + 1, :]
    theirs = recv_ref[base : base + 1, :]
    pieces = out_ref.shape[0]
    planes, tail_rows = notes_ref.shape[:2]
    tail_row = lax.broadcasted_iota(jnp.int32, (tail_rows, hd), 0)
    for p in range(pieces):
        j = p * rows // hd
        mt = mine[:, j : j + 1]
        pt = theirs[:, half + j : half + j + 1]
        one = jnp.ones_like(mt)
        a = jnp.where(first, jnp.exp(pt), one)
        b = jnp.where(first, one, jnp.exp(mt))
        lo = p * rows
        chip = own_ref[lo : lo + rows, :] * a + recv_ref[lo : lo + rows, :] * b
        out_ref[p, 0:rows, :] = chip.astype(BF16)
        d = jnp.broadcast_to(jnp.exp(mt + pt), (tail_rows, hd))
        notes = notes_ref[p * planes // pieces].astype(F32)
        d0 = d.astype(BF16).astype(F32)
        d1 = (d - d0).astype(BF16).astype(F32)
        d2 = d - d0 - d1
        first_ref[lo : lo + rows, :] = jnp.where(first, own_ref[lo : lo + rows, :], recv_ref[lo : lo + rows, :])
        tail = jnp.where(tail_row == 0, d0, jnp.where(tail_row == 1, d1, jnp.where(tail_row == 2, d2, notes)))
        out_ref[p, rows:, :] = tail.astype(BF16)
    rolled = pltpu.roll(theirs, hd - half, 1)
    first_ref[base:, :] = jnp.broadcast_to(jnp.where(first, mine, rolled), (TAIL, hd))


def scan_kernel(in_ref, out_ref):
    count, rows, hd = out_ref.shape
    state = jnp.zeros((rows, hd), F32)
    for c in range(count):
        out_ref[c, :, :] = state.astype(BF16)
        tail = in_ref[c, rows:, :].astype(F32)
        d = tail[0:1, :] + tail[1:2, :] + tail[2:3, :]
        state = state * d + in_ref[c, 0:rows, :].astype(F32)


def split_kernel(k_ref, pref_ref, first_ref, keep_ref, give_ref, *, half):
    hd = first_ref.shape[1]
    even = k_ref[0] == 0
    logs = first_ref[half * hd : half * hd + 1, :]
    for j in range(half):
        sl = slice(j * hd, (j + 1) * hd)
        before = pref_ref[sl, :].astype(F32)
        after = before * jnp.exp(logs[:, j : j + 1]) + first_ref[sl, :]
        keep_ref[sl, :] = jnp.where(even, before, after).astype(BF16)
        give_ref[sl, :] = jnp.where(even, after, before).astype(BF16)


def window_start(live, resp):
    tok = live.shape[1]
    token = lax.broadcasted_iota(jnp.int32, (1, tok), 1)
    return jnp.min(jnp.where(live, token, tok - resp), axis=1, keepdims=True).clip(0, tok - resp)


def inside_kernel(live_ref, dec_ref, q_ref, key_ref, val_ref, stream_ref, inside_ref, lifted_ref, near_ref):
    heads, tok = dec_ref.shape
    hd = q_ref.shape[1] // heads
    dec = dec_ref[...]
    run_c = running_cols(dec)
    run_r = running_rows(dec)
    lift = jnp.exp(run_c)
    cut = tok // 2
    tri = lower_tri(cut)
    resp = near_ref.shape[0] // 3
    picked = lax.broadcasted_iota(jnp.int32, (resp, tok), 0) + window_start(live_ref[...] == 1, resp)
    pick = jnp.where(lax.broadcasted_iota(jnp.int32, (resp, tok), 1) == picked, 1.0, 0.0).astype(BF16)
    for h in range(heads):
        cols = slice(h * hd, (h + 1) * hd)
        q = q_ref[:, cols]
        kk = key_ref[:, cols]
        v = val_ref[:, cols]
        lifted = (q.astype(F32) * lift[:, h : h + 1]).astype(BF16)
        lifted_ref[:, cols] = lifted
        rc = run_c[:, h : h + 1]
        rr = run_r[h : h + 1, :]
        f_aa = jnp.where(tri, jnp.exp(rc[:cut] - rr[:, :cut]), 0.0)
        f_bb = jnp.where(tri, jnp.exp(rc[cut:] - rr[:, cut:]), 0.0)
        f_ba = jnp.exp(rc[cut:] - rr[:, :cut])
        w_aa = (mm(q[:cut], kk[:cut], 1, 1) * f_aa).astype(BF16)
        s_b = mm(q[cut:], kk, 1, 1)
        w_b = (s_b * jnp.concatenate([f_ba, f_bb], axis=1)).astype(BF16)
        inside_ref[:cut, cols] = mm(w_aa, v[:cut])
        inside_ref[cut:, cols] = mm(w_b, v)
    near_ref[resp : 2 * resp, :] = mm(pick, lifted_ref[...])
    near_ref[2 * resp :, :] = mm(pick, stream_ref[...])
    rest = inside_ref[...]
    high = rest.astype(BF16)
    rest = rest - high.astype(F32)
    mid = rest.astype(BF16)
    low = (rest - mid.astype(F32)).astype(BF16)
    near_ref[:resp, :] = mm(pick, high) + mm(pick, mid) + mm(pick, low)


def head_norm(att):
    return att * lax.rsqrt(jnp.mean(att * att, axis=-1, keepdims=True) + ATTN_EPS)


def rows_kernel(k_ref, near_ref, keep_ref, other_ref, again_ref, fgain_ref, disp_ref, sent_hbm, mixed_ref, sent_ref, sems):
    hd = keep_ref.shape[1]
    half = keep_ref.shape[0] // hd
    k = k_ref[0]
    resp = near_ref.shape[0] // 3
    for r in range(2 * half):
        side = r // half
        off = pl.multiple_of((side ^ k) * (half * hd) + (r % half) * hd, hd)
        cols = pl.ds(off, hd)
        src = keep_ref if side == 0 else other_ref
        lifted = near_ref[resp : 2 * resp, cols].astype(BF16)
        att = near_ref[:resp, cols] + mm(lifted, src[(r % half) * hd : (r % half + 1) * hd, :], 1, 1)
        mixed_ref[:, cols] = near_ref[2 * resp :, cols] + head_norm(att) * again_ref[:, cols]
    mixed = mixed_ref[...]
    scale = lax.rsqrt(jnp.mean(mixed * mixed, axis=-1, keepdims=True) + NORM_EPS)
    ffn = (mixed * scale * fgain_ref[...]).astype(BF16)
    puts = []
    band = sent_ref.shape[0] // BANDS
    for b in range(BANDS):
        here = pl.ds(b * band, band)
        sent_ref[here, :] = mm(disp_ref[here, :], ffn).astype(BF16)
        puts.append(copy(sent_ref.at[here], sent_hbm.at[here], sems, b))
    for c in puts:
        c.wait()


def mixed_kernel(k_ref, from_ref, lifted_ref, inside_ref, stream_ref, keep_ref, other_ref, again_ref, base_ref, near_ref, mixed_ref):
    hd = keep_ref.shape[1]
    half = keep_ref.shape[0] // hd
    mine = pl.program_id(0) == k_ref[0]
    for j in range(half):
        cols = slice(j * hd, (j + 1) * hd)
        st = jnp.where(mine, keep_ref[cols, :].astype(F32), other_ref[cols, :].astype(F32)).astype(BF16)
        att = inside_ref[:, cols] + mm(lifted_ref[:, cols], st, 1, 1)
        mixed_ref[:, cols] = stream_ref[:, cols].astype(F32) + head_norm(att) * again_ref[:, cols]
    base_ref[...] = mixed_ref[...].astype(BF16)
    near_ref[...] = mixed_ref[pl.ds(pl.multiple_of(from_ref[0], 16), near_ref.shape[0]), :]


def noted(experts, resp, lanes):
    side = max(1, lanes // resp)
    return side, -(-experts // side)


def shift_table(resp, lanes, g, rows):
    j = lax.broadcasted_iota(jnp.int32, (resp, lanes) if rows else (lanes, resp), 0 if rows else 1)
    lane = lax.broadcasted_iota(jnp.int32, (resp, lanes) if rows else (lanes, resp), 1 if rows else 0)
    return jnp.where(lane == j + g * resp, 1.0, 0.0).astype(BF16)


def route_kernel(ids_ref, wts_ref, live_ref, disp_ref, notes_ref, *, experts):
    top, tok = ids_ref.shape
    slots, resp = disp_ref.shape
    planes, tail_rows, lanes = notes_ref.shape
    count = experts // planes
    live = live_ref[...] == 1
    e_row = lax.broadcasted_iota(jnp.int32, (experts, tok), 0)
    chosen = jnp.zeros((experts, tok), F32)
    weight = jnp.zeros((experts, tok), F32)
    for j in range(top):
        hit = (ids_ref[j : j + 1, :] == e_row) & live
        chosen = jnp.where(hit, 1.0, chosen)
        weight = jnp.where(hit, wts_ref[j : j + 1, :], weight)
    rows = lax.broadcasted_iota(jnp.int32, (tok, tok), 0)
    cols = lax.broadcasted_iota(jnp.int32, (tok, tok), 1)
    before = jnp.where(rows < cols, 1.0, 0.0).astype(BF16)
    place = mm(chosen.astype(BF16), before)
    place = jnp.where(chosen > 0.0, place, -1.0)
    s_row = lax.broadcasted_iota(jnp.int32, (slots, experts), 0)
    e_col = lax.broadcasted_iota(jnp.int32, (slots, experts), 1)
    spread = jnp.where(s_row // CAP == e_col, 1.0, 0.0).astype(BF16)
    slot_of = lax.broadcasted_iota(jnp.int32, (slots, tok), 0) % CAP
    hit = mm(spread, place.astype(BF16)) == slot_of.astype(F32)
    w_hi = weight.astype(BF16)
    w_lo = (weight - w_hi.astype(F32)).astype(BF16)
    picked = lax.broadcasted_iota(jnp.int32, (tok, resp), 1) + window_start(live, resp)
    pick = jnp.where(lax.broadcasted_iota(jnp.int32, (tok, resp), 0) == picked, 1.0, 0.0).astype(BF16)
    disp_ref[...] = mm(jnp.where(hit, 1.0, 0.0).astype(BF16), pick).astype(BF16)
    side, each = noted(count, resp, lanes)
    tail_row = lax.broadcasted_iota(jnp.int32, (tail_rows, lanes), 0)
    notes = [jnp.zeros((tail_rows, lanes), F32)] * planes
    for n, part in enumerate((w_hi, w_lo)):
        part = mm(part, pick).astype(BF16)
        placed = [mm(part, shift_table(resp, lanes, g, True)) for g in range(side)]
        for e in range(experts):
            at = e % count
            line = placed[at % side][e : e + 1, :]
            here = tail_row == DECAYS + n * each + at // side
            notes[e // count] = notes[e // count] + jnp.where(here, line, 0.0)
    for p in range(planes):
        notes_ref[p, :, :] = notes[p].astype(BF16)


def plan_kernel(at_ref, plane_ref, in_ref, *outs, planes, rows):
    lanes = in_ref.shape[2]
    resp = outs[0].shape[1]
    span = outs[0].shape[0] // 2
    count = span // CAP
    side, each = noted(count, resp, lanes)
    e_row = lax.broadcasted_iota(jnp.int32, (count, resp), 0)
    before = lax.broadcasted_iota(jnp.int32, (resp, resp), 0) < lax.broadcasted_iota(jnp.int32, (resp, resp), 1)
    before = jnp.where(before, 1.0, 0.0).astype(BF16)
    s_row = lax.broadcasted_iota(jnp.int32, (span, count), 0)
    e_col = lax.broadcasted_iota(jnp.int32, (span, count), 1)
    spread = jnp.where(s_row // CAP == e_col, 1.0, 0.0).astype(BF16)
    slot_of = (lax.broadcasted_iota(jnp.int32, (span, resp), 0) % CAP).astype(F32)
    for m in range(planes):
        pair = (plane_ref[0] ^ m) * count + at_ref[0]
        tail = in_ref[pair, rows:, :]
        moved = [mm(tail, shift_table(resp, lanes, g, False)) for g in range(side)]
        parts = []
        for n in range(2):
            part = jnp.zeros((count, resp), F32)
            for e in range(count):
                r = DECAYS + n * each + e // side
                part = part + jnp.where(e_row == e, moved[e % side][r : r + 1, :], 0.0)
            parts.append(part.astype(BF16))
        chosen = parts[0].astype(F32) > 0.0
        place = mm(jnp.where(chosen, 1.0, 0.0).astype(BF16), before)
        hit = mm(spread, jnp.where(chosen, place, -1.0).astype(BF16)) == slot_of
        for n in range(2):
            outs[m][n * span : (n + 1) * span, :] = jnp.where(hit, mm(spread, parts[n]), 0.0).astype(BF16)


def table_rows(tab_ref, n, at, count):
    lead = n * count * CAP
    rows = [tab_ref[pl.ds(pl.multiple_of(lead + (at ^ m) * CAP, CAP), CAP), :] for m in range(count)]
    return jnp.concatenate(rows, axis=0)


def combine_kernel(at_ref, *refs, planes, count):
    tabs, results, outs = refs[:planes], refs[planes : planes + count], refs[planes + count :]
    for m in range(planes):
        got = jnp.concatenate([results[q][m * CAP : (m + 1) * CAP, :] for q in range(count)], axis=0)
        hi = table_rows(tabs[m], 0, at_ref[0], count)
        lo = table_rows(tabs[m], 1, at_ref[0], count)
        outs[m][...] = (mm(hi, got, 0, 0) + mm(lo, got, 0, 0)).astype(outs[m].dtype)


def expert_kernel(at_ref, plane_ref, x_hbm, g0, u0, d0, g1, u1, d1, *refs, count, step):
    outs, (hid_out, gv, uv, dv, hid_ref, x_ref, sems) = refs[:count], refs[count:]
    units = g0.shape[1]
    rows, part = outs[0].shape
    cuts = range(0, units, step)
    gets = []
    for q in range(count):
        for m in range(rows // CAP):
            pair = (plane_ref[0] ^ m) * count + (at_ref[0] ^ q)
            gets.append(copy(x_hbm.at[pair], x_ref.at[pl.ds(q * rows + m * CAP, CAP)], sems, len(gets)))
    at = len(gets)
    for n, (g, u) in enumerate(((g0, u0), (g1, u1))):
        for c in cuts:
            cols = pl.ds(c, step)
            gets.append(copy(g.at[:, cols], gv.at[n, :, cols], sems, len(gets)))
            gets.append(copy(u.at[:, cols], uv.at[n, :, cols], sems, len(gets)))
    for n, d in enumerate((d0, d1)):
        gets.append(copy(d.at[:, pl.ds(0, part)], dv.at[n], sems, len(gets)))
    for c in gets[:at]:
        c.wait()
    many = count * rows
    block = min(256, many)
    for n in range(2):
        for c in cuts:
            gets[at].wait()
            gets[at + 1].wait()
            at += 2
            for r in range(0, many, block):
                x = x_ref[r : r + block, :]
                gate = mm(x, gv[n, :, c : c + step])
                up = mm(x, uv[n, :, c : c + step])
                hid_ref[n, r : r + block, c : c + step] = (gate / (1.0 + jnp.exp(-gate)) * up).astype(BF16)
    put = copy(hid_ref, hid_out, sems, len(gets))
    gets[at].wait()
    gets[at + 1].wait()
    down(hid_ref, dv, outs, block)
    put.wait()


def down(hid_ref, down_ref, outs, block):
    rows, part = outs[0].shape
    for r in range(0, rows * len(outs), block):
        for c in range(0, part, 256):
            cols = slice(c, c + 256)
            p0 = mm(hid_ref[0, r : r + block, :], down_ref[0, :, cols]).astype(BF16).astype(F32)
            p1 = mm(hid_ref[1, r : r + block, :], down_ref[1, :, cols]).astype(BF16).astype(F32)
            p = (p0 + p1).astype(BF16)
            for q in range(r // rows, (r + block) // rows):
                outs[q][:, cols] = p[q * rows - r : (q + 1) * rows - r, :]


def down_kernel(hid_ref, d0, d1, *refs, count, first):
    outs, (dv, sems) = refs[:count], refs[count:]
    part = outs[0].shape[1]
    gets = [copy(d.at[:, pl.ds(first, part)], dv.at[n], sems, n) for n, d in enumerate((d0, d1))]
    for c in gets:
        c.wait()
    down(hid_ref, dv, outs, min(256, hid_ref.shape[1]))


def final_kernel(start_ref, from_ref, base_hbm, near_ref, *refs, parts, planes):
    shares, (out_hbm, res_ref, sem) = refs[: parts * planes], refs[parts * planes :]
    many, width = near_ref.shape
    resp, part = shares[0].shape
    row = lax.broadcasted_iota(jnp.int32, (many, resp), 0)
    place = lax.broadcasted_iota(jnp.int32, (many, resp), 1) + (start_ref[0] - from_ref[0])
    spread = jnp.where(row == place, 1.0, 0.0).astype(BF16)
    for c in range(parts):
        cols = slice(c * part, (c + 1) * part)
        total = shares[c * planes][...]
        for m in range(1, planes):
            total = total + shares[c * planes + m][...].astype(F32)
        hi = total.astype(BF16)
        lo = (total - hi.astype(F32)).astype(BF16)
        res_ref[:, cols] = (near_ref[:, cols] + mm(spread, hi) + mm(spread, lo)).astype(BF16)
    put = pltpu.make_async_copy(res_ref, out_hbm.at[pl.ds(pl.multiple_of(from_ref[0], 16), many)], sem)
    put.start()
    put.wait()


def shards(
    stream_in,
    query_rows,
    key_rows,
    value_rows,
    log_decay,
    attn_gain,
    ffn_gain,
    expert_ids,
    route_weights,
    response_mask,
    gate_weight,
    up_weight,
    down_weight,
):
    tok, width = stream_in.shape
    heads = log_decay.shape[0]
    hd = width // heads
    half = heads // 2
    devices = lax.axis_size(BOTH)
    pairs = devices // 2
    experts = devices // 2
    slots = experts * CAP
    top = expert_ids.shape[1]
    resp = min(tok, slots // top)
    rows = half * hd // pairs
    planes = PLANES
    count = pairs // planes
    part = width // PARTS
    me = lax.axis_index(BOTH)
    bit = (me & 1).reshape(1).astype(jnp.int32)
    sds = jax.ShapeDtypeStruct

    span = half * hd
    own, send = pl.pallas_call(
        states_kernel,
        out_shape=[sds((span + TAIL, hd), F32)] * 2,
        in_specs=[SMEM, HBM, HBM, HBM],
        out_specs=[HBM, HBM],
        scratch_shapes=[pltpu.VMEM((2, tok, span), BF16)] * 2
        + [pltpu.VMEM((heads, tok), F32)]
        + [pltpu.VMEM((span + TAIL, hd), F32)] * 2
        + [DMA((7,))],
        compiler_params=params(),
        cost_estimate=cost(2 * tok * width * hd, 3 << 20),
        name="states",
    )(bit, key_rows, value_rows, log_decay)
    recv = partner(send)
    plane = lax.shift_right_logical(me, (2 * count).bit_length() - 1).reshape(1).astype(jnp.int32)
    at = (lax.shift_right_logical(me, 1) & (count - 1)).reshape(1).astype(jnp.int32)
    routing = (expert_ids.T, route_weights.T, response_mask.reshape(1, tok))
    table = sds((2 * count * CAP, resp), BF16)
    slot_rows = sds((slots, resp), BF16)
    tail = -(-(DECAYS + 2 * noted(count, resp, hd)[1]) // 16) * 16
    note = sds((planes, tail, hd), BF16)
    disp, notes = pl.pallas_call(
        functools.partial(route_kernel, experts=experts),
        grid=(1,),
        out_shape=[slot_rows, note],
        in_specs=[full(a) for a in routing],
        out_specs=[full(slot_rows), full(note)],
        compiler_params=params(),
        cost_estimate=cost(8 * tok * tok * slots, 1 << 20),
        name="route",
    )(*routing)
    recv, gate_own, up_own, down_own, disp, notes = lax.optimization_barrier(
        (recv, gate_weight, up_weight, down_weight, disp, notes)
    )
    gate_other, up_other, down_other = partner(gate_own), partner(up_own), partner(down_own)
    payload = sds((pairs, rows + tail, hd), BF16)
    packed, earlier = pl.pallas_call(
        functools.partial(pair_kernel, half=half, rows=rows),
        grid=(1,),
        out_shape=[payload, sds(own.shape, F32)],
        in_specs=[SMEM, full(own), full(recv), full(note)],
        out_specs=[full(payload), full(own)],
        compiler_params=params(63.4),
        name="pair",
    )(bit, own, recv, notes)
    gathered = across_pairs(packed)
    col = pl.BlockSpec((tok, width // 2), lambda i: (0, i))
    wcol = pl.BlockSpec((3 * resp, width // 2), lambda i: (0, i))
    inside, lifted, nearby = pl.pallas_call(
        inside_kernel,
        grid=(2,),
        out_shape=[
            sds((tok, width), F32),
            sds((tok, width), BF16),
            sds((3 * resp, width), F32),
        ],
        in_specs=[full(routing[2]), pl.BlockSpec((half, tok), lambda i: (i, 0)), col, col, col, col],
        out_specs=[col, col, wcol],
        compiler_params=params(),
        cost_estimate=cost(4 * tok * tok * width, 6 << 20),
        name="inside",
    )(routing[2], log_decay, query_rows, key_rows, value_rows, stream_in)
    gathered, inside, lifted, nearby = lax.optimization_barrier((gathered, inside, lifted, nearby))
    tables = pl.pallas_call(
        functools.partial(plan_kernel, planes=planes, rows=rows),
        grid=(1,),
        out_shape=[table] * planes,
        in_specs=[SMEM, SMEM, full(gathered)],
        out_specs=[full(table)] * planes,
        compiler_params=params(),
        cost_estimate=cost(1 << 24, 1 << 20),
        name="plan",
    )(at, plane, gathered)
    scanned = pl.pallas_call(
        scan_kernel,
        grid=(1,),
        out_shape=sds((pairs, rows, hd), BF16),
        in_specs=[full(gathered)],
        out_specs=full(sds((pairs, rows, hd), BF16)),
        compiler_params=params(8),
        name="scan",
    )(gathered)
    pref = across_pairs(scanned).reshape(half * hd, hd)
    pref, gate_other, up_other, down_other = lax.optimization_barrier((pref, gate_other, up_other, down_other))
    keep, give = pl.pallas_call(
        functools.partial(split_kernel, half=half),
        grid=(1,),
        out_shape=[sds((half * hd, hd), BF16)] * 2,
        in_specs=[SMEM, full(pref), full(earlier)],
        out_specs=[full(pref)] * 2,
        compiler_params=params(8),
        name="split",
    )(bit, pref, earlier)
    other = partner(give)

    again = attn_gain.reshape(1, width)
    window = (nearby, keep, other, again, ffn_gain.reshape(1, width), disp)
    sent = pl.pallas_call(
        rows_kernel,
        grid=(1,),
        out_shape=sds((slots, width), BF16),
        in_specs=[SMEM] + [full(a) for a in window],
        out_specs=HBM,
        scratch_shapes=[pltpu.VMEM((resp, width), F32), pltpu.VMEM((slots, width), BF16), DMA((BANDS,))],
        compiler_params=params(8),
        name="rows",
    )(bit, *window)
    arrived = across_pairs(sent.reshape(pairs, CAP, width))

    gain_col = pl.BlockSpec((1, width // 2), lambda i: (0, i))
    state_all = pl.BlockSpec((half * hd, hd), lambda i: (0, 0))
    keep, mask = lax.optimization_barrier((keep, response_mask))
    start = jnp.where(mask == 1, jnp.arange(tok, dtype=jnp.int32), tok - resp).min()
    start = jnp.minimum(start, tok - resp).astype(jnp.int32).reshape(1)
    near = min(tok, resp + 16)
    first = jnp.minimum(start & -16, tok - near)
    near_col = pl.BlockSpec((near, width // 2), lambda i: (0, i))
    base, around = pl.pallas_call(
        mixed_kernel,
        grid=(2,),
        out_shape=[sds((tok, width), BF16), sds((near, width), F32)],
        in_specs=[SMEM, SMEM, col, col, col, state_all, state_all, gain_col],
        out_specs=[col, near_col],
        scratch_shapes=[pltpu.VMEM((tok, width // 2), F32)],
        compiler_params=params(60),
        cost_estimate=cost(2 * tok * width * hd, 7 << 20),
        name="mixed",
    )(bit, first, lifted, inside, stream_in, keep, other, again)
    arrived, base, around, *tables = lax.optimization_barrier((arrived, base, around, *tables))

    row_part = sds((resp, part), BF16)
    chunk = sds((planes * CAP, part), BF16)
    units = gate_weight.shape[1]
    step = min(256, units)
    many = count * chunk.shape[0]
    hidden = sds((2, many, units), BF16)
    *results, hid = pl.pallas_call(
        functools.partial(expert_kernel, count=count, step=step),
        grid=(1,),
        out_shape=[chunk] * count + [hidden],
        in_specs=[SMEM, SMEM] + [HBM] * 7,
        out_specs=[full(chunk)] * count + [HBM],
        scratch_shapes=[pltpu.VMEM((2, width, units), BF16)] * 2
        + [pltpu.VMEM((2, units, part), BF16), pltpu.VMEM(hidden.shape, BF16), pltpu.VMEM((many, width), BF16)]
        + [DMA((pairs + 4 * (units // step) + 3,))],
        compiler_params=params(48),
        cost_estimate=cost(10 * many * width * units, 12 << 20),
        name="expert",
    )(at, plane, arrived, gate_own, up_own, down_own, gate_other, up_other, down_other)
    shares = []
    for c in range(PARTS):
        if c:
            results = pl.pallas_call(
                functools.partial(down_kernel, count=count, first=c * part),
                grid=(1,),
                out_shape=[chunk] * count,
                in_specs=[full(hid), HBM, HBM],
                out_specs=[full(chunk)] * count,
                scratch_shapes=[pltpu.VMEM((2, units, part), BF16), DMA((2,))],
                compiler_params=params(48),
                cost_estimate=cost(2 * many * width * units, 2 << 20),
                name="down",
            )(hid, down_own, down_other)
        back = [results[0]] + [apart(results[m], 2 * m) for m in range(1, count)]
        operands = (*tables, *back)
        kinds = [sds((resp, part), F32)] + [row_part] * (planes - 1)
        sums = pl.pallas_call(
            functools.partial(combine_kernel, planes=planes, count=count),
            grid=(1,),
            out_shape=kinds,
            in_specs=[SMEM] + [full(a) for a in operands],
            out_specs=[full(a) for a in kinds],
            compiler_params=params(8),
            name="combine",
        )(at, *operands)
        shares += [sums[0]] + [apart(sums[m], 2 * count * m) for m in range(1, planes)]

    return pl.pallas_call(
        functools.partial(final_kernel, parts=PARTS, planes=planes),
        grid=(1,),
        out_shape=sds((tok, width), BF16),
        in_specs=[SMEM, SMEM, HBM, full(around)] + [full(a) for a in shares],
        out_specs=HBM,
        scratch_shapes=[pltpu.VMEM((near, width), BF16), DMA],
        input_output_aliases={2: 0},
        compiler_params=params(8),
        name="final",
    )(start, first, base, around, *shares)


def solution(mesh):
    lead = P(BOTH, None)
    placed = (
        lead,
        lead,
        lead,
        lead,
        P(None, BOTH),
        P(),
        P(),
        lead,
        lead,
        P(BOTH),
        P(None, BOTH),
        P(None, BOTH),
        lead,
    )
    return jax.shard_map(shards, mesh=mesh, in_specs=placed, out_specs=lead, check_vma=False)
```

```python
import functools

import jax
import jax.numpy as jnp
from jax import lax
from jax.experimental import pallas as pl
from jax.experimental.pallas import tpu as pltpu
from jax.sharding import PartitionSpec as P

CAP = 16
TAIL = 8
DECAYS = 3
ATTN_EPS = 1e-05
NORM_EPS = 1e-06
PLANES = 4
PARTS = 2
BOTH = ("seq", "grp")
F32 = jnp.float32
BF16 = jnp.bfloat16
SMEM = pl.BlockSpec(memory_space=pltpu.SMEM)
HBM = pl.BlockSpec(memory_space=pltpu.HBM)
DMA = pltpu.SemaphoreType.DMA


def params(mb=60):
    return pltpu.CompilerParams(vmem_limit_bytes=int(mb * 1024 * 1024))


def full(x):
    return pl.BlockSpec(x.shape, lambda i, n=len(x.shape): (0,) * n)


def cost(flops, nbytes):
    return pl.CostEstimate(flops=flops, bytes_accessed=nbytes, transcendentals=0)


def mm(a, b, ca=1, cb=0):
    return lax.dot_general(a, b, (((ca,), (cb,)), ((), ())), preferred_element_type=F32)


def lower_tri(n):
    rows = lax.broadcasted_iota(jnp.int32, (n, n), 0)
    cols = lax.broadcasted_iota(jnp.int32, (n, n), 1)
    return rows >= cols


def running_cols(dec):
    tri = lower_tri(dec.shape[1]).astype(F32)
    return lax.dot_general(
        tri, dec, (((1,), (1,)), ((), ())), precision=lax.Precision.HIGHEST, preferred_element_type=F32
    )


def running_rows(dec):
    tri = lower_tri(dec.shape[1]).astype(F32)
    return lax.dot_general(
        dec, tri, (((1,), (1,)), ((), ())), precision=lax.Precision.HIGHEST, preferred_element_type=F32
    )


def partner(x):
    count = lax.axis_size("grp")
    return lax.ppermute(x, "grp", [(i, i ^ 1) for i in range(count)])


def apart(x, distance):
    return lax.ppermute(x, BOTH, [(i, i ^ distance) for i in range(lax.axis_size(BOTH))])


def across_pairs(x):
    count = lax.axis_size(BOTH)
    groups = [list(range(k, count, 2)) for k in range(2)]
    return lax.all_to_all(x, BOTH, 0, 0, tiled=True, axis_index_groups=groups)


def copy(src, dst, sems, n):
    c = pltpu.make_async_copy(src, dst, sems.at[n])
    c.start()
    return c


def states_kernel(k_ref, key_hbm, val_hbm, dec_hbm, own_hbm, send_hbm, key_ref, val_ref, dec_ref, own_ref, send_ref, sems):
    heads, tok = dec_ref.shape
    half = heads // 2
    hd = own_ref.shape[1]
    span = half * hd
    k = k_ref[0]
    get_dec = copy(dec_hbm, dec_ref, sems, 0)
    gets = []
    for n in range(2):
        cols = pl.ds(pl.multiple_of((k ^ 1 ^ n) * span, span), span)
        gets.append(copy(key_hbm.at[:, cols], key_ref.at[n], sems, 1 + 2 * n))
        gets.append(copy(val_hbm.at[:, cols], val_ref.at[n], sems, 2 + 2 * n))
    get_dec.wait()
    mine = dec_ref[pl.ds(pl.multiple_of(k * half, half), half), :]
    theirs = dec_ref[pl.ds(pl.multiple_of((1 - k) * half, half), half), :]
    run = running_cols(jnp.concatenate([mine, theirs], axis=0))
    total = run[tok - 1 : tok, :]
    fac = jnp.exp(total - run)
    tail = jnp.broadcast_to(jnp.pad(total, ((0, 0), (0, hd - heads))), (TAIL, hd))
    puts = []
    for n, dst, out, first in ((0, send_ref, send_hbm, half), (1, own_ref, own_hbm, 0)):
        gets[2 * n].wait()
        gets[2 * n + 1].wait()
        for j in range(half):
            cols = slice(j * hd, (j + 1) * hd)
            scaled = (key_ref[n, :, cols].astype(F32) * fac[:, first + j : first + j + 1]).astype(BF16)
            dst[cols, :] = mm(val_ref[n, :, cols], scaled, 0, 0)
        dst[span:, :] = tail
        puts.append(copy(dst, out, sems, 5 + n))
    for c in puts:
        c.wait()


def pair_kernel(k_ref, own_ref, recv_ref, notes_ref, out_ref, first_ref, *, half, rows):
    hd = own_ref.shape[1]
    first = k_ref[0] == 0
    base = half * hd
    mine = own_ref[base : base + 1, :]
    theirs = recv_ref[base : base + 1, :]
    pieces = out_ref.shape[0]
    planes, tail_rows = notes_ref.shape[:2]
    tail_row = lax.broadcasted_iota(jnp.int32, (tail_rows, hd), 0)
    for p in range(pieces):
        j = p * rows // hd
        mt = mine[:, j : j + 1]
        pt = theirs[:, half + j : half + j + 1]
        one = jnp.ones_like(mt)
        a = jnp.where(first, jnp.exp(pt), one)
        b = jnp.where(first, one, jnp.exp(mt))
        lo = p * rows
        chip = own_ref[lo : lo + rows, :] * a + recv_ref[lo : lo + rows, :] * b
        out_ref[p, 0:rows, :] = chip.astype(BF16)
        d = jnp.broadcast_to(jnp.exp(mt + pt), (tail_rows, hd))
        notes = notes_ref[p * planes // pieces].astype(F32)
        d0 = d.astype(BF16).astype(F32)
        d1 = (d - d0).astype(BF16).astype(F32)
        d2 = d - d0 - d1
        first_ref[lo : lo + rows, :] = jnp.where(first, own_ref[lo : lo + rows, :], recv_ref[lo : lo + rows, :])
        tail = jnp.where(tail_row == 0, d0, jnp.where(tail_row == 1, d1, jnp.where(tail_row == 2, d2, notes)))
        out_ref[p, rows:, :] = tail.astype(BF16)
    rolled = pltpu.roll(theirs, hd - half, 1)
    first_ref[base:, :] = jnp.broadcast_to(jnp.where(first, mine, rolled), (TAIL, hd))


def scan_kernel(in_ref, out_ref):
    count, rows, hd = out_ref.shape
    state = jnp.zeros((rows, hd), F32)
    for c in range(count):
        out_ref[c, :, :] = state.astype(BF16)
        tail = in_ref[c, rows:, :].astype(F32)
        d = tail[0:1, :] + tail[1:2, :] + tail[2:3, :]
        state = state * d + in_ref[c, 0:rows, :].astype(F32)


def split_kernel(k_ref, pref_ref, first_ref, keep_ref, give_ref, *, half):
    hd = first_ref.shape[1]
    even = k_ref[0] == 0
    logs = first_ref[half * hd : half * hd + 1, :]
    for j in range(half):
        sl = slice(j * hd, (j + 1) * hd)
        before = pref_ref[sl, :].astype(F32)
        after = before * jnp.exp(logs[:, j : j + 1]) + first_ref[sl, :]
        keep_ref[sl, :] = jnp.where(even, before, after).astype(BF16)
        give_ref[sl, :] = jnp.where(even, after, before).astype(BF16)


def window_start(live, resp):
    tok = live.shape[1]
    token = lax.broadcasted_iota(jnp.int32, (1, tok), 1)
    return jnp.min(jnp.where(live, token, tok - resp), axis=1, keepdims=True).clip(0, tok - resp)


def inside_kernel(live_ref, dec_ref, q_ref, key_ref, val_ref, stream_ref, inside_ref, lifted_ref, near_ref):
    heads, tok = dec_ref.shape
    hd = q_ref.shape[1] // heads
    dec = dec_ref[...]
    run_c = running_cols(dec)
    run_r = running_rows(dec)
    lift = jnp.exp(run_c)
    cut = tok // 2
    tri = lower_tri(cut)
    resp = near_ref.shape[0] // 3
    picked = lax.broadcasted_iota(jnp.int32, (resp, tok), 0) + window_start(live_ref[...] == 1, resp)
    pick = jnp.where(lax.broadcasted_iota(jnp.int32, (resp, tok), 1) == picked, 1.0, 0.0).astype(BF16)
    for h in range(heads):
        cols = slice(h * hd, (h + 1) * hd)
        q = q_ref[:, cols]
        kk = key_ref[:, cols]
        v = val_ref[:, cols]
        lifted = (q.astype(F32) * lift[:, h : h + 1]).astype(BF16)
        lifted_ref[:, cols] = lifted
        rc = run_c[:, h : h + 1]
        rr = run_r[h : h + 1, :]
        f_aa = jnp.where(tri, jnp.exp(rc[:cut] - rr[:, :cut]), 0.0)
        f_bb = jnp.where(tri, jnp.exp(rc[cut:] - rr[:, cut:]), 0.0)
        f_ba = jnp.exp(rc[cut:] - rr[:, :cut])
        w_aa = (mm(q[:cut], kk[:cut], 1, 1) * f_aa).astype(BF16)
        s_b = mm(q[cut:], kk, 1, 1)
        w_b = (s_b * jnp.concatenate([f_ba, f_bb], axis=1)).astype(BF16)
        inside_ref[:cut, cols] = mm(w_aa, v[:cut])
        inside_ref[cut:, cols] = mm(w_b, v)
    near_ref[resp : 2 * resp, :] = mm(pick, lifted_ref[...])
    near_ref[2 * resp :, :] = mm(pick, stream_ref[...])
    rest = inside_ref[...]
    high = rest.astype(BF16)
    rest = rest - high.astype(F32)
    mid = rest.astype(BF16)
    low = (rest - mid.astype(F32)).astype(BF16)
    near_ref[:resp, :] = mm(pick, high) + mm(pick, mid) + mm(pick, low)


def head_norm(att):
    return att * lax.rsqrt(jnp.mean(att * att, axis=-1, keepdims=True) + ATTN_EPS)


def half_rows(first, near_ref, state_ref, again_ref, mixed_ref, base):
    hd = state_ref.shape[1]
    resp = near_ref.shape[0] // 3
    for j in range(state_ref.shape[0] // hd):
        cols = pl.ds(pl.multiple_of(first + j * hd, hd), hd)
        lifted = near_ref[resp : 2 * resp, cols].astype(BF16)
        att = near_ref[:resp, cols] + mm(lifted, state_ref[j * hd : (j + 1) * hd, :], 1, 1)
        here = pl.ds(pl.multiple_of(base + j * hd, hd), hd)
        mixed_ref[:, here] = near_ref[2 * resp :, cols] + head_norm(att) * again_ref[:, cols]


def mine_kernel(k_ref, near_ref, keep_ref, again_ref, mixed_ref):
    half_rows(k_ref[0] * keep_ref.shape[0], near_ref, keep_ref, again_ref, mixed_ref, 0)


def rows_kernel(k_ref, near_ref, mine_ref, other_ref, again_ref, fgain_ref, disp_ref, sent_ref, mixed_ref):
    span = other_ref.shape[0]
    k = k_ref[0]
    other = pl.multiple_of((1 - k) * span, span)
    half_rows(other, near_ref, other_ref, again_ref, mixed_ref, other)
    mixed_ref[:, pl.ds(pl.multiple_of(k * span, span), span)] = mine_ref[...]
    mixed = mixed_ref[...]
    scale = lax.rsqrt(jnp.mean(mixed * mixed, axis=-1, keepdims=True) + NORM_EPS)
    ffn = (mixed * scale * fgain_ref[...]).astype(BF16)
    sent_ref[...] = mm(disp_ref[...], ffn).astype(BF16)


def mixed_kernel(k_ref, from_ref, lifted_ref, inside_ref, stream_ref, keep_ref, other_ref, again_ref, base_ref, near_ref, mixed_ref):
    hd = keep_ref.shape[1]
    half = keep_ref.shape[0] // hd
    mine = pl.program_id(0) == k_ref[0]
    for j in range(half):
        cols = slice(j * hd, (j + 1) * hd)
        st = jnp.where(mine, keep_ref[cols, :].astype(F32), other_ref[cols, :].astype(F32)).astype(BF16)
        att = inside_ref[:, cols] + mm(lifted_ref[:, cols], st, 1, 1)
        mixed_ref[:, cols] = stream_ref[:, cols].astype(F32) + head_norm(att) * again_ref[:, cols]
    base_ref[...] = mixed_ref[...].astype(BF16)
    near_ref[...] = mixed_ref[pl.ds(pl.multiple_of(from_ref[0], 16), near_ref.shape[0]), :]


def noted(experts, resp, lanes):
    side = max(1, lanes // resp)
    return side, -(-experts // side)


def shift_table(resp, lanes, g, rows):
    j = lax.broadcasted_iota(jnp.int32, (resp, lanes) if rows else (lanes, resp), 0 if rows else 1)
    lane = lax.broadcasted_iota(jnp.int32, (resp, lanes) if rows else (lanes, resp), 1 if rows else 0)
    return jnp.where(lane == j + g * resp, 1.0, 0.0).astype(BF16)


def route_kernel(ids_ref, wts_ref, live_ref, disp_ref, notes_ref, *, experts):
    top, tok = ids_ref.shape
    slots, resp = disp_ref.shape
    planes, tail_rows, lanes = notes_ref.shape
    count = experts // planes
    live = live_ref[...] == 1
    e_row = lax.broadcasted_iota(jnp.int32, (experts, tok), 0)
    chosen = jnp.zeros((experts, tok), F32)
    weight = jnp.zeros((experts, tok), F32)
    for j in range(top):
        hit = (ids_ref[j : j + 1, :] == e_row) & live
        chosen = jnp.where(hit, 1.0, chosen)
        weight = jnp.where(hit, wts_ref[j : j + 1, :], weight)
    rows = lax.broadcasted_iota(jnp.int32, (tok, tok), 0)
    cols = lax.broadcasted_iota(jnp.int32, (tok, tok), 1)
    before = jnp.where(rows < cols, 1.0, 0.0).astype(BF16)
    place = mm(chosen.astype(BF16), before)
    place = jnp.where(chosen > 0.0, place, -1.0)
    s_row = lax.broadcasted_iota(jnp.int32, (slots, experts), 0)
    e_col = lax.broadcasted_iota(jnp.int32, (slots, experts), 1)
    spread = jnp.where(s_row // CAP == e_col, 1.0, 0.0).astype(BF16)
    slot_of = lax.broadcasted_iota(jnp.int32, (slots, tok), 0) % CAP
    hit = mm(spread, place.astype(BF16)) == slot_of.astype(F32)
    w_hi = weight.astype(BF16)
    w_lo = (weight - w_hi.astype(F32)).astype(BF16)
    picked = lax.broadcasted_iota(jnp.int32, (tok, resp), 1) + window_start(live, resp)
    pick = jnp.where(lax.broadcasted_iota(jnp.int32, (tok, resp), 0) == picked, 1.0, 0.0).astype(BF16)
    disp_ref[...] = mm(jnp.where(hit, 1.0, 0.0).astype(BF16), pick).astype(BF16)
    side, each = noted(count, resp, lanes)
    tail_row = lax.broadcasted_iota(jnp.int32, (tail_rows, lanes), 0)
    notes = [jnp.zeros((tail_rows, lanes), F32)] * planes
    for n, part in enumerate((w_hi, w_lo)):
        part = mm(part, pick).astype(BF16)
        placed = [mm(part, shift_table(resp, lanes, g, True)) for g in range(side)]
        for e in range(experts):
            at = e % count
            line = placed[at % side][e : e + 1, :]
            here = tail_row == DECAYS + n * each + at // side
            notes[e // count] = notes[e // count] + jnp.where(here, line, 0.0)
    for p in range(planes):
        notes_ref[p, :, :] = notes[p].astype(BF16)


def plan_kernel(at_ref, plane_ref, in_ref, *outs, planes, rows):
    lanes = in_ref.shape[2]
    resp = outs[0].shape[1]
    span = outs[0].shape[0] // 2
    count = span // CAP
    side, each = noted(count, resp, lanes)
    e_row = lax.broadcasted_iota(jnp.int32, (count, resp), 0)
    before = lax.broadcasted_iota(jnp.int32, (resp, resp), 0) < lax.broadcasted_iota(jnp.int32, (resp, resp), 1)
    before = jnp.where(before, 1.0, 0.0).astype(BF16)
    s_row = lax.broadcasted_iota(jnp.int32, (span, count), 0)
    e_col = lax.broadcasted_iota(jnp.int32, (span, count), 1)
    spread = jnp.where(s_row // CAP == e_col, 1.0, 0.0).astype(BF16)
    slot_of = (lax.broadcasted_iota(jnp.int32, (span, resp), 0) % CAP).astype(F32)
    for m in range(planes):
        pair = (plane_ref[0] ^ m) * count + at_ref[0]
        tail = in_ref[pair, rows:, :]
        moved = [mm(tail, shift_table(resp, lanes, g, False)) for g in range(side)]
        parts = []
        for n in range(2):
            part = jnp.zeros((count, resp), F32)
            for e in range(count):
                r = DECAYS + n * each + e // side
                part = part + jnp.where(e_row == e, moved[e % side][r : r + 1, :], 0.0)
            parts.append(part.astype(BF16))
        chosen = parts[0].astype(F32) > 0.0
        place = mm(jnp.where(chosen, 1.0, 0.0).astype(BF16), before)
        hit = mm(spread, jnp.where(chosen, place, -1.0).astype(BF16)) == slot_of
        for n in range(2):
            outs[m][n * span : (n + 1) * span, :] = jnp.where(hit, mm(spread, parts[n]), 0.0).astype(BF16)


def table_rows(tab_ref, n, at, count):
    lead = n * count * CAP
    rows = [tab_ref[pl.ds(pl.multiple_of(lead + (at ^ m) * CAP, CAP), CAP), :] for m in range(count)]
    return jnp.concatenate(rows, axis=0)


def combine_kernel(at_ref, *refs, planes, count):
    tabs, results, outs = refs[:planes], refs[planes : planes + count], refs[planes + count :]
    for m in range(planes):
        got = jnp.concatenate([results[q][m * CAP : (m + 1) * CAP, :] for q in range(count)], axis=0)
        hi = table_rows(tabs[m], 0, at_ref[0], count)
        lo = table_rows(tabs[m], 1, at_ref[0], count)
        outs[m][...] = (mm(hi, got, 0, 0) + mm(lo, got, 0, 0)).astype(outs[m].dtype)


def expert_kernel(at_ref, plane_ref, x_hbm, g0, u0, d0, g1, u1, d1, *refs, count, step):
    outs, (hid_out, gv, uv, dv, hid_ref, x_ref, sems) = refs[:count], refs[count:]
    units = g0.shape[1]
    rows, part = outs[0].shape
    cuts = range(0, units, step)
    gets = []
    for q in range(count):
        for m in range(rows // CAP):
            pair = (plane_ref[0] ^ m) * count + (at_ref[0] ^ q)
            gets.append(copy(x_hbm.at[pair], x_ref.at[pl.ds(q * rows + m * CAP, CAP)], sems, len(gets)))
    at = len(gets)
    for n, (g, u) in enumerate(((g0, u0), (g1, u1))):
        for c in cuts:
            cols = pl.ds(c, step)
            gets.append(copy(g.at[:, cols], gv.at[n, :, cols], sems, len(gets)))
            gets.append(copy(u.at[:, cols], uv.at[n, :, cols], sems, len(gets)))
    for n, d in enumerate((d0, d1)):
        gets.append(copy(d.at[:, pl.ds(0, part)], dv.at[n], sems, len(gets)))
    for c in gets[:at]:
        c.wait()
    many = count * rows
    block = min(256, many)
    for n in range(2):
        for c in cuts:
            gets[at].wait()
            gets[at + 1].wait()
            at += 2
            for r in range(0, many, block):
                x = x_ref[r : r + block, :]
                gate = mm(x, gv[n, :, c : c + step])
                up = mm(x, uv[n, :, c : c + step])
                hid_ref[n, r : r + block, c : c + step] = (gate / (1.0 + jnp.exp(-gate)) * up).astype(BF16)
    put = copy(hid_ref, hid_out, sems, len(gets))
    gets[at].wait()
    gets[at + 1].wait()
    down(hid_ref, dv, outs, block)
    put.wait()


def down(hid_ref, down_ref, outs, block):
    rows, part = outs[0].shape
    for r in range(0, rows * len(outs), block):
        for c in range(0, part, 256):
            cols = slice(c, c + 256)
            p0 = mm(hid_ref[0, r : r + block, :], down_ref[0, :, cols]).astype(BF16).astype(F32)
            p1 = mm(hid_ref[1, r : r + block, :], down_ref[1, :, cols]).astype(BF16).astype(F32)
            p = (p0 + p1).astype(BF16)
            for q in range(r // rows, (r + block) // rows):
                outs[q][:, cols] = p[q * rows - r : (q + 1) * rows - r, :]


def down_kernel(hid_ref, d0, d1, *refs, count, first):
    outs, (dv, sems) = refs[:count], refs[count:]
    part = outs[0].shape[1]
    gets = [copy(d.at[:, pl.ds(first, part)], dv.at[n], sems, n) for n, d in enumerate((d0, d1))]
    for c in gets:
        c.wait()
    down(hid_ref, dv, outs, min(256, hid_ref.shape[1]))


def final_kernel(start_ref, from_ref, base_hbm, near_ref, *refs, parts, planes):
    shares, (out_hbm, res_ref, sem) = refs[: parts * planes], refs[parts * planes :]
    many, width = near_ref.shape
    resp, part = shares[0].shape
    row = lax.broadcasted_iota(jnp.int32, (many, resp), 0)
    place = lax.broadcasted_iota(jnp.int32, (many, resp), 1) + (start_ref[0] - from_ref[0])
    spread = jnp.where(row == place, 1.0, 0.0).astype(BF16)
    for c in range(parts):
        cols = slice(c * part, (c + 1) * part)
        total = shares[c * planes][...]
        for m in range(1, planes):
            total = total + shares[c * planes + m][...].astype(F32)
        hi = total.astype(BF16)
        lo = (total - hi.astype(F32)).astype(BF16)
        res_ref[:, cols] = (near_ref[:, cols] + mm(spread, hi) + mm(spread, lo)).astype(BF16)
    put = pltpu.make_async_copy(res_ref, out_hbm.at[pl.ds(pl.multiple_of(from_ref[0], 16), many)], sem)
    put.start()
    put.wait()


def shards(
    stream_in,
    query_rows,
    key_rows,
    value_rows,
    log_decay,
    attn_gain,
    ffn_gain,
    expert_ids,
    route_weights,
    response_mask,
    gate_weight,
    up_weight,
    down_weight,
):
    tok, width = stream_in.shape
    heads = log_decay.shape[0]
    hd = width // heads
    half = heads // 2
    devices = lax.axis_size(BOTH)
    pairs = devices // 2
    experts = devices // 2
    slots = experts * CAP
    top = expert_ids.shape[1]
    resp = min(tok, slots // top)
    rows = half * hd // pairs
    planes = PLANES
    count = pairs // planes
    part = width // PARTS
    me = lax.axis_index(BOTH)
    bit = (me & 1).reshape(1).astype(jnp.int32)
    sds = jax.ShapeDtypeStruct

    span = half * hd
    own, send = pl.pallas_call(
        states_kernel,
        out_shape=[sds((span + TAIL, hd), F32)] * 2,
        in_specs=[SMEM, HBM, HBM, HBM],
        out_specs=[HBM, HBM],
        scratch_shapes=[pltpu.VMEM((2, tok, span), BF16)] * 2
        + [pltpu.VMEM((heads, tok), F32)]
        + [pltpu.VMEM((span + TAIL, hd), F32)] * 2
        + [DMA((7,))],
        compiler_params=params(),
        cost_estimate=cost(2 * tok * width * hd, 3 << 20),
        name="states",
    )(bit, key_rows, value_rows, log_decay)
    recv = partner(send)
    plane = lax.shift_right_logical(me, (2 * count).bit_length() - 1).reshape(1).astype(jnp.int32)
    at = (lax.shift_right_logical(me, 1) & (count - 1)).reshape(1).astype(jnp.int32)
    routing = (expert_ids.T, route_weights.T, response_mask.reshape(1, tok))
    table = sds((2 * count * CAP, resp), BF16)
    slot_rows = sds((slots, resp), BF16)
    tail = -(-(DECAYS + 2 * noted(count, resp, hd)[1]) // 16) * 16
    note = sds((planes, tail, hd), BF16)
    disp, notes = pl.pallas_call(
        functools.partial(route_kernel, experts=experts),
        grid=(1,),
        out_shape=[slot_rows, note],
        in_specs=[full(a) for a in routing],
        out_specs=[full(slot_rows), full(note)],
        compiler_params=params(),
        cost_estimate=cost(8 * tok * tok * slots, 1 << 20),
        name="route",
    )(*routing)
    recv, gate_own, up_own, down_own, disp, notes = lax.optimization_barrier(
        (recv, gate_weight, up_weight, down_weight, disp, notes)
    )
    gate_other, up_other, down_other = partner(gate_own), partner(up_own), partner(down_own)
    payload = sds((pairs, rows + tail, hd), BF16)
    packed, earlier = pl.pallas_call(
        functools.partial(pair_kernel, half=half, rows=rows),
        grid=(1,),
        out_shape=[payload, sds(own.shape, F32)],
        in_specs=[SMEM, full(own), full(recv), full(note)],
        out_specs=[full(payload), full(own)],
        compiler_params=params(63.4),
        name="pair",
    )(bit, own, recv, notes)
    gathered = across_pairs(packed)
    col = pl.BlockSpec((tok, width // 2), lambda i: (0, i))
    wcol = pl.BlockSpec((3 * resp, width // 2), lambda i: (0, i))
    inside, lifted, nearby = pl.pallas_call(
        inside_kernel,
        grid=(2,),
        out_shape=[
            sds((tok, width), F32),
            sds((tok, width), BF16),
            sds((3 * resp, width), F32),
        ],
        in_specs=[full(routing[2]), pl.BlockSpec((half, tok), lambda i: (i, 0)), col, col, col, col],
        out_specs=[col, col, wcol],
        compiler_params=params(),
        cost_estimate=cost(4 * tok * tok * width, 6 << 20),
        name="inside",
    )(routing[2], log_decay, query_rows, key_rows, value_rows, stream_in)
    gathered, inside, lifted, nearby = lax.optimization_barrier((gathered, inside, lifted, nearby))
    tables = pl.pallas_call(
        functools.partial(plan_kernel, planes=planes, rows=rows),
        grid=(1,),
        out_shape=[table] * planes,
        in_specs=[SMEM, SMEM, full(gathered)],
        out_specs=[full(table)] * planes,
        compiler_params=params(8),
        cost_estimate=cost(1 << 24, 1 << 20),
        name="plan",
    )(at, plane, gathered)
    scanned = pl.pallas_call(
        scan_kernel,
        grid=(1,),
        out_shape=sds((pairs, rows, hd), BF16),
        in_specs=[full(gathered)],
        out_specs=full(sds((pairs, rows, hd), BF16)),
        compiler_params=params(8),
        name="scan",
    )(gathered)
    pref = across_pairs(scanned).reshape(half * hd, hd)
    pref, gate_other, up_other, down_other = lax.optimization_barrier((pref, gate_other, up_other, down_other))
    keep, give = pl.pallas_call(
        functools.partial(split_kernel, half=half),
        grid=(1,),
        out_shape=[sds((half * hd, hd), BF16)] * 2,
        in_specs=[SMEM, full(pref), full(earlier)],
        out_specs=[full(pref)] * 2,
        compiler_params=params(8),
        name="split",
    )(bit, pref, earlier)
    other = partner(give)

    again = attn_gain.reshape(1, width)
    first_half = (nearby, keep, again)
    mine = pl.pallas_call(
        mine_kernel,
        grid=(1,),
        out_shape=sds((resp, width // 2), F32),
        in_specs=[SMEM] + [full(a) for a in first_half],
        out_specs=full(sds((resp, width // 2), F32)),
        compiler_params=params(8),
        cost_estimate=cost(2 * resp * width * hd, 1 << 20),
        name="mine",
    )(bit, *first_half)
    window = (nearby, mine, other, again, ffn_gain.reshape(1, width), disp)
    sent = pl.pallas_call(
        rows_kernel,
        grid=(1,),
        out_shape=sds((slots, width), BF16),
        in_specs=[SMEM] + [full(a) for a in window],
        out_specs=full(sds((slots, width), BF16)),
        scratch_shapes=[pltpu.VMEM((resp, width), F32)],
        compiler_params=params(8),
        name="rows",
    )(bit, *window)
    arrived = across_pairs(sent.reshape(pairs, CAP, width))

    gain_col = pl.BlockSpec((1, width // 2), lambda i: (0, i))
    state_all = pl.BlockSpec((half * hd, hd), lambda i: (0, 0))
    keep, mask = lax.optimization_barrier((keep, response_mask))
    start = jnp.where(mask == 1, jnp.arange(tok, dtype=jnp.int32), tok - resp).min()
    start = jnp.minimum(start, tok - resp).astype(jnp.int32).reshape(1)
    near = min(tok, resp + 16)
    first = jnp.minimum(start & -16, tok - near)
    near_col = pl.BlockSpec((near, width // 2), lambda i: (0, i))
    base, around = pl.pallas_call(
        mixed_kernel,
        grid=(2,),
        out_shape=[sds((tok, width), BF16), sds((near, width), F32)],
        in_specs=[SMEM, SMEM, col, col, col, state_all, state_all, gain_col],
        out_specs=[col, near_col],
        scratch_shapes=[pltpu.VMEM((tok, width // 2), F32)],
        compiler_params=params(60),
        cost_estimate=cost(2 * tok * width * hd, 7 << 20),
        name="mixed",
    )(bit, first, lifted, inside, stream_in, keep, other, again)
    arrived, base, around, *tables = lax.optimization_barrier((arrived, base, around, *tables))

    row_part = sds((resp, part), BF16)
    chunk = sds((planes * CAP, part), BF16)
    units = gate_weight.shape[1]
    step = min(256, units)
    many = count * chunk.shape[0]
    hidden = sds((2, many, units), BF16)
    *results, hid = pl.pallas_call(
        functools.partial(expert_kernel, count=count, step=step),
        grid=(1,),
        out_shape=[chunk] * count + [hidden],
        in_specs=[SMEM, SMEM] + [HBM] * 7,
        out_specs=[full(chunk)] * count + [HBM],
        scratch_shapes=[pltpu.VMEM((2, width, units), BF16)] * 2
        + [pltpu.VMEM((2, units, part), BF16), pltpu.VMEM(hidden.shape, BF16), pltpu.VMEM((many, width), BF16)]
        + [DMA((pairs + 4 * (units // step) + 3,))],
        compiler_params=params(48),
        cost_estimate=cost(10 * many * width * units, 12 << 20),
        name="expert",
    )(at, plane, arrived, gate_own, up_own, down_own, gate_other, up_other, down_other)
    shares = []
    for c in range(PARTS):
        if c:
            results = pl.pallas_call(
                functools.partial(down_kernel, count=count, first=c * part),
                grid=(1,),
                out_shape=[chunk] * count,
                in_specs=[full(hid), HBM, HBM],
                out_specs=[full(chunk)] * count,
                scratch_shapes=[pltpu.VMEM((2, units, part), BF16), DMA((2,))],
                compiler_params=params(48),
                cost_estimate=cost(2 * many * width * units, 2 << 20),
                name="down",
            )(hid, down_own, down_other)
        back = [results[0]] + [apart(results[m], 2 * m) for m in range(1, count)]
        operands = (*tables, *back)
        kinds = [sds((resp, part), F32)] + [row_part] * (planes - 1)
        sums = pl.pallas_call(
            functools.partial(combine_kernel, planes=planes, count=count),
            grid=(1,),
            out_shape=kinds,
            in_specs=[SMEM] + [full(a) for a in operands],
            out_specs=[full(a) for a in kinds],
            compiler_params=params(8),
            name="combine",
        )(at, *operands)
        shares += [sums[0]] + [apart(sums[m], 2 * count * m) for m in range(1, planes)]

    return pl.pallas_call(
        functools.partial(final_kernel, parts=PARTS, planes=planes),
        grid=(1,),
        out_shape=sds((tok, width), BF16),
        in_specs=[SMEM, SMEM, HBM, full(around)] + [full(a) for a in shares],
        out_specs=HBM,
        scratch_shapes=[pltpu.VMEM((near, width), BF16), DMA],
        input_output_aliases={2: 0},
        compiler_params=params(8),
        name="final",
    )(start, first, base, around, *shares)


def solution(mesh):
    lead = P(BOTH, None)
    placed = (
        lead,
        lead,
        lead,
        lead,
        P(None, BOTH),
        P(),
        P(),
        lead,
        lead,
        P(BOTH),
        P(None, BOTH),
        P(None, BOTH),
        lead,
    )
    return jax.shard_map(shards, mesh=mesh, in_specs=placed, out_specs=lead, check_vma=False)
```
